256 devices in a mesh: tm: 128 (over x, y, z), space: 2 (over core).
Axes of the slice: x: 4, y: 4, z: 8, core: 2. Of those that a mesh axis runs over, the one named last changes fastest.
Arguments:
- window_state: float32 [128, 512, 512], P('tm', 'space'), may hold values from -6 to 6
- prior_window: float32 [128, 512, 512], P('tm', 'space'), may hold values from -6 to 6
- conductivity: float32 [512, 512], P('space'), may hold values from 0.5 to 2
Outputs:
- updated: float32 [128, 512, 512], P('tm', 'space')
The draws below stay inside these ranges and needn't reach their ends.
All inputs are finite; a program needn't handle non-finite values.
Results may differ from the reference program's by a relative error of at most 0.0003.
Values sent between devices are 32-bit elements; how exact they have to be, the bound alone decides.
A program may use at most 64 MiB of HBM per device.

```python
import math
import jax
import jax.numpy as jnp
from jax import lax

NX = 512
NY = 512
SWEEPS = 24
STEPS = 128


def steps_of(stream_key, extent, shards, least, high):
    loudness = 1.0
    for position, shards_of in shards:
        steps = jax.random.uniform(jax.random.fold_in(jax.random.fold_in(stream_key, 6), position), (shards_of,), jnp.float32, least / len(shards), high / len(shards))
        loudness = loudness * jnp.repeat(jnp.exp(steps), extent[position] // shards_of).reshape((-1,) + (1,) * (len(extent) - 1 - position))
    return loudness


def centred(stream_key, dims, width, reach, split=(), kind=jnp.bfloat16):
    entries = jax.random.normal(stream_key, dims, jnp.float32) * width
    if len(split) > 0:
        entries = steps_of(stream_key, dims, split, -0.22, 0.18) * entries
    return jnp.clip(entries, min=-reach, max=reach).astype(kind)


def setup_inputs(seed: int = 0) -> dict:
    streams_of = jax.random.split(jax.random.key(seed), 4)
    return {
        "window_state": centred(streams_of[0], (STEPS, NX, NY), 1.0, 6.0, ((0, 128), (1, 2)), jnp.float32),
        "prior_window": centred(streams_of[1], (STEPS, NX, NY), 1.0, 6.0, ((0, 128), (1, 2)), jnp.float32),
        "conductivity": jnp.clip(jnp.exp(math.log(2.0) - 1.3862944 * jax.random.uniform(streams_of[2], (NX, NY), jnp.float32) ** steps_of(streams_of[2], (NX, NY), ((0, 2),), -0.2, 0.2)), 0.5, 2.0),
    }


time_ratio = 2.0
window_alpha = 0.01
spectral_bound = 24.0


def conductance(conductivity, values):
    return conductivity * (1.0 + 0.5 * jnp.tanh(values))


def beside_all(padded):
    return (padded[..., :-2, 1:-1], padded[..., 2:, 1:-1], padded[..., 1:-1, :-2], padded[..., 1:-1, 2:])


def flux_of(values_pad, coeff_pad):
    values = values_pad[..., 1:-1, 1:-1]
    coeff = coeff_pad[..., 1:-1, 1:-1]
    summed = jnp.zeros_like(values)
    for near_value, near_coeff in zip(beside_all(values_pad), beside_all(coeff_pad)):
        summed = summed + 0.5 * (coeff + near_coeff) * (near_value - values)
    return summed


def frozen_weights(coeff_pad):
    coeff = coeff_pad[..., 1:-1, 1:-1]
    facing = tuple(0.5 * time_ratio * (coeff + near_coeff) for near_coeff in beside_all(coeff_pad))
    return facing + (facing[0] + facing[1] + facing[2] + facing[3],)


def operator_image(search_pad, shift_value, weights):
    search = search_pad[:, 1:-1, 1:-1]
    nearby_list = beside_all(search_pad)
    nearby = weights[0] * nearby_list[0] + weights[1] * nearby_list[1] + weights[2] * nearby_list[2] + weights[3] * nearby_list[3]
    central = weights[4]
    image_real = shift_value[0] * search[0] - shift_value[1] * search[1] + central * search[0] - nearby[0]
    image_imag = shift_value[0] * search[1] + shift_value[1] * search[0] + central * search[1] - nearby[1]
    return jnp.stack([image_real, image_imag])


def complex_times(left_pair, right_pair):
    return (left_pair[0] * right_pair[0] - left_pair[1] * right_pair[1], left_pair[0] * right_pair[1] + left_pair[1] * right_pair[0])


def complex_inverse(pair_value):
    scaling = 1.0 / (pair_value[0] * pair_value[0] + pair_value[1] * pair_value[1])
    return (pair_value[0] * scaling, -pair_value[1] * scaling)


def scaled_field(pair_value, field_pair):
    return jnp.stack([pair_value[0] * field_pair[0] - pair_value[1] * field_pair[1], pair_value[0] * field_pair[1] + pair_value[1] * field_pair[0]])


def frequency_scalars(frequency, length):
    angle = 2.0 * math.pi * frequency.astype(jnp.float32) / length
    beta = math.exp(math.log(window_alpha) / length)
    shift_value = (1.0 - beta * jnp.cos(angle), beta * jnp.sin(angle))
    half_span = 0.5 * spectral_bound * time_ratio
    center = (shift_value[0] + half_span, shift_value[1])
    relative = (center[0] / half_span, center[1] / half_span)
    return shift_value, center, relative, half_span


def chebyshev(source_pair, center, relative, half_span, apply_op, inside):
    search = scaled_field(complex_inverse(center), source_pair) * inside
    factor = complex_inverse(relative)

    def one_sweep(counter, carried):
        solution, remain, search, factor_real, factor_imag = carried
        applied = apply_op(search)
        solution = solution + search
        remain = remain - applied
        renewed = complex_inverse((2.0 * relative[0] - factor_real, 2.0 * relative[1] - factor_imag))
        lead_factor = complex_times(renewed, (factor_real, factor_imag))
        rest_factor = (2.0 * renewed[0] / half_span, 2.0 * renewed[1] / half_span)
        search = (scaled_field(lead_factor, search) + scaled_field(rest_factor, remain)) * inside
        return solution, remain, search, renewed[0], renewed[1]

    initial = (jnp.zeros_like(source_pair), source_pair, search, factor[0], factor[1])
    solution, remain, search, factor_real, factor_imag = lax.fori_loop(0, SWEEPS, one_sweep, initial)
    return solution + search


def reference(window_state, prior_window, conductivity):
    length = window_state.shape[0]
    initial = prior_window[length - 1]
    before = jnp.concatenate([initial[None], window_state[:-1]], axis=0)
    coeff = conductance(conductivity[None], window_state)
    values_pad = jnp.pad(window_state, ((0, 0), (1, 1), (1, 1)))
    coeff_pad = jnp.pad(coeff, ((0, 0), (1, 1), (1, 1)))
    residual = before - window_state + time_ratio * flux_of(values_pad, coeff_pad)
    counter = jnp.arange(length).astype(jnp.float32)
    damping = jnp.exp(counter * (math.log(window_alpha) / length))
    spectrum = jnp.fft.fft(residual * damping[:, None, None], axis=0)
    spec_real = jnp.real(spectrum)
    spec_imag = jnp.imag(spectrum)
    frozen = conductance(conductivity, initial)
    weights = frozen_weights(jnp.pad(frozen, 1))

    def solve_one(element):
        frequency, part_real, part_imag = element
        shift_value, center, relative, half_span = frequency_scalars(frequency, length)

        def apply_op(search):
            return operator_image(jnp.pad(search, ((0, 0), (1, 1), (1, 1))), shift_value, weights)

        return chebyshev(jnp.stack([part_real, part_imag]), center, relative, half_span, apply_op, 1.0)

    solved = lax.map(solve_one, (jnp.arange(length).astype(jnp.int32), spec_real, spec_imag))
    combined = solved[:, 0] + 1j * solved[:, 1]
    correction = jnp.real(jnp.fft.ifft(combined, axis=0)) / damping[:, None, None]
    return window_state + correction
```

```python
import math

import jax
import jax.numpy as jnp
import numpy as np
from jax import lax
from jax.experimental import pallas as pl
from jax.experimental.pallas import tpu as pltpu
from jax.sharding import PartitionSpec as P

SWEEPS = 24
STEPS = 128
TAU = 2.0
ALPHA = 0.01
HALF = 12.0 * TAU

NQ, NZ = 16, 8
ROWS, COLS = 256, 512
STRIP = 16
BLOCK = 128
HALO = 24
SPAN = BLOCK + 2 * HALO
PAD = 8
SHIFT_PARTS = 4
MESH = pl.DeviceIdType.MESH

T_DELTA, T_IN, T_OUT, T_TWIDDLE, T_WIDTH = 0, 75, 76, 80, 96


def shift_of(frequency):
    beta = math.exp(math.log(ALPHA) / STEPS)
    angle = 2.0 * math.pi * frequency / STEPS
    return 1.0 - beta * math.cos(angle) + 1j * beta * math.sin(angle)


def polynomial_of(frequency):
    points = 64
    theta = (np.arange(points) + 0.5) * np.pi / points
    image_factor = shift_of(frequency) + HALF * (np.cos(theta) + 1.0)
    center = shift_of(frequency) + HALF
    relative = center / HALF
    solution = np.zeros(points, complex)
    remain = np.ones(points, complex)
    search = remain / center
    factor = 1.0 / relative
    for _ in range(SWEEPS):
        solution = solution + search
        remain = remain - image_factor * search
        renewed = 1.0 / (2.0 * relative - factor)
        search = renewed * factor * search + (2.0 * renewed / HALF) * remain
        factor = renewed
    values = solution + search
    first = [2.0 / points * np.sum(values * np.cos(k * theta)) for k in range(SWEEPS + 3)]
    first[0] = first[0] / 2
    second = [(first[k] - first[k + 2]) / 2 for k in range(SWEEPS + 1)]
    second[0] = first[0] - first[2] / 2
    return np.array(second)


def frequency_of(pair, slot):
    if pair:
        return pair + 16 * slot
    return 16 * slot if slot < 4 else 8 + 32 * (slot - 4)


def scalar_table():
    table = np.zeros((STEPS, T_WIDTH))
    for step in range(STEPS):
        plane, ring = step // NZ, step % NZ
        slot = plane % 8
        delta = polynomial_of(frequency_of(ring, slot))
        real, imag, last = delta.real, delta.imag, delta.real
        if ring == 0 and slot == 0:
            imag, last = 0.0 * imag, polynomial_of(64).real
        table[step, 0:75:3], table[step, 1:75:3], table[step, 2:75:3] = real, imag, last
        table[step, T_IN] = math.exp(math.log(ALPHA) * step / STEPS)
        table[step, T_OUT] = math.exp(-math.log(ALPHA) * step / STEPS) / STEPS
        for k in range(NZ):
            angle = 2.0 * math.pi * ring * k / STEPS
            table[step, T_TWIDDLE + 2 * k] = math.cos(angle)
            table[step, T_TWIDDLE + 2 * k + 1] = math.sin(angle)
    return table.astype(np.float32).reshape(-1)


def turned(value, turn):
    real, imag = value
    turn = turn % 1.0
    if turn == 0.0:
        return value
    if turn == 0.25:
        return ((-imag if imag is not None else None), real)
    if turn == 0.5:
        return (-real, -imag if imag is not None else None)
    if turn == 0.75:
        return (imag, -real)
    cosine, sine = math.cos(2 * math.pi * turn), math.sin(2 * math.pi * turn)
    if imag is None:
        return (cosine * real, sine * real)
    if turn % 0.25 == 0.125:
        scale = math.sqrt(0.5)
        if turn == 0.125:
            return (scale * (real - imag), scale * (real + imag))
        if turn == 0.375:
            return (-scale * (real + imag), scale * (real - imag))
        if turn == 0.625:
            return (scale * (imag - real), -scale * (real + imag))
        return (scale * (real + imag), scale * (imag - real))
    return (cosine * real - sine * imag, sine * real + cosine * imag)


def part_sum(left, right):
    if left is None:
        return right
    return left if right is None else left + right


def part_difference(left, right):
    if right is None:
        return left
    return -right if left is None else left - right


def plus(left, right):
    return (part_sum(left[0], right[0]), part_sum(left[1], right[1]))


def minus(left, right):
    return (part_difference(left[0], right[0]), part_difference(left[1], right[1]))


def conjugate(value):
    return (value[0], None if value[1] is None else -value[1])


def real_forward(values):
    count = len(values)
    if count == 2:
        return [(values[0] + values[1], None), (values[0] - values[1], None)]
    even, odd = real_forward(values[0::2]), real_forward(values[1::2])
    result = [None] * (count // 2 + 1)
    for k in range(count // 4 + 1):
        term = turned(odd[k], -k / count)
        result[k] = plus(even[k], term)
        if k < count // 4:
            result[count // 2 - k] = conjugate(minus(even[k], term))
    return result


def real_backward(values):
    count = 2 * (len(values) - 1)
    if count == 2:
        return [values[0][0] + values[1][0], values[0][0] - values[1][0]]
    even, odd = [], []
    for k in range(count // 4):
        mirror = conjugate(values[count // 2 - k])
        even.append(plus(values[k], mirror))
        odd.append(turned(minus(values[k], mirror), k / count))
    middle = values[count // 4]
    even.append((2.0 * middle[0], None))
    odd.append((-2.0 * middle[1], None))
    result = [None] * count
    result[0::2], result[1::2] = real_backward(even), real_backward(odd)
    return result


def complex_transform(values, sign):
    count = len(values)
    if count == 1:
        return values
    even = complex_transform(values[0::2], sign)
    odd = complex_transform(values[1::2], sign)
    odd = [turned(odd[k], sign * k / count) for k in range(count // 2)]
    return [plus(a, b) for a, b in zip(even, odd)] + [minus(a, b) for a, b in zip(even, odd)]


def conductance(conductivity, values):
    return conductivity * (1.0 + 0.5 * jnp.tanh(values))


def kernel(
    table, w, prior, cond, out,
    wp, qp, edge, prev, res, a1, yb, a2, sb, fsrc, fstrip, fq, ta, tb, xb, wts, a3, ub, a4, cb, corr,
    edge_send, edge_recv, shift_send, shift_recv,
    f1_send, f1_recv, f2_send, f2_recv, f3_send, f3_more, f3_recv,
    p2_send, p2_recv, p3_send, p3_recv, p4_send, p4_more, p4_recv,
    p6_send, p6_recv, p7_send, p7_recv, p8_send, p8_recv,
):
    n = lax.axis_index("tm")
    core = lax.axis_index("space")
    q, z = n // NZ, n % NZ
    half, slot = q // 8, q % 8
    other = 1 - core
    crossing = jnp.logical_or(q < 2, q >= NQ - 2)
    table_row = n * T_WIDTH

    def scalar(index):
        return table[table_row + index]

    def plane(distance):
        return ((q + distance) % NQ) * NZ + z

    def ring(distance):
        return q * NZ + (z + distance) % NZ

    def in_half(distance):
        return (8 * half + (slot + distance) % 8) * NZ + z

    def copy(src, dst, send, recv, step, space):
        return pltpu.make_async_remote_copy(
            src_ref=src, dst_ref=dst, send_sem=send, recv_sem=recv,
            device_id=(step, space), device_id_type=MESH,
        )

    barrier = pltpu.get_barrier_semaphore()

    def greet(step, space):
        pl.semaphore_signal(barrier, inc=1, device_id=(step, space), device_id_type=MESH)

    def greet_plane(d, carry):
        greet(plane(d), core)
        return carry

    def greet_ring(d, carry):
        greet(ring(d), core)
        return carry

    lax.fori_loop(1, NQ, greet_plane, 0)
    lax.fori_loop(1, NZ, greet_ring, 0)
    greet((n + STEPS - 1) % STEPS, core)
    greet(n, other)
    beyond = 14 * (1 - half)
    greet(beyond * NZ + z, other)
    greet((beyond + 1) * NZ + z, other)
    pl.semaphore_wait(barrier, NQ - 1 + NZ - 1 + 2 + jnp.where(crossing, 8, 0))

    part_rows = ROWS // SHIFT_PARTS
    after = (n + 1) % STEPS

    def shift_copy(src, part):
        rows = pl.ds(part * part_rows, part_rows)
        return copy(
            src.at[rows], prev.at[rows], shift_send.at[part], shift_recv.at[part], after, core
        )

    def edge_copies(row):
        return [
            copy(src.at[pl.ds(row, 8)], edge.at[k], edge_send.at[k], edge_recv.at[k], n, other)
            for k, src in enumerate((w, cond))
        ]

    edge_row = pl.multiple_of((1 - core) * (ROWS - 8), 8)
    for each in edge_copies(edge_row):
        each.start()

    @pl.when(n == STEPS - 1)
    def _():
        for part in range(SHIFT_PARTS):
            shift_copy(prior, part).start()

    @pl.when(n != STEPS - 1)
    def _():
        for part in range(SHIFT_PARTS):
            shift_copy(w, part).start()

    def f1_copy(d):
        target = (q + d) % NQ
        rows = pl.ds(pl.multiple_of(target * STRIP, STRIP), STRIP)
        return copy(
            fsrc.at[:, rows], fstrip, f1_send.at[d], f1_recv.at[0], target * NZ + z, core
        )

    def f2_copy(d):
        return copy(fstrip, fstrip, f2_send.at[d], f2_recv.at[0], ring(d), core)

    @pl.when(n == STEPS - 1)
    def _():
        fsrc[0] = conductance(cond[...], prior[...])

        def start(d, carry):
            f1_copy(d).start()
            return carry

        lax.fori_loop(1, NQ, start, 0)
        fstrip[...] = fsrc[:, (NQ - 1) * STRIP : NQ * STRIP]

    zero_rows = jnp.zeros((8, COLS), jnp.float32)
    wp[PAD : PAD + ROWS] = w[...]
    qp[PAD : PAD + ROWS] = conductance(cond[...], w[...])
    for ref in (wp, qp):
        ref[0:PAD] = zero_rows
        ref[PAD + ROWS : PAD + ROWS + 8] = zero_rows
    for each in edge_copies(edge_row):
        each.wait_recv()
    beside = pl.multiple_of((1 - core) * (PAD + ROWS), 8)
    wp[pl.ds(beside, 8)] = edge[0]
    qp[pl.ds(beside, 8)] = conductance(edge[1], edge[0])

    column = lax.broadcasted_iota(jnp.int32, (8, COLS), 1)
    first_column, last_column = column == 0, column == COLS - 1

    def four_beside(window):
        center = window[8:16]
        return (
            window[7:15],
            window[9:17],
            pltpu.roll(center, 1, 1),
            pltpu.roll(center, COLS - 1, 1),
        )

    def inside_four(window):
        up, down, left, right = four_beside(window)
        return (up, down, jnp.where(first_column, 0.0, left), jnp.where(last_column, 0.0, right))

    damping = scalar(T_IN)

    def flux_rows(t, carry):
        rows = pl.ds(pl.multiple_of(t * 8, 8), 24)
        state, coeff = wp[rows], qp[rows]
        here, coeff_here = state[8:16], coeff[8:16]
        total = -here
        for near, near_coeff in zip(inside_four(state), inside_four(coeff)):
            total = total + (0.5 * TAU) * (coeff_here + near_coeff) * (near - here)
        res[pl.ds(pl.multiple_of(t * 8, 8), 8)] = total
        return carry

    lax.fori_loop(0, ROWS // 8, flux_rows, 0)

    def p2_copy(target, d):
        rows = pl.ds(pl.multiple_of(target * STRIP, STRIP), STRIP)
        return copy(
            res.at[rows], a1.at[q], p2_send.at[d], p2_recv.at[d], target * NZ + z, core
        )

    strips_each = NQ // SHIFT_PARTS
    for part in range(SHIFT_PARTS):
        shift_copy(w, part).wait_recv()
        rows = slice(part * part_rows, (part + 1) * part_rows)
        res[rows] = (res[rows] + prev[rows]) * damping

        def send(k, carry):
            target = part * strips_each + k

            @pl.when(target != q)
            def _():
                p2_copy(target, (target - q + NQ) % NQ).start()

            return carry

        lax.fori_loop(0, strips_each, send, 0)
    a1[q] = res[pl.ds(pl.multiple_of(q * STRIP, STRIP), STRIP)]

    @pl.when(z == NZ - 1)
    def _():
        @pl.when(q != NQ - 1)
        def _():
            f1_copy(1).wait_recv()

        def start(d, carry):
            f2_copy(d).start()
            return carry

        lax.fori_loop(1, NZ, start, 0)

    def p2_arrived(d, carry):
        p2_copy((q + d) % NQ, d).wait_recv()
        return carry

    lax.fori_loop(1, NQ, p2_arrived, 0)

    def tiles(body):
        def one(t, carry):
            rows = pl.ds(pl.multiple_of((t // 4) * 8, 8), 8)
            columns = pl.ds(pl.multiple_of((t % 4) * 128, 128), 128)
            body(rows, columns)
            return carry

        lax.fori_loop(0, 8, one, 0)

    def plane_forward(rows, columns):
        result = real_forward([a1[k, rows, columns] for k in range(NQ)])
        yb[0, 0, rows, columns] = result[0][0]
        yb[0, 1, rows, columns] = result[8][0]
        for k in range(1, 8):
            yb[k, 0, rows, columns] = result[k][0]
            yb[k, 1, rows, columns] = result[k][1]

    tiles(plane_forward)

    def ring_copy(src, dst, send, recv, d):
        return copy(src.at[(z + d) % NZ], dst.at[z], send.at[d], recv.at[d], ring(d), core)

    def p3_copy(d):
        return ring_copy(yb, a2, p3_send, p3_recv, d)

    def p3_start(d, carry):
        p3_copy(d).start()
        return carry

    lax.fori_loop(1, NZ, p3_start, 0)
    a2[z] = yb[z]

    def main_copy(src, dst, send, recv, d):
        rows = pl.ds(pl.multiple_of(PAD + HALO + slot * STRIP, 8), STRIP)
        return copy(src((slot + d) % 8), dst.at[:, rows], send.at[d], recv.at[d], in_half(d), core)

    edges = ((0, 0, 16, 152), (1, 0, 8, 168), (6, 8, 8, 0), (7, 0, 16, 8))

    def more_copy(src, dst, send, recv, kind, target_slot):
        index, first, count, offset = edges[kind]
        same = (half == 0) if index >= 6 else (half == 1)
        return copy(
            src(target_slot).at[:, pl.ds(first, count)],
            dst.at[:, pl.ds(PAD + offset, count)],
            send.at[target_slot],
            recv.at[8 + kind],
            (8 * (1 - half) + target_slot) * NZ + z,
            jnp.where(same, core, other),
        )

    def spread_start(src, dst, send, more, recv):
        def start(d, carry):
            main_copy(src, dst, send, recv, d).start()
            return carry

        lax.fori_loop(1, 8, start, 0)
        for kind in range(4):

            @pl.when(slot == edges[kind][0])
            def _():
                def start_more(k, carry):
                    more_copy(src, dst, more, recv, kind, k).start()
                    return carry

                lax.fori_loop(0, 8, start_more, 0)

        own = pl.ds(pl.multiple_of(PAD + HALO + slot * STRIP, 8), STRIP)
        dst[:, own] = src(slot)[...]

    def spread_arrived(src, dst, send, more, recv):
        def arrived(d, carry):
            main_copy(src, dst, send, recv, d).wait_recv()
            return carry

        lax.fori_loop(1, 8, arrived, 0)
        for kind in range(4):
            more_copy(src, dst, more, recv, kind, 0).wait_recv()

    def spread_sent(src, dst, send, more, recv):
        def sent(d, carry):
            main_copy(src, dst, send, recv, d).wait_send()
            return carry

        lax.fori_loop(1, 8, sent, 0)
        for kind in range(4):

            @pl.when(slot == edges[kind][0])
            def _():
                def sent_more(k, carry):
                    more_copy(src, dst, more, recv, kind, k).wait_send()
                    return carry

                lax.fori_loop(0, 8, sent_more, 0)

    @pl.when(z != NZ - 1)
    def _():
        f2_copy(1).wait_recv()

    f3 = (lambda k: fstrip, fq, f3_send, f3_more, f3_recv)
    spread_start(*f3)

    for field in range(2):
        for ref in (ta, tb):
            ref[field, 0:PAD] = zero_rows
            ref[field, PAD + SPAN : PAD + SPAN + PAD] = zero_rows
        tb[field, PAD : PAD + SPAN] = jnp.zeros((SPAN, COLS), jnp.float32)
    fq[0, 0:PAD] = zero_rows
    fq[0, PAD + SPAN : PAD + SPAN + PAD] = zero_rows

    def p3_arrived(d, carry):
        p3_copy(d).wait_recv()
        return carry

    lax.fori_loop(1, NZ, p3_arrived, 0)

    twiddle = [(scalar(T_TWIDDLE + 2 * k), scalar(T_TWIDDLE + 2 * k + 1)) for k in range(NZ)]

    @pl.when(z != 0)
    def _():
        def ring_forward(rows, columns):
            values = []
            for k in range(NZ):
                real, imag = a2[k, 0, rows, columns], a2[k, 1, rows, columns]
                cosine, sine = twiddle[k]
                if k:
                    real, imag = cosine * real + sine * imag, cosine * imag - sine * real
                values.append((real, imag))
            for k, value in enumerate(complex_transform(values, -1.0)):
                sb[k, 0, rows, columns] = value[0]
                sb[k, 1, rows, columns] = value[1]

        tiles(ring_forward)

    @pl.when(z == 0)
    def _():
        def ring_forward(rows, columns):
            even = real_forward([a2[k, 0, rows, columns] for k in range(NZ)])
            sb[0, 0, rows, columns] = even[0][0]
            sb[0, 1, rows, columns] = even[4][0]
            odd = []
            for k in range(4):
                value = (a2[k, 1, rows, columns], -a2[k + 4, 1, rows, columns])
                odd.append(turned(value, -k / 16))
            odd = complex_transform(odd, -1.0)
            for k, value in list(zip((1, 2, 3), even[1:4])) + list(zip((4, 5, 6, 7), odd)):
                sb[k, 0, rows, columns] = value[0]
                sb[k, 1, rows, columns] = value[1]

        tiles(ring_forward)

    p4 = (lambda k: sb.at[k], ta, p4_send, p4_more, p4_recv)
    spread_start(*p4)

    spread_arrived(*f3)
    top = core * ROWS + half * BLOCK - HALO

    def weight_rows(t, carry):
        rows = pl.ds(pl.multiple_of(t * 8, 8), 8)
        window = fq[0, pl.ds(pl.multiple_of(t * 8, 8), 24)]
        up, down, left, right = inside_four(window)
        row = lax.broadcasted_iota(jnp.int32, (8, COLS), 0) + (top + t * 8)
        up = jnp.where(row == 0, 0.0, up)
        down = jnp.where(row == 2 * ROWS - 1, 0.0, down)
        here = window[8:16]
        scale = TAU / HALF
        up, down, left, right = (scale * (here + each) for each in (up, down, left, right))
        wts[4, rows] = up + down + left + right - 2.0
        wts[0, rows] = jnp.where(row == 0, 0.0, up)
        wts[1, rows] = jnp.where(row == 2 * ROWS - 1, 0.0, down)
        wts[2, rows] = jnp.where(first_column, 0.0, left)
        wts[3, rows] = jnp.where(last_column, 0.0, right)
        return carry

    lax.fori_loop(0, SPAN // 8, weight_rows, 0)
    spread_arrived(*p4)

    exact = (HALO // 8, (HALO + BLOCK) // 8)
    first = [scalar(T_DELTA + k) for k in range(3)]

    def begin(t, carry):
        rows = pl.ds(pl.multiple_of(t * 8 + PAD + HALO, 8), 8)
        into = pl.ds(pl.multiple_of(t * 8, 8), 8)
        real, imag = ta[0, rows], ta[1, rows]
        xb[0, into] = first[0] * real - first[1] * imag
        xb[1, into] = first[1] * real + first[2] * imag
        return carry

    lax.fori_loop(0, BLOCK // 8, begin, 0)

    def swept(now, old, t):
        rows = pl.ds(pl.multiple_of(t * 8 + PAD, 8), 8)
        weight_row = pl.ds(pl.multiple_of(t * 8, 8), 8)
        up_w, down_w, left_w, right_w, here_w = (wts[k, weight_row] for k in range(5))
        fresh, here = [], []
        for field in range(2):
            window = now[field, pl.ds(pl.multiple_of(t * 8, 8), 24)]
            up, down, left, right = four_beside(window)
            center = window[8:16]
            value = here_w * center - old[field, rows]
            value = value - up_w * up - down_w * down - (left_w * left + right_w * right)
            old[field, rows] = value
            fresh.append(value)
            here.append(center)
        return here, fresh

    def two_sweeps(m, carry):
        k = 2 * m + 1
        low = k // 8
        lax.fori_loop(low, SPAN // 8 - low, lambda t, c: (swept(ta, tb, t), c)[1], 0)
        low = (k + 1) // 8
        factors = [scalar(T_DELTA + 3 * k + each) for each in range(6)]
        lax.fori_loop(low, exact[0], lambda t, c: (swept(tb, ta, t), c)[1], 0)

        def add(t, c):
            here, fresh = swept(tb, ta, t)
            into = pl.ds(pl.multiple_of((t - exact[0]) * 8, 8), 8)
            xb[0, into] = xb[0, into] + (
                factors[0] * here[0] - factors[1] * here[1]
                + (factors[3] * fresh[0] - factors[4] * fresh[1])
            )
            xb[1, into] = xb[1, into] + (
                factors[1] * here[0] + factors[2] * here[1]
                + (factors[4] * fresh[0] + factors[5] * fresh[1])
            )
            return c

        lax.fori_loop(exact[0], exact[1], add, 0)
        lax.fori_loop(exact[1], SPAN // 8 - low, lambda t, c: (swept(tb, ta, t), c)[1], 0)
        return carry

    lax.fori_loop(0, SWEEPS // 2, two_sweeps, 0)

    def p6_copy(d):
        rows = pl.ds(pl.multiple_of(((slot + d) % 8) * STRIP, STRIP), STRIP)
        return copy(
            xb.at[:, rows], a3.at[slot], p6_send.at[d], p6_recv.at[d], in_half(d), core
        )

    def p6_start(d, carry):
        p6_copy(d).start()
        return carry

    def p6_arrived(d, carry):
        p6_copy(d).wait_recv()
        return carry

    lax.fori_loop(1, 8, p6_start, 0)
    a3[slot] = xb[:, pl.ds(pl.multiple_of(slot * STRIP, STRIP), STRIP)]
    lax.fori_loop(1, 8, p6_arrived, 0)

    @pl.when(z != 0)
    def _():
        def ring_backward(rows, columns):
            values = [(a3[k, 0, rows, columns], a3[k, 1, rows, columns]) for k in range(8)]
            for k, (real, imag) in enumerate(complex_transform(values, 1.0)):
                cosine, sine = twiddle[k]
                if k:
                    real, imag = cosine * real - sine * imag, cosine * imag + sine * real
                ub[k, 0, rows, columns] = real
                ub[k, 1, rows, columns] = imag

        tiles(ring_backward)

    @pl.when(z == 0)
    def _():
        def ring_backward(rows, columns):
            values = [(a3[k, 0, rows, columns], a3[k, 1, rows, columns]) for k in range(8)]
            even = [(values[0][0], None)] + values[1:4] + [(values[0][1], None)]
            for k, value in enumerate(real_backward(even)):
                ub[k, 0, rows, columns] = value
            for k, value in enumerate(complex_transform(values[4:8], 1.0)):
                real, imag = turned(value, k / 16)
                ub[k, 1, rows, columns] = 2.0 * real
                ub[k + 4, 1, rows, columns] = -2.0 * imag

        tiles(ring_backward)

    def p7_copy(d):
        return ring_copy(ub, a4, p7_send, p7_recv, d)

    def p7_start(d, carry):
        p7_copy(d).start()
        return carry

    def p7_arrived(d, carry):
        p7_copy(d).wait_recv()
        return carry

    lax.fori_loop(1, NZ, p7_start, 0)
    a4[z] = ub[z]
    lax.fori_loop(1, NZ, p7_arrived, 0)

    def plane_backward(rows, columns):
        values = [(a4[k, 0, rows, columns], a4[k, 1, rows, columns]) for k in range(8)]
        values = [(values[0][0], None)] + values[1:] + [(values[0][1], None)]
        for k, value in enumerate(real_backward(values)):
            cb[k, rows, columns] = value

    tiles(plane_backward)

    own_rows = pl.ds(pl.multiple_of(q * STRIP, STRIP), STRIP)

    def p8_copy(d):
        return copy(
            cb.at[(q + d) % NQ], corr.at[own_rows], p8_send.at[d], p8_recv.at[d], plane(d), core
        )

    def p8_start(d, carry):
        p8_copy(d).start()
        return carry

    def p8_arrived(d, carry):
        p8_copy(d).wait_recv()
        return carry

    lax.fori_loop(1, NQ, p8_start, 0)
    corr[own_rows] = cb[q]

    for each in edge_copies(edge_row):
        each.wait_send()
    for part in range(SHIFT_PARTS):
        shift_copy(w, part).wait_send()

    @pl.when(n == STEPS - 1)
    def _():
        def sent(d, carry):
            f1_copy(d).wait_send()
            return carry

        lax.fori_loop(1, NQ, sent, 0)

    @pl.when(z == NZ - 1)
    def _():
        def sent(d, carry):
            f2_copy(d).wait_send()
            return carry

        lax.fori_loop(1, NZ, sent, 0)

    def plane_sent(d, carry):
        p2_copy((q + d) % NQ, d).wait_send()
        return carry

    lax.fori_loop(1, NQ, plane_sent, 0)

    def ring_sent(d, carry):
        p3_copy(d).wait_send()
        p6_copy(d).wait_send()
        p7_copy(d).wait_send()
        return carry

    lax.fori_loop(1, NZ, ring_sent, 0)
    spread_sent(*f3)
    spread_sent(*p4)

    lax.fori_loop(1, NQ, p8_arrived, 0)
    out[...] = w[...] + scalar(T_OUT) * corr[...]

    def last_sent(d, carry):
        p8_copy(d).wait_send()
        return carry

    lax.fori_loop(1, NQ, last_sent, 0)


def body(window_state, prior_window, conductivity):
    f32 = jnp.float32
    dma = pltpu.SemaphoreType.DMA
    vmem = pl.BlockSpec(memory_space=pltpu.VMEM)
    padded_rows = ROWS + 2 * PAD
    span = SPAN + 2 * PAD
    shapes = [
        (padded_rows, COLS),
        (padded_rows, COLS),
        (2, 8, COLS),
        (ROWS, COLS),
        (ROWS, COLS),
        (NQ, STRIP, COLS),
        (8, 2, STRIP, COLS),
        (8, 2, STRIP, COLS),
        (8, 2, STRIP, COLS),
        (1, ROWS, COLS),
        (1, STRIP, COLS),
        (1, span, COLS),
        (2, span, COLS),
        (2, span, COLS),
        (2, BLOCK, COLS),
        (5, SPAN, COLS),
        (8, 2, STRIP, COLS),
        (8, 2, STRIP, COLS),
        (8, 2, STRIP, COLS),
        (NQ, STRIP, COLS),
        (ROWS, COLS),
    ]
    sems = [2, 2, SHIFT_PARTS, SHIFT_PARTS, 16, 1, 8, 1, 8, 8, 12, 16, 16, 8, 8, 8, 8, 12]
    sems += [8, 8, 8, 8, 16, 16]
    updated = pl.pallas_call(
        kernel,
        out_shape=jax.ShapeDtypeStruct((ROWS, COLS), f32),
        in_specs=[pl.BlockSpec(memory_space=pltpu.SMEM), vmem, vmem, vmem],
        out_specs=vmem,
        scratch_shapes=[pltpu.VMEM(shape, f32) for shape in shapes]
        + [dma((count,)) for count in sems],
        compiler_params=pltpu.CompilerParams(
            collective_id=0, has_side_effects=True, vmem_limit_bytes=40 * 1024 * 1024
        ),
    )(jnp.asarray(scalar_table()), window_state[0], prior_window[0], conductivity)
    return updated[None]


def solution(mesh):
    in_specs = (P("tm", "space", None), P("tm", "space", None), P("space", None))
    out_specs = P("tm", "space", None)
    return jax.shard_map(body, mesh=mesh, in_specs=in_specs, out_specs=out_specs, check_vma=False)
```

```python
import math

import jax
import jax.numpy as jnp
import numpy as np
from jax import lax
from jax.experimental import pallas as pl
from jax.experimental.pallas import tpu as pltpu
from jax.sharding import PartitionSpec as P

SWEEPS = 24
STEPS = 128
TAU = 2.0
ALPHA = 0.01
HALF = 12.0 * TAU

NQ, NZ = 16, 8
ROWS, COLS = 256, 512
STRIP = 16
BLOCK = 128
HALO = 24
SPAN = BLOCK + 2 * HALO
PAD = 8
GROUPS = SPAN // 8
SHIFT_PARTS = 4
MESH = pl.DeviceIdType.MESH

T_DELTA, T_IN, T_OUT, T_TWIDDLE, T_WIDTH = 0, 75, 76, 80, 96


def shift_of(frequency):
    beta = math.exp(math.log(ALPHA) / STEPS)
    angle = 2.0 * math.pi * frequency / STEPS
    return 1.0 - beta * math.cos(angle) + 1j * beta * math.sin(angle)


def polynomial_of(frequency):
    points = 64
    theta = (np.arange(points) + 0.5) * np.pi / points
    image_factor = shift_of(frequency) + HALF * (np.cos(theta) + 1.0)
    center = shift_of(frequency) + HALF
    relative = center / HALF
    solution = np.zeros(points, complex)
    remain = np.ones(points, complex)
    search = remain / center
    factor = 1.0 / relative
    for _ in range(SWEEPS):
        solution = solution + search
        remain = remain - image_factor * search
        renewed = 1.0 / (2.0 * relative - factor)
        search = renewed * factor * search + (2.0 * renewed / HALF) * remain
        factor = renewed
    values = solution + search
    first = [2.0 / points * np.sum(values * np.cos(k * theta)) for k in range(SWEEPS + 3)]
    first[0] = first[0] / 2
    second = [(first[k] - first[k + 2]) / 2 for k in range(SWEEPS + 1)]
    second[0] = first[0] - first[2] / 2
    return np.array(second)


def frequency_of(pair, slot):
    if pair:
        return pair + 16 * slot
    return 16 * slot if slot < 4 else 8 + 32 * (slot - 4)


def scalar_table():
    table = np.zeros((STEPS, T_WIDTH))
    for step in range(STEPS):
        plane, ring = step // NZ, step % NZ
        slot = plane % 8
        delta = polynomial_of(frequency_of(ring, slot))
        real, imag, last = delta.real, delta.imag, delta.real
        if ring == 0 and slot == 0:
            imag, last = 0.0 * imag, polynomial_of(64).real
        table[step, 0:75:3], table[step, 1:75:3], table[step, 2:75:3] = real, imag, last
        table[step, T_IN] = math.exp(math.log(ALPHA) * step / STEPS)
        table[step, T_OUT] = math.exp(-math.log(ALPHA) * step / STEPS) / STEPS
        for k in range(NZ):
            angle = 2.0 * math.pi * ring * k / STEPS
            table[step, T_TWIDDLE + 2 * k] = math.cos(angle)
            table[step, T_TWIDDLE + 2 * k + 1] = math.sin(angle)
    return table.astype(np.float32).reshape(-1)


def turned(value, turn):
    real, imag = value
    turn = turn % 1.0
    if turn == 0.0:
        return value
    if turn == 0.25:
        return ((-imag if imag is not None else None), real)
    if turn == 0.5:
        return (-real, -imag if imag is not None else None)
    if turn == 0.75:
        return (imag, -real)
    cosine, sine = math.cos(2 * math.pi * turn), math.sin(2 * math.pi * turn)
    if imag is None:
        return (cosine * real, sine * real)
    if turn % 0.25 == 0.125:
        scale = math.sqrt(0.5)
        if turn == 0.125:
            return (scale * (real - imag), scale * (real + imag))
        if turn == 0.375:
            return (-scale * (real + imag), scale * (real - imag))
        if turn == 0.625:
            return (scale * (imag - real), -scale * (real + imag))
        return (scale * (real + imag), scale * (imag - real))
    return (cosine * real - sine * imag, sine * real + cosine * imag)


def part_sum(left, right):
    if left is None:
        return right
    return left if right is None else left + right


def part_difference(left, right):
    if right is None:
        return left
    return -right if left is None else left - right


def plus(left, right):
    return (part_sum(left[0], right[0]), part_sum(left[1], right[1]))


def minus(left, right):
    return (part_difference(left[0], right[0]), part_difference(left[1], right[1]))


def conjugate(value):
    return (value[0], None if value[1] is None else -value[1])


def real_forward(values):
    count = len(values)
    if count == 2:
        return [(values[0] + values[1], None), (values[0] - values[1], None)]
    even, odd = real_forward(values[0::2]), real_forward(values[1::2])
    result = [None] * (count // 2 + 1)
    for k in range(count // 4 + 1):
        term = turned(odd[k], -k / count)
        result[k] = plus(even[k], term)
        if k < count // 4:
            result[count // 2 - k] = conjugate(minus(even[k], term))
    return result


def real_backward(values):
    count = 2 * (len(values) - 1)
    if count == 2:
        return [values[0][0] + values[1][0], values[0][0] - values[1][0]]
    even, odd = [], []
    for k in range(count // 4):
        mirror = conjugate(values[count // 2 - k])
        even.append(plus(values[k], mirror))
        odd.append(turned(minus(values[k], mirror), k / count))
    middle = values[count // 4]
    even.append((2.0 * middle[0], None))
    odd.append((-2.0 * middle[1], None))
    result = [None] * count
    result[0::2], result[1::2] = real_backward(even), real_backward(odd)
    return result


def complex_transform(values, sign):
    count = len(values)
    if count == 1:
        return values
    even = complex_transform(values[0::2], sign)
    odd = complex_transform(values[1::2], sign)
    odd = [turned(odd[k], sign * k / count) for k in range(count // 2)]
    return [plus(a, b) for a, b in zip(even, odd)] + [minus(a, b) for a, b in zip(even, odd)]


def conductance(conductivity, values):
    return conductivity * (1.0 + 0.5 * jnp.tanh(values))


def kernel(
    table, w, prior, cond_in, out,
    cond, wp, qp, edge, prev, res, a1, yb, a2, sb, fsrc, fstrip, fmix, fq, ta, ti, tj, xi, xb,
    wts, west, a3, ub, a4, cb, corr, load_sem,
    edge_send, edge_recv, shift_send, shift_recv,
    f1_send, f1_recv, f2_send, f2_recv, f3_send, f3_more, f3_recv,
    p2_send, p2_recv, p3_send, p3_recv, p4_send, p4_more, p4_recv,
    p6_send, p6_recv, p7_send, p7_recv, p8_send, p8_recv,
):
    n = lax.axis_index("tm")
    core = lax.axis_index("space")
    q, z = n // NZ, n % NZ
    half, slot = q // 8, q % 8
    other = 1 - core
    crossing = jnp.logical_or(q < 2, q >= NQ - 2)
    table_row = n * T_WIDTH

    def scalar(index):
        return table[table_row + index]

    def plane(distance):
        return ((q + distance) % NQ) * NZ + z

    def ring(distance):
        return q * NZ + (z + distance) % NZ

    def in_half(distance):
        return (8 * half + (slot + distance) % 8) * NZ + z

    def copy(src, dst, send, recv, step, space):
        return pltpu.make_async_remote_copy(
            src_ref=src, dst_ref=dst, send_sem=send, recv_sem=recv,
            device_id=(step, space), device_id_type=MESH,
        )

    loads = [
        pltpu.make_async_copy(w, wp.at[pl.ds(PAD, ROWS)], load_sem.at[0]),
        pltpu.make_async_copy(cond_in, cond, load_sem.at[1]),
    ]
    for each in loads:
        each.start()
    barrier = pltpu.get_barrier_semaphore()

    def greet(step, space):
        pl.semaphore_signal(barrier, inc=1, device_id=(step, space), device_id_type=MESH)

    def greet_plane(d, carry):
        greet(plane(d), core)
        return carry

    def greet_ring(d, carry):
        greet(ring(d), core)
        return carry

    lax.fori_loop(1, NQ, greet_plane, 0)
    lax.fori_loop(1, NZ, greet_ring, 0)
    greet((n + STEPS - 1) % STEPS, core)
    greet(n, other)
    beyond = 14 * (1 - half)
    greet(beyond * NZ + z, other)
    greet((beyond + 1) * NZ + z, other)
    pl.semaphore_wait(barrier, NQ - 1 + NZ - 1 + 2 + jnp.where(crossing, 8, 0))

    part_rows = ROWS // SHIFT_PARTS
    after = (n + 1) % STEPS

    def shift_copy(src, part):
        rows = pl.ds(part * part_rows, part_rows)
        return copy(
            src.at[rows], prev.at[rows], shift_send.at[part], shift_recv.at[part], after, core
        )

    def edge_copies(row):
        return [
            copy(src.at[pl.ds(row, 8)], edge.at[k], edge_send.at[k], edge_recv.at[k], n, other)
            for k, src in enumerate((w, cond_in))
        ]

    edge_row = pl.multiple_of((1 - core) * (ROWS - 8), 8)
    for each in edge_copies(edge_row):
        each.start()

    @pl.when(n == STEPS - 1)
    def _():
        for part in range(SHIFT_PARTS):
            shift_copy(prior, part).start()

    @pl.when(n != STEPS - 1)
    def _():
        for part in range(SHIFT_PARTS):
            shift_copy(w, part).start()

    for each in loads:
        each.wait()

    def f1_copy(d):
        target = (q + d) % NQ
        rows = pl.ds(pl.multiple_of(target * STRIP, STRIP), STRIP)
        return copy(
            fsrc.at[:, rows], fstrip, f1_send.at[d], f1_recv.at[0], target * NZ + z, core
        )

    def f2_copy(d):
        return copy(fstrip, fstrip, f2_send.at[d], f2_recv.at[0], ring(d), core)

    @pl.when(n == STEPS - 1)
    def _():
        load = pltpu.make_async_copy(prior, fsrc.at[0], load_sem.at[2])
        load.start()
        load.wait()
        fsrc[0] = conductance(cond[...], fsrc[0])

        def start(d, carry):
            f1_copy(d).start()
            return carry

        lax.fori_loop(1, NQ, start, 0)
        fstrip[...] = fsrc[:, (NQ - 1) * STRIP : NQ * STRIP]

    zero_rows = jnp.zeros((8, COLS), jnp.float32)
    qp[PAD : PAD + ROWS] = conductance(cond[...], wp[PAD : PAD + ROWS])
    for ref in (wp, qp):
        ref[0:PAD] = zero_rows
        ref[PAD + ROWS : PAD + ROWS + 8] = zero_rows
    for each in edge_copies(edge_row):
        each.wait_recv()
    beside = pl.multiple_of((1 - core) * (PAD + ROWS), 8)
    wp[pl.ds(beside, 8)] = edge[0]
    qp[pl.ds(beside, 8)] = conductance(edge[1], edge[0])

    column = lax.broadcasted_iota(jnp.int32, (8, COLS), 1)
    first_column, last_column = column == 0, column == COLS - 1

    def four_beside(window):
        center = window[8:16]
        return (
            window[7:15],
            window[9:17],
            pltpu.roll(center, 1, 1),
            pltpu.roll(center, COLS - 1, 1),
        )

    def inside_four(window):
        up, down, left, right = four_beside(window)
        return (up, down, jnp.where(first_column, 0.0, left), jnp.where(last_column, 0.0, right))

    damping = scalar(T_IN)

    def flux_rows(t, carry):
        rows = pl.ds(pl.multiple_of(t * 8, 8), 24)
        state, coeff = wp[rows], qp[rows]
        here, coeff_here = state[8:16], coeff[8:16]
        total = -here
        for near, near_coeff in zip(inside_four(state), inside_four(coeff)):
            total = total + (0.5 * TAU) * (coeff_here + near_coeff) * (near - here)
        res[pl.ds(pl.multiple_of(t * 8, 8), 8)] = total
        return carry

    lax.fori_loop(0, ROWS // 8, flux_rows, 0)

    def p2_copy(target, d):
        rows = pl.ds(pl.multiple_of(target * STRIP, STRIP), STRIP)
        return copy(
            res.at[rows], a1.at[q], p2_send.at[d], p2_recv.at[d], target * NZ + z, core
        )

    strips_each = NQ // SHIFT_PARTS
    for part in range(SHIFT_PARTS):
        shift_copy(w, part).wait_recv()
        rows = slice(part * part_rows, (part + 1) * part_rows)
        res[rows] = (res[rows] + prev[rows]) * damping

        def send(k, carry):
            target = part * strips_each + k

            @pl.when(target != q)
            def _():
                p2_copy(target, (target - q + NQ) % NQ).start()

            return carry

        lax.fori_loop(0, strips_each, send, 0)
    a1[q] = res[pl.ds(pl.multiple_of(q * STRIP, STRIP), STRIP)]

    @pl.when(z == NZ - 1)
    def _():
        @pl.when(q != NQ - 1)
        def _():
            f1_copy(1).wait_recv()

        def start(d, carry):
            f2_copy(d).start()
            return carry

        lax.fori_loop(1, NZ, start, 0)

    def p2_arrived(d, carry):
        p2_copy((q + d) % NQ, d).wait_recv()
        return carry

    lax.fori_loop(1, NQ, p2_arrived, 0)

    def tiles(body):
        def one(t, carry):
            rows = pl.ds(pl.multiple_of((t // 4) * 8, 8), 8)
            body(rows, t % 4)
            return carry

        lax.fori_loop(0, 8, one, 0)

    def tile_columns(u):
        return pl.ds(pl.multiple_of(u * 128, 128), 128)

    def plane_forward(rows, u):
        columns = tile_columns(u)
        result = real_forward([a1[k, rows, columns] for k in range(NQ)])
        yb[0, 0, rows, columns] = result[0][0]
        yb[0, 1, rows, columns] = result[8][0]
        for k in range(1, 8):
            yb[k, 0, rows, columns] = result[k][0]
            yb[k, 1, rows, columns] = result[k][1]

    tiles(plane_forward)

    def ring_copy(src, dst, send, recv, d):
        return copy(src.at[(z + d) % NZ], dst.at[z], send.at[d], recv.at[d], ring(d), core)

    def p3_copy(d):
        return ring_copy(yb, a2, p3_send, p3_recv, d)

    def p3_start(d, carry):
        p3_copy(d).start()
        return carry

    lax.fori_loop(1, NZ, p3_start, 0)
    a2[z] = yb[z]

    def main_copy(src, dst, send, recv, d):
        rows = pl.ds(pl.multiple_of(HALO + slot * STRIP, 8), STRIP)
        return copy(src((slot + d) % 8), dst.at[:, :, rows], send.at[d], recv.at[d], in_half(d), core)

    edges = ((0, 0, 16, 152), (1, 0, 8, 168), (6, 8, 8, 0), (7, 0, 16, 8))

    def more_copy(src, dst, send, recv, kind, target_slot):
        index, first, count, offset = edges[kind]
        same = (half == 0) if index >= 6 else (half == 1)
        return copy(
            src(target_slot).at[:, :, pl.ds(first, count)],
            dst.at[:, :, pl.ds(offset, count)],
            send.at[target_slot],
            recv.at[8 + kind],
            (8 * (1 - half) + target_slot) * NZ + z,
            jnp.where(same, core, other),
        )

    def spread_start(src, dst, send, more, recv):
        def start(d, carry):
            main_copy(src, dst, send, recv, d).start()
            return carry

        lax.fori_loop(1, 8, start, 0)
        for kind in range(4):

            @pl.when(slot == edges[kind][0])
            def _():
                def start_more(k, carry):
                    more_copy(src, dst, more, recv, kind, k).start()
                    return carry

                lax.fori_loop(0, 8, start_more, 0)

        own = pl.ds(pl.multiple_of(HALO + slot * STRIP, 8), STRIP)
        dst[:, :, own] = src(slot)[...]

    def spread_arrived(src, dst, send, more, recv):
        def arrived(d, carry):
            main_copy(src, dst, send, recv, d).wait_recv()
            return carry

        lax.fori_loop(1, 8, arrived, 0)
        for kind in range(4):
            more_copy(src, dst, more, recv, kind, 0).wait_recv()

    def spread_sent(src, dst, send, more, recv):
        def sent(d, carry):
            main_copy(src, dst, send, recv, d).wait_send()
            return carry

        lax.fori_loop(1, 8, sent, 0)
        for kind in range(4):

            @pl.when(slot == edges[kind][0])
            def _():
                def sent_more(k, carry):
                    more_copy(src, dst, more, recv, kind, k).wait_send()
                    return carry

                lax.fori_loop(0, 8, sent_more, 0)

    @pl.when(z != NZ - 1)
    def _():
        f2_copy(1).wait_recv()

    lane = lax.broadcasted_iota(jnp.int32, (8, 128), 1)
    sublane = lax.broadcasted_iota(jnp.int32, (8, 128), 0)

    def picked(parts, index, choice):
        parts = [jnp.take_along_axis(part, index, axis=1) for part in parts]
        low = jnp.where(choice == 0, parts[0], parts[1])
        return jnp.where(choice < 2, low, jnp.where(choice == 2, parts[2], parts[3]))

    def columns_spread(parts):
        return [picked(parts, 4 * (lane % 32) + u, lane // 32) for u in range(4)]

    def columns_joined(parts):
        return [picked(parts, 32 * u + lane // 4, lane % 4) for u in range(4)]

    def quarters(value):
        return [value[:, u * 128 : (u + 1) * 128] for u in range(4)]

    def rearranged(ref, change):
        def one(t, carry):
            rows = pl.ds(pl.multiple_of((t % 2) * 8, 8), 8)
            for field in range(2):
                parts = change([ref[t // 2, field, u, rows] for u in range(4)])
                for u, part in enumerate(parts):
                    ref[t // 2, field, u, rows] = part
            return carry

        lax.fori_loop(0, 16, one, 0, unroll=4)

    for first in (0, 8):
        for u, part in enumerate(columns_spread(quarters(fstrip[0, first : first + 8]))):
            fmix[0, u, first : first + 8] = part

    f3 = (lambda k: fmix, fq, f3_send, f3_more, f3_recv)
    spread_start(*f3)

    def p3_arrived(d, carry):
        p3_copy(d).wait_recv()
        return carry

    lax.fori_loop(1, NZ, p3_arrived, 0)

    twiddle = [(scalar(T_TWIDDLE + 2 * k), scalar(T_TWIDDLE + 2 * k + 1)) for k in range(NZ)]

    @pl.when(z != 0)
    def _():
        def ring_forward(rows, u):
            columns = tile_columns(u)
            values = []
            for k in range(NZ):
                real, imag = a2[k, 0, rows, columns], a2[k, 1, rows, columns]
                cosine, sine = twiddle[k]
                if k:
                    real, imag = cosine * real + sine * imag, cosine * imag - sine * real
                values.append((real, imag))
            for k, value in enumerate(complex_transform(values, -1.0)):
                sb[k, 0, u, rows] = value[0]
                sb[k, 1, u, rows] = value[1]

        tiles(ring_forward)

    @pl.when(z == 0)
    def _():
        def ring_forward(rows, u):
            columns = tile_columns(u)
            even = real_forward([a2[k, 0, rows, columns] for k in range(NZ)])
            sb[0, 0, u, rows] = even[0][0]
            sb[0, 1, u, rows] = even[4][0]
            odd = []
            for k in range(4):
                value = (a2[k, 1, rows, columns], -a2[k + 4, 1, rows, columns])
                odd.append(turned(value, -k / 16))
            odd = complex_transform(odd, -1.0)
            for k, value in list(zip((1, 2, 3), even[1:4])) + list(zip((4, 5, 6, 7), odd)):
                sb[k, 0, u, rows] = value[0]
                sb[k, 1, u, rows] = value[1]

        tiles(ring_forward)

    rearranged(sb, columns_spread)
    p4 = (lambda k: sb.at[k], ta, p4_send, p4_more, p4_recv)
    spread_start(*p4)

    spread_arrived(*f3)
    top = core * ROWS + half * BLOCK - HALO
    scale = TAU / HALF

    def spaced(ref, field, t):
        rows = pl.ds(t, 8, stride=GROUPS)
        return [ref[field, u, rows] for u in range(4)]

    def weights(t, here, below):
        row = GROUPS * sublane + t
        closed = (row == SPAN - 1) | (row + top == 2 * ROWS - 1) | (row + top == -1)
        rim = (row + top == 0) | (row + top == 2 * ROWS - 1)
        before = pltpu.roll(here[3], 1, 1)
        beyond = [here[1], here[2], here[3], pltpu.roll(here[0], 127, 1)]
        west[t] = jnp.where(lane == 0, 0.0, scale * (here[0] + before))
        for u in range(4):
            columns = slice(u * 128, (u + 1) * 128)
            wts[0, t, :, columns] = jnp.where(closed, 0.0, scale * (here[u] + below[u]))
            east = scale * (here[u] + beyond[u])
            center = jnp.where(rim, scale * here[u], 0.0) - 2.0
            if u == 0:
                center = center + jnp.where(lane == 0, scale * here[u], 0.0)
            if u == 3:
                center = center + jnp.where(lane == 127, scale * here[u], 0.0)
                east = jnp.where(lane == 127, 0.0, east)
            wts[1, t, :, columns] = east
            wts[2, t, :, columns] = center

    def weight_rows(t, carry):
        weights(t, spaced(fq, 0, t), spaced(fq, 0, t + 1))
        return carry

    lax.fori_loop(0, GROUPS - 1, weight_rows, 0)
    weights(
        GROUPS - 1,
        spaced(fq, 0, GROUPS - 1),
        [pltpu.roll(part, 7, 0) for part in spaced(fq, 0, 0)],
    )
    tj[...] = jnp.zeros(tj.shape, jnp.float32)
    spread_arrived(*p4)

    first = [scalar(T_DELTA + k) for k in range(3)]

    def begin(t, carry):
        real, imag = spaced(ta, 0, t), spaced(ta, 1, t)
        for u in range(4):
            columns = slice(u * 128, (u + 1) * 128)
            ti[0, t, :, columns] = real[u]
            ti[1, t, :, columns] = imag[u]
            xi[0, t, :, columns] = first[0] * real[u] - first[1] * imag[u]
            xi[1, t, :, columns] = first[1] * real[u] + first[2] * imag[u]
        return carry

    lax.fori_loop(0, GROUPS, begin, 0, unroll=2)

    def swept_row(now, old, t, here, below, flux_above, factors):
        south, east, center = (quarters(wts[k, t]) for k in range(3))
        west_weight = west[t]
        fresh, flux_below = [], []
        for field in range(2):
            v = here[field]
            before, beyond = pltpu.roll(v[3], 1, 1), pltpu.roll(v[0], 127, 1)
            eastward = [east[u] * ((v[u + 1] if u < 3 else beyond) - v[u]) for u in range(4)]
            westward = [west_weight * (v[0] - before)] + eastward[:3]
            downward = [south[u] * (below[field][u] - v[u]) for u in range(4)]
            result = []
            for u in range(4):
                columns = slice(u * 128, (u + 1) * 128)
                value = (center[u] * v[u] - old[field, t, :, columns]) + (
                    (flux_above[field][u] - downward[u]) + (westward[u] - eastward[u])
                )
                old[field, t, :, columns] = value
                result.append(value)
            fresh.append(result)
            flux_below.append(downward)
        if factors is not None:
            for u in range(4):
                columns = slice(u * 128, (u + 1) * 128)
                real, imag = here[0][u], here[1][u]
                xi[0, t, :, columns] = xi[0, t, :, columns] + (
                    (factors[0] * real - factors[1] * imag)
                    + (factors[3] * fresh[0][u] - factors[4] * fresh[1][u])
                )
                xi[1, t, :, columns] = xi[1, t, :, columns] + (
                    (factors[1] * real + factors[2] * imag)
                    + (factors[4] * fresh[0][u] + factors[5] * fresh[1][u])
                )
        return flux_below

    def sweep(now, old, factors):
        begin_rows = [quarters(now[field, 0]) for field in range(2)]
        wrapped = [[pltpu.roll(part, 7, 0) for part in begin_rows[field]] for field in range(2)]
        end_rows = [quarters(now[field, GROUPS - 1]) for field in range(2)]
        end_south = quarters(wts[0, GROUPS - 1])
        flux_above = [
            [
                pltpu.roll(end_south[u] * (wrapped[field][u] - end_rows[field][u]), 1, 0)
                for u in range(4)
            ]
            for field in range(2)
        ]

        def one(t, carried):
            here, above = carried
            below = [quarters(now[field, t + 1]) for field in range(2)]
            return below, swept_row(now, old, t, here, below, above, factors)

        here, above = lax.fori_loop(
            0, GROUPS - 1, one, (begin_rows, flux_above), unroll=GROUPS - 1
        )
        swept_row(now, old, GROUPS - 1, here, wrapped, above, factors)

    def two_sweeps(m, carry):
        k = 2 * m + 1
        factors = [scalar(T_DELTA + 3 * k + each) for each in range(6)]
        sweep(ti, tj, None)
        sweep(tj, ti, factors)
        return carry

    lax.fori_loop(0, SWEEPS // 2, two_sweeps, 0)

    def finish(t, carry):
        for field in range(2):
            for u in range(4):
                columns = slice(u * 128, (u + 1) * 128)
                xb[field, u, pl.ds(t, 8, stride=GROUPS)] = xi[field, t, :, columns]
        return carry

    lax.fori_loop(0, GROUPS, finish, 0, unroll=2)

    def p6_copy(d):
        rows = pl.ds(pl.multiple_of(HALO + ((slot + d) % 8) * STRIP, 8), STRIP)
        return copy(
            xb.at[:, :, rows], a3.at[slot], p6_send.at[d], p6_recv.at[d], in_half(d), core
        )

    def p6_start(d, carry):
        p6_copy(d).start()
        return carry

    def p6_arrived(d, carry):
        p6_copy(d).wait_recv()
        return carry

    lax.fori_loop(1, 8, p6_start, 0)
    a3[slot] = xb[:, :, pl.ds(pl.multiple_of(HALO + slot * STRIP, 8), STRIP)]
    lax.fori_loop(1, 8, p6_arrived, 0)

    @pl.when(z != 0)
    def _():
        def ring_backward(rows, u):
            values = [(a3[k, 0, u, rows], a3[k, 1, u, rows]) for k in range(8)]
            for k, (real, imag) in enumerate(complex_transform(values, 1.0)):
                cosine, sine = twiddle[k]
                if k:
                    real, imag = cosine * real - sine * imag, cosine * imag + sine * real
                ub[k, 0, u, rows] = real
                ub[k, 1, u, rows] = imag

        tiles(ring_backward)

    @pl.when(z == 0)
    def _():
        def ring_backward(rows, u):
            values = [(a3[k, 0, u, rows], a3[k, 1, u, rows]) for k in range(8)]
            even = [(values[0][0], None)] + values[1:4] + [(values[0][1], None)]
            for k, value in enumerate(real_backward(even)):
                ub[k, 0, u, rows] = value
            for k, value in enumerate(complex_transform(values[4:8], 1.0)):
                real, imag = turned(value, k / 16)
                ub[k, 1, u, rows] = 2.0 * real
                ub[k + 4, 1, u, rows] = -2.0 * imag

        tiles(ring_backward)

    rearranged(ub, columns_joined)

    def p7_copy(d):
        return ring_copy(ub, a4, p7_send, p7_recv, d)

    def p7_start(d, carry):
        p7_copy(d).start()
        return carry

    def p7_arrived(d, carry):
        p7_copy(d).wait_recv()
        return carry

    lax.fori_loop(1, NZ, p7_start, 0)
    a4[z] = ub[z]
    lax.fori_loop(1, NZ, p7_arrived, 0)

    def plane_backward(rows, u):
        columns = tile_columns(u)
        values = [(a4[k, 0, u, rows], a4[k, 1, u, rows]) for k in range(8)]
        values = [(values[0][0], None)] + values[1:] + [(values[0][1], None)]
        for k, value in enumerate(real_backward(values)):
            cb[k, rows, columns] = value

    tiles(plane_backward)

    own_rows = pl.ds(pl.multiple_of(q * STRIP, STRIP), STRIP)

    def p8_copy(d):
        return copy(
            cb.at[(q + d) % NQ], corr.at[own_rows], p8_send.at[d], p8_recv.at[d], plane(d), core
        )

    def p8_start(d, carry):
        p8_copy(d).start()
        return carry

    def p8_arrived(d, carry):
        p8_copy(d).wait_recv()
        return carry

    lax.fori_loop(1, NQ, p8_start, 0)
    corr[own_rows] = cb[q]

    for each in edge_copies(edge_row):
        each.wait_send()
    for part in range(SHIFT_PARTS):
        shift_copy(w, part).wait_send()

    @pl.when(n == STEPS - 1)
    def _():
        def sent(d, carry):
            f1_copy(d).wait_send()
            return carry

        lax.fori_loop(1, NQ, sent, 0)

    @pl.when(z == NZ - 1)
    def _():
        def sent(d, carry):
            f2_copy(d).wait_send()
            return carry

        lax.fori_loop(1, NZ, sent, 0)

    def plane_sent(d, carry):
        p2_copy((q + d) % NQ, d).wait_send()
        return carry

    lax.fori_loop(1, NQ, plane_sent, 0)

    def ring_sent(d, carry):
        p3_copy(d).wait_send()
        p6_copy(d).wait_send()
        p7_copy(d).wait_send()
        return carry

    lax.fori_loop(1, NZ, ring_sent, 0)
    spread_sent(*f3)
    spread_sent(*p4)

    lax.fori_loop(1, NQ, p8_arrived, 0)
    out[...] = wp[PAD : PAD + ROWS] + scalar(T_OUT) * corr[...]

    def last_sent(d, carry):
        p8_copy(d).wait_send()
        return carry

    lax.fori_loop(1, NQ, last_sent, 0)


def body(window_state, prior_window, conductivity):
    f32 = jnp.float32
    dma = pltpu.SemaphoreType.DMA
    vmem = pl.BlockSpec(memory_space=pltpu.VMEM)
    padded_rows = ROWS + 2 * PAD
    shapes = [
        (ROWS, COLS),
        (padded_rows, COLS),
        (padded_rows, COLS),
        (2, 8, COLS),
        (ROWS, COLS),
        (ROWS, COLS),
        (NQ, STRIP, COLS),
        (8, 2, STRIP, COLS),
        (8, 2, STRIP, COLS),
        (8, 2, 4, STRIP, 128),
        (1, ROWS, COLS),
        (1, STRIP, COLS),
        (1, 4, STRIP, 128),
        (1, 4, SPAN, 128),
        (2, 4, SPAN, 128),
        (2, GROUPS, 8, COLS),
        (2, GROUPS, 8, COLS),
        (2, GROUPS, 8, COLS),
        (2, 4, SPAN, 128),
        (3, GROUPS, 8, COLS),
        (GROUPS, 8, 128),
        (8, 2, 4, STRIP, 128),
        (8, 2, 4, STRIP, 128),
        (8, 2, 4, STRIP, 128),
        (NQ, STRIP, COLS),
        (ROWS, COLS),
    ]
    sems = [3, 2, 2, SHIFT_PARTS, SHIFT_PARTS, 16, 1, 8, 1, 8, 8, 12, 16, 16, 8, 8, 8, 8, 12]
    sems += [8, 8, 8, 8, 16, 16]
    updated = pl.pallas_call(
        kernel,
        out_shape=jax.ShapeDtypeStruct((ROWS, COLS), f32),
        in_specs=[pl.BlockSpec(memory_space=pltpu.SMEM)] + 3 * [pl.BlockSpec(memory_space=pl.ANY)],
        out_specs=vmem,
        scratch_shapes=[pltpu.VMEM(shape, f32) for shape in shapes]
        + [dma((count,)) for count in sems],
        compiler_params=pltpu.CompilerParams(
            collective_id=0, has_side_effects=True, vmem_limit_bytes=40 * 1024 * 1024
        ),
    )(jnp.asarray(scalar_table()), window_state[0], prior_window[0], conductivity)
    return updated[None]


def solution(mesh):
    in_specs = (P("tm", "space", None), P("tm", "space", None), P("space", None))
    out_specs = P("tm", "space", None)
    return jax.shard_map(body, mesh=mesh, in_specs=in_specs, out_specs=out_specs, check_vma=False)
```

```python
import math

import jax
import jax.numpy as jnp
import numpy as np
from jax import lax
from jax.experimental import pallas as pl
from jax.experimental.pallas import tpu as pltpu
from jax.sharding import PartitionSpec as P

SWEEPS = 24
STEPS = 128
TAU = 2.0
ALPHA = 0.01
HALF = 12.0 * TAU

NQ, NZ = 16, 8
ROWS, COLS = 256, 512
STRIP = 16
BLOCK = 128
HALO = 24
SPAN = BLOCK + 2 * HALO
PAD = 8
GROUP = 8
GROUPS = SPAN // 8
MESH = pl.DeviceIdType.MESH

T_DELTA, T_IN, T_NEXT, T_OUT, T_TWIDDLE, T_WIDTH = 0, 75, 76, 77, 80, 128


def shift_of(frequency):
    beta = math.exp(math.log(ALPHA) / STEPS)
    angle = 2.0 * math.pi * frequency / STEPS
    return 1.0 - beta * math.cos(angle) + 1j * beta * math.sin(angle)


def polynomial_of(frequency):
    points = 64
    theta = (np.arange(points) + 0.5) * np.pi / points
    image_factor = shift_of(frequency) + HALF * (np.cos(theta) + 1.0)
    center = shift_of(frequency) + HALF
    relative = center / HALF
    solution = np.zeros(points, complex)
    remain = np.ones(points, complex)
    search = remain / center
    factor = 1.0 / relative
    for _ in range(SWEEPS):
        solution = solution + search
        remain = remain - image_factor * search
        renewed = 1.0 / (2.0 * relative - factor)
        search = renewed * factor * search + (2.0 * renewed / HALF) * remain
        factor = renewed
    values = solution + search
    first = [2.0 / points * np.sum(values * np.cos(k * theta)) for k in range(SWEEPS + 3)]
    first[0] = first[0] / 2
    second = [(first[k] - first[k + 2]) / 2 for k in range(SWEEPS + 1)]
    second[0] = first[0] - first[2] / 2
    return np.array(second)


def frequency_of(pair, slot):
    if pair:
        return pair + 16 * slot
    return 16 * slot if slot < 4 else 8 + 32 * (slot - 4)


def scalar_table():
    table = np.zeros((STEPS, T_WIDTH))
    for step in range(STEPS):
        plane, ring = step // NZ, step % NZ
        slot = plane % 8
        delta = polynomial_of(frequency_of(ring, slot))
        real, imag, last = delta.real, delta.imag, delta.real
        if ring == 0 and slot == 0:
            imag, last = 0.0 * imag, polynomial_of(64).real
        table[step, 0:75:3], table[step, 1:75:3], table[step, 2:75:3] = real, imag, last
        table[step, T_IN] = math.exp(math.log(ALPHA) * step / STEPS)
        following = (step + 1) % STEPS
        table[step, T_NEXT] = math.exp(math.log(ALPHA) * following / STEPS)
        table[step, T_OUT] = math.exp(-math.log(ALPHA) * step / STEPS) / STEPS
        for k in range(NZ + 1):
            angle = 2.0 * math.pi * ring * k / STEPS
            table[step, T_TWIDDLE + 2 * k] = math.cos(angle)
            table[step, T_TWIDDLE + 2 * k + 1] = math.sin(angle)
    return table.astype(np.float32).reshape(STEPS, 1, T_WIDTH)


def turned(value, turn):
    real, imag = value
    turn = turn % 1.0
    if turn == 0.0:
        return value
    if turn == 0.25:
        return ((-imag if imag is not None else None), real)
    if turn == 0.5:
        return (-real, -imag if imag is not None else None)
    if turn == 0.75:
        return (imag, -real)
    cosine, sine = math.cos(2 * math.pi * turn), math.sin(2 * math.pi * turn)
    if imag is None:
        return (cosine * real, sine * real)
    if turn % 0.25 == 0.125:
        scale = math.sqrt(0.5)
        if turn == 0.125:
            return (scale * (real - imag), scale * (real + imag))
        if turn == 0.375:
            return (-scale * (real + imag), scale * (real - imag))
        if turn == 0.625:
            return (scale * (imag - real), -scale * (real + imag))
        return (scale * (real + imag), scale * (imag - real))
    return (cosine * real - sine * imag, sine * real + cosine * imag)


def part_sum(left, right):
    if left is None:
        return right
    return left if right is None else left + right


def part_difference(left, right):
    if right is None:
        return left
    return -right if left is None else left - right


def plus(left, right):
    return (part_sum(left[0], right[0]), part_sum(left[1], right[1]))


def minus(left, right):
    return (part_difference(left[0], right[0]), part_difference(left[1], right[1]))


def conjugate(value):
    return (value[0], None if value[1] is None else -value[1])


def real_forward(values):
    count = len(values)
    if count == 2:
        return [(values[0] + values[1], None), (values[0] - values[1], None)]
    even, odd = real_forward(values[0::2]), real_forward(values[1::2])
    result = [None] * (count // 2 + 1)
    for k in range(count // 4 + 1):
        term = turned(odd[k], -k / count)
        result[k] = plus(even[k], term)
        if k < count // 4:
            result[count // 2 - k] = conjugate(minus(even[k], term))
    return result


def real_backward(values):
    count = 2 * (len(values) - 1)
    if count == 2:
        return [values[0][0] + values[1][0], values[0][0] - values[1][0]]
    even, odd = [], []
    for k in range(count // 4):
        mirror = conjugate(values[count // 2 - k])
        even.append(plus(values[k], mirror))
        odd.append(turned(minus(values[k], mirror), k / count))
    middle = values[count // 4]
    even.append((2.0 * middle[0], None))
    odd.append((-2.0 * middle[1], None))
    result = [None] * count
    result[0::2], result[1::2] = real_backward(even), real_backward(odd)
    return result


def complex_transform(values, sign):
    count = len(values)
    if count == 1:
        return values
    even = complex_transform(values[0::2], sign)
    odd = complex_transform(values[1::2], sign)
    odd = [turned(odd[k], sign * k / count) for k in range(count // 2)]
    return [plus(a, b) for a, b in zip(even, odd)] + [minus(a, b) for a, b in zip(even, odd)]


def conductance(conductivity, values):
    return conductivity * (1.0 + 0.5 * jnp.tanh(values))


def kernel(
    table_in, w, w_strips, prior, cond_in, out,
    table, cond, wp, qp, edge, flux, prev, res, a1, yb, a2, sb, pb, fsrc, fstrip, fmix, fq,
    ta, ti, tj, xi, xb, wts, west, a3, ub, a4, cb, corr, load_sem,
    edge_send, edge_recv, shift_send, shift_recv,
    f1_send, f1_recv, f2_send, f2_recv, f3_send, f3_more, f3_recv,
    p2_send, p2_recv, p3_send, p3_recv, p4_send, p4_more, p4_recv,
    p6_send, p6_recv, p7_send, p7_recv, p8_send, p8_recv,
):
    n = lax.axis_index("tm")
    core = lax.axis_index("space")
    q, z = n // NZ, n % NZ
    half, slot = q // 8, q % 8
    other = 1 - core
    crossing = jnp.logical_or(q < 2, q >= NQ - 2)
    owner = n == STEPS - 1

    def scalar(index):
        return table[0, index]

    def plane(distance):
        return ((q + distance) % NQ) * NZ + z

    def ring(distance):
        return q * NZ + (z + distance) % NZ

    def in_half(distance):
        return (8 * half + (slot + distance) % 8) * NZ + z

    def copy(src, dst, send, recv, step, space):
        return pltpu.make_async_remote_copy(
            src_ref=src, dst_ref=dst, send_sem=send, recv_sem=recv,
            device_id=(step, space), device_id_type=MESH,
        )

    def each(low, high, act):
        def one(d, carry):
            act(d)
            return carry

        lax.fori_loop(low, high, one, 0)

    loads = [
        pltpu.make_async_copy(w, wp.at[pl.ds(PAD, ROWS)], load_sem.at[0]),
        pltpu.make_async_copy(cond_in, cond, load_sem.at[1]),
        pltpu.make_async_copy(table_in.at[n], table, load_sem.at[2]),
    ]
    for load in loads:
        load.start()
    prior_load = pltpu.make_async_copy(prior, pb, load_sem.at[3])

    @pl.when(owner)
    def _():
        prior_load.start()

    barrier = pltpu.get_barrier_semaphore()

    def greet(step, space):
        pl.semaphore_signal(barrier, inc=1, device_id=(step, space), device_id_type=MESH)

    greet(n, other)
    before, after = (n + STEPS - 1) % STEPS, (n + 1) % STEPS
    greet(before, core)
    greet(after, core)
    each(1, NQ, lambda d: greet(plane(d), core))
    each(1, NZ, lambda d: greet(ring(d), core))
    beyond = 14 * (1 - half)
    greet(beyond * NZ + z, other)
    greet((beyond + 1) * NZ + z, other)

    zero_rows = jnp.zeros((8, COLS), jnp.float32)
    for load in loads:
        load.wait()
    qp[PAD : PAD + ROWS] = conductance(cond[...], wp[PAD : PAD + ROWS])
    for ref in (wp, qp):
        ref[0:PAD] = zero_rows
        ref[PAD + ROWS : PAD + ROWS + 8] = zero_rows

    pl.semaphore_wait(barrier, NQ - 1 + NZ - 1 + 3 + jnp.where(crossing, 8, 0))

    edge_row = pl.multiple_of((1 - core) * (ROWS - 8), 8)
    edges_out = [
        copy(src.at[pl.ds(edge_row, 8)], edge.at[k], edge_send.at[k], edge_recv.at[k], n, other)
        for k, src in enumerate((w, cond_in))
    ]
    for item in edges_out:
        item.start()

    def group_rows(r):
        return pl.ds(r * GROUP, GROUP)

    def shift_on(src, r):
        return copy(
            src.at[pl.ds(0, 8), group_rows(r)], prev.at[pl.ds(0, 8), group_rows(r)],
            shift_send.at[0, r], shift_recv.at[0, r], after, core,
        )

    def shift_back(r):
        return copy(
            flux.at[pl.ds(8, 8), group_rows(r)], prev.at[pl.ds(8, 8), group_rows(r)],
            shift_send.at[1, r], shift_recv.at[1, r], before, core,
        )

    @pl.when(jnp.logical_not(owner))
    def _():
        for r in range(2):
            shift_on(w_strips, r).start()

    @pl.when(owner)
    def _():
        prior_load.wait()
        for r in range(2):
            shift_on(pb, r).start()

    column = lax.broadcasted_iota(jnp.int32, (8, COLS), 1)
    first_column, last_column = column == 0, column == COLS - 1

    def inside_four(window):
        center = window[8:16]
        return (
            window[7:15],
            window[9:17],
            jnp.where(first_column, 0.0, pltpu.roll(center, 1, 1)),
            jnp.where(last_column, 0.0, pltpu.roll(center, COLS - 1, 1)),
        )

    def fluxes(first_strip, r):
        def one(k, carry):
            rows = pl.ds(pl.multiple_of(k * STRIP + r * GROUP, 8), 24)
            state, coeff = wp[rows], qp[rows]
            here, coeff_here = state[8:16], coeff[8:16]
            total = -here
            for near, near_coeff in zip(inside_four(state), inside_four(coeff)):
                total = total + (0.5 * TAU) * (coeff_here + near_coeff) * (near - here)
            flux[k, group_rows(r)] = total
            return carry

        lax.fori_loop(first_strip, first_strip + 8, one, 0, unroll=2)

    fluxes(8, 0)
    shift_back(0).start()
    for item in edges_out:
        item.wait_recv()
    beside = pl.multiple_of((1 - core) * (PAD + ROWS), 8)
    wp[pl.ds(beside, 8)] = edge[0]
    qp[pl.ds(beside, 8)] = conductance(edge[1], edge[0])
    fluxes(8, 1)
    shift_back(1).start()

    def f1_copy(d):
        target = (q + d) % NQ
        return copy(
            fsrc.at[target], fstrip, f1_send.at[d], f1_recv.at[0], target * NZ + z, core
        )

    def f2_copy(d):
        return copy(fstrip, fstrip, f2_send.at[d], f2_recv.at[0], ring(d), core)

    @pl.when(owner)
    def _():
        def one(k, carry):
            rows = pl.ds(pl.multiple_of(k * STRIP, STRIP), STRIP)
            fsrc[k] = conductance(cond[rows], pb[k])
            return carry

        lax.fori_loop(0, NQ, one, 0, unroll=2)
        each(1, NQ, lambda d: f1_copy(d).start())
        fstrip[...] = fsrc[NQ - 1]

    fluxes(0, 0)
    fluxes(0, 1)

    def p2_copy(r, d):
        target = (q + d) % NQ
        return copy(
            res.at[target, group_rows(r)], a1.at[q, group_rows(r)],
            p2_send.at[r, d], p2_recv.at[r, d], target * NZ + z, core,
        )

    damping, damping_next = scalar(T_IN), scalar(T_NEXT)

    def residuals(r):
        rows = group_rows(r)

        def on(k, carry):
            res[k, rows] = (prev[k, rows] + flux[k, rows]) * damping
            return carry

        def back(k, carry):
            own = wp[pl.ds(pl.multiple_of(PAD + k * STRIP + r * GROUP, 8), GROUP)]
            res[k, rows] = (own + prev[k, rows]) * damping_next
            return carry

        def back_first(k, carry):
            res[k, rows] = (pb[k, rows] + prev[k, rows]) * damping_next
            return carry

        shift_back(r).wait_recv()

        @pl.when(jnp.logical_not(owner))
        def _():
            lax.fori_loop(8, 16, back, 0, unroll=4)

        @pl.when(owner)
        def _():
            lax.fori_loop(8, 16, back_first, 0, unroll=4)

        shift_on(w_strips, r).wait_recv()
        lax.fori_loop(0, 8, on, 0, unroll=4)
        each(1, NQ, lambda d: p2_copy(r, d).start())
        a1[q, rows] = res[q, rows]

    residuals(0)
    residuals(1)

    @pl.when(z == NZ - 1)
    def _():
        @pl.when(q != NQ - 1)
        def _():
            f1_copy(1).wait_recv()

        each(1, NZ, lambda d: f2_copy(d).start())

    def tiles(body):
        def one(u, carry):
            body(u, pl.ds(pl.multiple_of(u * 128, 128), 128))
            return carry

        lax.fori_loop(0, 4, one, 0, unroll=2)

    def plane_forward(r):
        rows = group_rows(r)

        def body(u, columns):
            result = real_forward([a1[k, rows, columns] for k in range(NQ)])
            yb[0, 0, rows, columns] = result[0][0]
            yb[0, 1, rows, columns] = result[8][0]
            for k in range(1, 8):
                yb[k, 0, rows, columns] = result[k][0]
                yb[k, 1, rows, columns] = result[k][1]

        tiles(body)

    def p3_copy(r, d):
        rows = group_rows(r)
        return copy(
            yb.at[(z + d) % NZ, :, rows], a2.at[z, :, rows],
            p3_send.at[r, d], p3_recv.at[r, d], ring(d), core,
        )

    for r in range(2):
        each(1, NQ, lambda d: p2_copy(r, d).wait_recv())
        plane_forward(r)
        each(1, NZ, lambda d: p3_copy(r, d).start())
        a2[z, :, group_rows(r)] = yb[z, :, group_rows(r)]

    lane = lax.broadcasted_iota(jnp.int32, (8, 128), 1)
    sublane = lax.broadcasted_iota(jnp.int32, (8, 128), 0)

    def one_of(parts, choice):
        low = jnp.where(choice == 0, parts[0], parts[1])
        return jnp.where(choice < 2, low, jnp.where(choice == 2, parts[2], parts[3]))

    def moved(part, index):
        return jnp.take_along_axis(part, index, axis=1)

    within, block = lane % 4, lane // 32

    def columns_spread(parts):
        mixed = [one_of(parts, (within + s) % 4) for s in range(4)]
        mixed = [moved(mixed[s], 4 * (lane % 32) + (block - s) % 4) for s in range(4)]
        return [one_of(mixed, (block - u) % 4) for u in range(4)]

    def columns_joined(parts):
        mixed = [one_of(parts, (block - s) % 4) for s in range(4)]
        mixed = [moved(mixed[s], 32 * ((within + s) % 4) + lane // 4) for s in range(4)]
        return [one_of(mixed, (u - within) % 4) for u in range(4)]

    def quarters(value):
        return [value[:, u * 128 : (u + 1) * 128] for u in range(4)]

    def rearranged(ref, r, change):
        rows = group_rows(r)

        def one(t, carry):
            for field in range(2):
                parts = change([ref[t, field, u, rows] for u in range(4)])
                for u, part in enumerate(parts):
                    ref[t, field, u, rows] = part
            return carry

        lax.fori_loop(0, 8, one, 0, unroll=4)

    def main_copy(r, src, dst, send, recv, d):
        rows = pl.ds(pl.multiple_of(HALO + slot * STRIP + r * GROUP, 8), GROUP)
        return copy(
            src((slot + d) % 8).at[:, :, group_rows(r)], dst.at[:, :, rows],
            send.at[r, d], recv.at[r, d], in_half(d), core,
        )

    edges = (((0, 152), (1, 168), (7, 8)), ((0, 160), (6, 0), (7, 16)))

    def more_copy(r, src, dst, send, recv, kind, target_slot):
        index, offset = edges[r][kind]
        same = (half == 0) if index >= 6 else (half == 1)
        return copy(
            src(target_slot).at[:, :, group_rows(r)],
            dst.at[:, :, pl.ds(offset, GROUP)],
            send.at[r, target_slot],
            recv.at[r, 8 + kind],
            (8 * (1 - half) + target_slot) * NZ + z,
            jnp.where(same, core, other),
        )

    def spread_start(r, src, dst, send, more, recv):
        each(1, 8, lambda d: main_copy(r, src, dst, send, recv, d).start())
        for kind in range(3):

            @pl.when(slot == edges[r][kind][0])
            def _():
                each(0, 8, lambda k: more_copy(r, src, dst, more, recv, kind, k).start())

        own = pl.ds(pl.multiple_of(HALO + slot * STRIP + r * GROUP, 8), GROUP)
        dst[:, :, own] = src(slot)[:, :, group_rows(r)]

    def spread_arrived(r, src, dst, send, more, recv):
        each(1, 8, lambda d: main_copy(r, src, dst, send, recv, d).wait_recv())
        for kind in range(3):
            more_copy(r, src, dst, more, recv, kind, 0).wait_recv()

    def spread_sent(r, src, dst, send, more, recv):
        each(1, 8, lambda d: main_copy(r, src, dst, send, recv, d).wait_send())
        for kind in range(3):

            @pl.when(slot == edges[r][kind][0])
            def _():
                each(0, 8, lambda k: more_copy(r, src, dst, more, recv, kind, k).wait_send())

    @pl.when(z != NZ - 1)
    def _():
        f2_copy(1).wait_recv()

    for row in (0, 8):
        for u, part in enumerate(columns_spread(quarters(fstrip[row : row + 8]))):
            fmix[0, u, row : row + 8] = part

    f3 = (lambda k: fmix, fq, f3_send, f3_more, f3_recv)
    for r in range(2):
        spread_start(r, *f3)

    for r in range(2):
        spread_arrived(r, *f3)
    top = core * ROWS + half * BLOCK - HALO
    scale = TAU / HALF

    def spaced(ref, field, t):
        rows = pl.ds(t, 8, stride=GROUPS)
        return [ref[field, u, rows] for u in range(4)]

    def weights(t, here, below):
        row = GROUPS * sublane + t
        closed = (row == SPAN - 1) | (row + top == 2 * ROWS - 1) | (row + top == -1)
        rim = (row + top == 0) | (row + top == 2 * ROWS - 1)
        before = pltpu.roll(here[3], 1, 1)
        beyond = [here[1], here[2], here[3], pltpu.roll(here[0], 127, 1)]
        west[t] = jnp.where(lane == 0, 0.0, scale * (here[0] + before))
        for u in range(4):
            columns = slice(u * 128, (u + 1) * 128)
            wts[0, t, :, columns] = jnp.where(closed, 0.0, scale * (here[u] + below[u]))
            east = scale * (here[u] + beyond[u])
            center = jnp.where(rim, scale * here[u], 0.0) - 2.0
            if u == 0:
                center = center + jnp.where(lane == 0, scale * here[u], 0.0)
            if u == 3:
                center = center + jnp.where(lane == 127, scale * here[u], 0.0)
                east = jnp.where(lane == 127, 0.0, east)
            wts[1, t, :, columns] = east
            wts[2, t, :, columns] = center

    def weight_rows(t, carry):
        weights(t, spaced(fq, 0, t), spaced(fq, 0, t + 1))
        return carry

    lax.fori_loop(0, GROUPS - 1, weight_rows, 0, unroll=3)
    weights(
        GROUPS - 1,
        spaced(fq, 0, GROUPS - 1),
        [pltpu.roll(part, 7, 0) for part in spaced(fq, 0, 0)],
    )
    tj[...] = jnp.zeros(tj.shape, jnp.float32)

    twiddle = [(scalar(T_TWIDDLE + 2 * k), scalar(T_TWIDDLE + 2 * k + 1)) for k in range(NZ)]
    start = 2 * NZ * half
    twiddle_first = (scalar(T_TWIDDLE + start), scalar(T_TWIDDLE + start + 1))
    sign = jnp.where(half == 1, -1.0, 1.0)

    def source(k):
        return (k + NZ - half) % NZ

    def ring_forward(r):
        rows = group_rows(r)

        @pl.when(z != 0)
        def _():
            def body(u, columns):
                values = []
                for k in range(NZ):
                    real, imag = a2[source(k), 0, rows, columns], a2[source(k), 1, rows, columns]
                    cosine, sine = twiddle[k] if k else twiddle_first
                    values.append((cosine * real + sine * imag, cosine * imag - sine * real))
                for k, value in enumerate(complex_transform(values, -1.0)):
                    sb[k, 0, u, rows] = value[0]
                    sb[k, 1, u, rows] = value[1]

            tiles(body)

        @pl.when(z == 0)
        def _():
            def body(u, columns):
                even = real_forward([a2[source(k), 0, rows, columns] for k in range(NZ)])
                sb[0, 0, u, rows] = even[0][0]
                sb[0, 1, u, rows] = even[4][0]
                values = [a2[source(k), 1, rows, columns] for k in range(NZ)]
                values[0] = sign * values[0]
                odd = [turned((values[k], -values[k + 4]), -k / 16) for k in range(4)]
                odd = complex_transform(odd, -1.0)
                for k, value in list(zip((1, 2, 3), even[1:4])) + list(zip((4, 5, 6, 7), odd)):
                    sb[k, 0, u, rows] = value[0]
                    sb[k, 1, u, rows] = value[1]

            tiles(body)

    p4 = (lambda k: sb.at[k], ta, p4_send, p4_more, p4_recv)
    for r in range(2):
        each(1, NZ, lambda d: p3_copy(r, d).wait_recv())
        ring_forward(r)
        rearranged(sb, r, columns_spread)
        spread_start(r, *p4)
    for r in range(2):
        spread_arrived(r, *p4)


    first = [scalar(T_DELTA + k) for k in range(3)]

    def begin(t, carry):
        real, imag = spaced(ta, 0, t), spaced(ta, 1, t)
        for u in range(4):
            columns = slice(u * 128, (u + 1) * 128)
            ti[0, t, :, columns] = real[u]
            ti[1, t, :, columns] = imag[u]
            xi[0, t, :, columns] = first[0] * real[u] - first[1] * imag[u]
            xi[1, t, :, columns] = first[1] * real[u] + first[2] * imag[u]
        return carry

    lax.fori_loop(0, GROUPS, begin, 0, unroll=2)

    def swept_row(now, old, t, here, below, flux_above, factors):
        south, east, center = (quarters(wts[k, t]) for k in range(3))
        west_weight = west[t]
        fresh, flux_below = [], []
        for field in range(2):
            v = here[field]
            before, beyond = pltpu.roll(v[3], 1, 1), pltpu.roll(v[0], 127, 1)
            eastward = [east[u] * ((v[u + 1] if u < 3 else beyond) - v[u]) for u in range(4)]
            westward = [west_weight * (v[0] - before)] + eastward[:3]
            downward = [south[u] * (below[field][u] - v[u]) for u in range(4)]
            result = []
            for u in range(4):
                columns = slice(u * 128, (u + 1) * 128)
                value = (center[u] * v[u] - old[field, t, :, columns]) + (
                    (flux_above[field][u] - downward[u]) + (westward[u] - eastward[u])
                )
                old[field, t, :, columns] = value
                result.append(value)
            fresh.append(result)
            flux_below.append(downward)
        if factors is not None:
            for u in range(4):
                columns = slice(u * 128, (u + 1) * 128)
                real, imag = here[0][u], here[1][u]
                xi[0, t, :, columns] = xi[0, t, :, columns] + (
                    (factors[0] * real - factors[1] * imag)
                    + (factors[3] * fresh[0][u] - factors[4] * fresh[1][u])
                )
                xi[1, t, :, columns] = xi[1, t, :, columns] + (
                    (factors[1] * real + factors[2] * imag)
                    + (factors[4] * fresh[0][u] + factors[5] * fresh[1][u])
                )
        return flux_below

    def sweep(now, old, factors):
        begin_rows = [quarters(now[field, 0]) for field in range(2)]
        wrapped = [[pltpu.roll(part, 7, 0) for part in begin_rows[field]] for field in range(2)]
        end_rows = [quarters(now[field, GROUPS - 1]) for field in range(2)]
        end_south = quarters(wts[0, GROUPS - 1])
        flux_above = [
            [
                pltpu.roll(end_south[u] * (wrapped[field][u] - end_rows[field][u]), 1, 0)
                for u in range(4)
            ]
            for field in range(2)
        ]

        def one(t, carried):
            here, above = carried
            below = [quarters(now[field, t + 1]) for field in range(2)]
            return below, swept_row(now, old, t, here, below, above, factors)

        here, above = lax.fori_loop(
            0, GROUPS - 1, one, (begin_rows, flux_above), unroll=GROUPS - 1
        )
        swept_row(now, old, GROUPS - 1, here, wrapped, above, factors)

    def two_sweeps(m, carry):
        k = 2 * m + 1
        factors = [scalar(T_DELTA + 3 * k + each) for each in range(6)]
        sweep(ti, tj, None)
        sweep(tj, ti, factors)
        return carry

    lax.fori_loop(0, SWEEPS // 2, two_sweeps, 0)

    def finish(t, carry):
        for field in range(2):
            for u in range(4):
                columns = slice(u * 128, (u + 1) * 128)
                xb[field, u, pl.ds(t, 8, stride=GROUPS)] = xi[field, t, :, columns]
        return carry

    lax.fori_loop(0, GROUPS, finish, 0, unroll=2)

    def p6_copy(r, d):
        rows = pl.ds(pl.multiple_of(HALO + ((slot + d) % 8) * STRIP + r * GROUP, 8), GROUP)
        return copy(
            xb.at[:, :, rows], a3.at[slot, :, :, group_rows(r)],
            p6_send.at[r, d], p6_recv.at[r, d], in_half(d), core,
        )

    for r in range(2):
        each(1, 8, lambda d: p6_copy(r, d).start())
        own = pl.ds(pl.multiple_of(HALO + slot * STRIP + r * GROUP, 8), GROUP)
        a3[slot, :, :, group_rows(r)] = xb[:, :, own]

    def ring_backward(r):
        rows = group_rows(r)

        @pl.when(z != 0)
        def _():
            def body(u, columns):
                values = [(a3[k, 0, u, rows], a3[k, 1, u, rows]) for k in range(8)]
                for k, (real, imag) in enumerate(complex_transform(values, 1.0)):
                    cosine, sine = twiddle[k]
                    if k:
                        real, imag = cosine * real - sine * imag, cosine * imag + sine * real
                    ub[k, 0, u, rows] = real
                    ub[k, 1, u, rows] = imag

            tiles(body)

        @pl.when(z == 0)
        def _():
            def body(u, columns):
                values = [(a3[k, 0, u, rows], a3[k, 1, u, rows]) for k in range(8)]
                even = [(values[0][0], None)] + values[1:4] + [(values[0][1], None)]
                for k, value in enumerate(real_backward(even)):
                    ub[k, 0, u, rows] = value
                for k, value in enumerate(complex_transform(values[4:8], 1.0)):
                    real, imag = turned(value, k / 16)
                    ub[k, 1, u, rows] = 2.0 * real
                    ub[k + 4, 1, u, rows] = -2.0 * imag

            tiles(body)

    def p7_copy(r, d):
        rows = group_rows(r)
        return copy(
            ub.at[(z + d) % NZ, :, :, rows], a4.at[z, :, :, rows],
            p7_send.at[r, d], p7_recv.at[r, d], ring(d), core,
        )

    for r in range(2):
        each(1, 8, lambda d: p6_copy(r, d).wait_recv())
        ring_backward(r)
        rearranged(ub, r, columns_joined)
        each(1, NZ, lambda d: p7_copy(r, d).start())
        a4[z, :, :, group_rows(r)] = ub[z, :, :, group_rows(r)]

    def plane_backward(r):
        rows = group_rows(r)

        def body(u, columns):
            values = [(a4[k, 0, u, rows], a4[k, 1, u, rows]) for k in range(8)]
            values = [(values[0][0], None)] + values[1:] + [(values[0][1], None)]
            for k, value in enumerate(real_backward(values)):
                cb[k, rows, columns] = value

        tiles(body)

    def p8_copy(r, d):
        rows = group_rows(r)
        return copy(
            cb.at[(q + d) % NQ, rows], corr.at[q, rows],
            p8_send.at[r, d], p8_recv.at[r, d], plane(d), core,
        )

    for r in range(2):
        each(1, NZ, lambda d: p7_copy(r, d).wait_recv())
        plane_backward(r)
        each(1, NQ, lambda d: p8_copy(r, d).start())
        corr[q, group_rows(r)] = cb[q, group_rows(r)]

    for item in edges_out:
        item.wait_send()
    for r in range(2):
        shift_on(w_strips, r).wait_send()
        shift_back(r).wait_send()

    @pl.when(owner)
    def _():
        each(1, NQ, lambda d: f1_copy(d).wait_send())

    @pl.when(z == NZ - 1)
    def _():
        each(1, NZ, lambda d: f2_copy(d).wait_send())

    for r in range(2):
        each(1, NQ, lambda d: p2_copy(r, d).wait_send())
        for sent in (p3_copy, p6_copy, p7_copy):
            each(1, NZ, lambda d: sent(r, d).wait_send())
        spread_sent(r, *f3)
        spread_sent(r, *p4)

    scale_out = scalar(T_OUT)
    for r in range(2):
        rows = group_rows(r)
        each(1, NQ, lambda d: p8_copy(r, d).wait_recv())

        def write(k, carry):
            own = wp[pl.ds(pl.multiple_of(PAD + k * STRIP + r * GROUP, 8), GROUP)]
            out[k, rows] = own + scale_out * corr[k, rows]
            return carry

        lax.fori_loop(0, NQ, write, 0, unroll=4)
    for r in range(2):
        each(1, NQ, lambda d: p8_copy(r, d).wait_send())


def body(window_state, prior_window, conductivity):
    f32 = jnp.float32
    dma = pltpu.SemaphoreType.DMA
    padded_rows = ROWS + 2 * PAD
    strips = (NQ, STRIP, COLS)
    pairs = (8, 2, STRIP, COLS)
    pairs_apart = (8, 2, 4, STRIP, 128)
    shapes = [
        (ROWS, COLS),
        (padded_rows, COLS),
        (padded_rows, COLS),
        (2, 8, COLS),
        strips,
        strips,
        strips,
        strips,
        pairs,
        pairs,
        pairs_apart,
        strips,
        strips,
        (STRIP, COLS),
        (1, 4, STRIP, 128),
        (1, 4, SPAN, 128),
        (2, 4, SPAN, 128),
        (2, GROUPS, 8, COLS),
        (2, GROUPS, 8, COLS),
        (2, GROUPS, 8, COLS),
        (2, 4, SPAN, 128),
        (3, GROUPS, 8, COLS),
        (GROUPS, 8, 128),
        pairs_apart,
        pairs_apart,
        pairs_apart,
        strips,
        strips,
    ]
    sems = [(4,), (2,), (2,), (2, 2), (2, 2), (16,), (1,), (8,), (1,), (2, 8), (2, 8), (2, 11)]
    sems += [(2, 16), (2, 16), (2, 8), (2, 8), (2, 8), (2, 8), (2, 11)]
    sems += [(2, 8), (2, 8), (2, 8), (2, 8), (2, 16), (2, 16)]
    updated = pl.pallas_call(
        kernel,
        out_shape=jax.ShapeDtypeStruct(strips, f32),
        in_specs=5 * [pl.BlockSpec(memory_space=pl.ANY)],
        out_specs=pl.BlockSpec(memory_space=pltpu.VMEM),
        scratch_shapes=[pltpu.SMEM((1, T_WIDTH), f32)]
        + [pltpu.VMEM(shape, f32) for shape in shapes]
        + [dma(shape) for shape in sems],
        compiler_params=pltpu.CompilerParams(
            collective_id=0, has_side_effects=True, vmem_limit_bytes=60 * 1024 * 1024
        ),
    )(
        jnp.asarray(scalar_table()),
        window_state[0],
        window_state.reshape(strips),
        prior_window.reshape(strips),
        conductivity,
    )
    return updated.reshape(1, ROWS, COLS)


def solution(mesh):
    in_specs = (P("tm", "space", None), P("tm", "space", None), P("space", None))
    out_specs = P("tm", "space", None)
    return jax.shard_map(body, mesh=mesh, in_specs=in_specs, out_specs=out_specs, check_vma=False)
```

```python
import math

import jax
import jax.numpy as jnp
import numpy as np
from jax import lax
from jax.experimental import pallas as pl
from jax.experimental.pallas import tpu as pltpu
from jax.sharding import PartitionSpec as P

SWEEPS = 24
STEPS = 128
TAU = 2.0
ALPHA = 0.01
HALF = 12.0 * TAU

NQ, NZ = 16, 8
ROWS, COLS = 256, 512
STRIP = 16
BLOCK = 128
HALO = 24
SPAN = BLOCK + 2 * HALO
PAD = 8
GROUP = 8
GROUPS = SPAN // 8
MESH = pl.DeviceIdType.MESH

T_DELTA, T_IN, T_NEXT, T_TWIDDLE, T_OUT, T_WIDTH = 0, 75, 76, 80, 100, 128


def shift_of(frequency):
    beta = math.exp(math.log(ALPHA) / STEPS)
    angle = 2.0 * math.pi * frequency / STEPS
    return 1.0 - beta * math.cos(angle) + 1j * beta * math.sin(angle)


def polynomial_of(frequency):
    points = 64
    theta = (np.arange(points) + 0.5) * np.pi / points
    image_factor = shift_of(frequency) + HALF * (np.cos(theta) + 1.0)
    center = shift_of(frequency) + HALF
    relative = center / HALF
    solution = np.zeros(points, complex)
    remain = np.ones(points, complex)
    search = remain / center
    factor = 1.0 / relative
    for _ in range(SWEEPS):
        solution = solution + search
        remain = remain - image_factor * search
        renewed = 1.0 / (2.0 * relative - factor)
        search = renewed * factor * search + (2.0 * renewed / HALF) * remain
        factor = renewed
    values = solution + search
    first = [2.0 / points * np.sum(values * np.cos(k * theta)) for k in range(SWEEPS + 3)]
    first[0] = first[0] / 2
    second = [(first[k] - first[k + 2]) / 2 for k in range(SWEEPS + 1)]
    second[0] = first[0] - first[2] / 2
    return np.array(second)


def frequency_of(pair, slot):
    if pair:
        return pair + 16 * slot
    return 16 * slot if slot < 4 else 8 + 32 * (slot - 4)


def scalar_table():
    table = np.zeros((STEPS, T_WIDTH))
    for step in range(STEPS):
        plane, ring = step // NZ, step % NZ
        slot = plane % 8
        delta = polynomial_of(frequency_of(ring, slot))
        real, imag, last = delta.real, delta.imag, delta.real
        if ring == 0 and slot == 0:
            imag, last = 0.0 * imag, polynomial_of(64).real
        table[step, 0:75:3], table[step, 1:75:3], table[step, 2:75:3] = real, imag, last
        table[step, T_IN] = math.exp(math.log(ALPHA) * step / STEPS)
        following = (step + 1) % STEPS
        table[step, T_NEXT] = math.exp(math.log(ALPHA) * following / STEPS)
        for k in range(NQ):
            arrival = NZ * k + ring
            table[step, T_OUT + k] = math.exp(-math.log(ALPHA) * arrival / STEPS) / STEPS
        for k in range(NZ + 1):
            angle = 2.0 * math.pi * ring * k / STEPS
            table[step, T_TWIDDLE + 2 * k] = math.cos(angle)
            table[step, T_TWIDDLE + 2 * k + 1] = math.sin(angle)
    return table.astype(np.float32).reshape(STEPS, 1, T_WIDTH)


def turned(value, turn):
    real, imag = value
    turn = turn % 1.0
    if turn == 0.0:
        return value
    if turn == 0.25:
        return ((-imag if imag is not None else None), real)
    if turn == 0.5:
        return (-real, -imag if imag is not None else None)
    if turn == 0.75:
        return (imag, -real)
    cosine, sine = math.cos(2 * math.pi * turn), math.sin(2 * math.pi * turn)
    if imag is None:
        return (cosine * real, sine * real)
    if turn % 0.25 == 0.125:
        scale = math.sqrt(0.5)
        if turn == 0.125:
            return (scale * (real - imag), scale * (real + imag))
        if turn == 0.375:
            return (-scale * (real + imag), scale * (real - imag))
        if turn == 0.625:
            return (scale * (imag - real), -scale * (real + imag))
        return (scale * (real + imag), scale * (imag - real))
    return (cosine * real - sine * imag, sine * real + cosine * imag)


def part_sum(left, right):
    if left is None:
        return right
    return left if right is None else left + right


def part_difference(left, right):
    if right is None:
        return left
    return -right if left is None else left - right


def plus(left, right):
    return (part_sum(left[0], right[0]), part_sum(left[1], right[1]))


def minus(left, right):
    return (part_difference(left[0], right[0]), part_difference(left[1], right[1]))


def conjugate(value):
    return (value[0], None if value[1] is None else -value[1])


def real_forward(values):
    count = len(values)
    if count == 2:
        return [(values[0] + values[1], None), (values[0] - values[1], None)]
    even, odd = real_forward(values[0::2]), real_forward(values[1::2])
    result = [None] * (count // 2 + 1)
    for k in range(count // 4 + 1):
        term = turned(odd[k], -k / count)
        result[k] = plus(even[k], term)
        if k < count // 4:
            result[count // 2 - k] = conjugate(minus(even[k], term))
    return result


def real_backward(values):
    count = 2 * (len(values) - 1)
    if count == 2:
        return [values[0][0] + values[1][0], values[0][0] - values[1][0]]
    even, odd = [], []
    for k in range(count // 4):
        mirror = conjugate(values[count // 2 - k])
        even.append(plus(values[k], mirror))
        odd.append(turned(minus(values[k], mirror), k / count))
    middle = values[count // 4]
    even.append((2.0 * middle[0], None))
    odd.append((-2.0 * middle[1], None))
    result = [None] * count
    result[0::2], result[1::2] = real_backward(even), real_backward(odd)
    return result


def complex_transform(values, sign):
    count = len(values)
    if count == 1:
        return values
    even = complex_transform(values[0::2], sign)
    odd = complex_transform(values[1::2], sign)
    odd = [turned(odd[k], sign * k / count) for k in range(count // 2)]
    return [plus(a, b) for a, b in zip(even, odd)] + [minus(a, b) for a, b in zip(even, odd)]


def conductance(conductivity, values):
    return conductivity * (1.0 + 0.5 * jnp.tanh(values))


def kernel(
    table_in, w, w_strips, prior, cond_in, out,
    table, cond, wp, qp, edge, flux, prev, res, a1, yb, a2, sb, pb, fstrip, fmix, fq,
    ta, ti, tj, xi, xb, wts, west, a3, ub, a4, cb, load_sem,
    edge_send, edge_recv, shift_send, shift_recv,
    f1_send, f1_recv, f2_send, f2_recv, f3_send, f3_recv, fh_send, fh_recv,
    p2_send, p2_recv, p3_send, p3_recv, p4_send, p4_recv, p4h_send, p4h_recv,
    p6_send, p6_recv, p7_send, p7_recv, p8_send, p8_recv,
):
    n = lax.axis_index("tm")
    core = lax.axis_index("space")
    q, z = n // NZ, n % NZ
    half, slot = q // 8, q % 8
    other = 1 - core
    apart = half != core
    owner = n == STEPS - 1

    def scalar(index):
        return table[0, index]

    def plane(distance):
        return ((q + distance) % NQ) * NZ + z

    def ring(distance):
        return q * NZ + (z + distance) % NZ

    def partner(k):
        return (8 * core + k) * NZ + z

    def copy(src, dst, send, recv, step, space):
        return pltpu.make_async_remote_copy(
            src_ref=src, dst_ref=dst, send_sem=send, recv_sem=recv,
            device_id=(step, space), device_id_type=MESH,
        )

    def each(low, high, act):
        def one(d, carry):
            act(d)
            return carry

        lax.fori_loop(low, high, one, 0)

    loads = [
        pltpu.make_async_copy(w, wp.at[pl.ds(PAD, ROWS)], load_sem.at[0]),
        pltpu.make_async_copy(cond_in, cond, load_sem.at[1]),
        pltpu.make_async_copy(table_in.at[n], table, load_sem.at[2]),
    ]
    for load in loads:
        load.start()
    prior_load = pltpu.make_async_copy(prior, pb, load_sem.at[3])

    @pl.when(owner)
    def _():
        prior_load.start()

    barrier = pltpu.get_barrier_semaphore()

    def greet(step, space):
        pl.semaphore_signal(barrier, inc=1, device_id=(step, space), device_id_type=MESH)

    greet(n, other)
    before, after = (n + STEPS - 1) % STEPS, (n + 1) % STEPS
    greet(before, core)
    greet(after, core)
    each(1, NQ, lambda d: greet(plane(d), core))
    each(1, NZ, lambda d: greet(ring(d), core))

    @pl.when(apart)
    def _():
        each(0, 8, lambda k: greet(partner(k), half))

    zero_rows = jnp.zeros((8, COLS), jnp.float32)
    for load in loads:
        load.wait()
    qp[PAD : PAD + ROWS] = conductance(cond[...], wp[PAD : PAD + ROWS])
    for ref in (wp, qp):
        ref[0:PAD] = zero_rows
        ref[PAD + ROWS : PAD + ROWS + 8] = zero_rows

    pl.semaphore_wait(barrier, NQ - 1 + NZ - 1 + 3 + jnp.where(apart, 8, 0))

    edge_row = pl.multiple_of((1 - core) * (ROWS - 8), 8)
    edges_out = [
        copy(src.at[pl.ds(edge_row, 8)], edge.at[k], edge_send.at[k], edge_recv.at[k], n, other)
        for k, src in enumerate((w, cond_in))
    ]
    for item in edges_out:
        item.start()

    def group_rows(r):
        return pl.ds(r * GROUP, GROUP)

    def shift_on(src, r):
        return copy(
            src.at[pl.ds(0, 8), group_rows(r)], prev.at[pl.ds(0, 8), group_rows(r)],
            shift_send.at[0, r], shift_recv.at[0, r], after, core,
        )

    def shift_back(r):
        return copy(
            flux.at[pl.ds(8, 8), group_rows(r)], prev.at[pl.ds(8, 8), group_rows(r)],
            shift_send.at[1, r], shift_recv.at[1, r], before, core,
        )

    @pl.when(jnp.logical_not(owner))
    def _():
        for r in range(2):
            shift_on(w_strips, r).start()

    def f1_copy(d):
        target = (q + d) % NQ
        return copy(
            prior.at[target], fstrip, f1_send.at[d], f1_recv.at[0], target * NZ + z, core
        )

    def f2_copy(d):
        return copy(fstrip, fstrip, f2_send.at[d], f2_recv.at[0], ring(d), core)

    @pl.when(owner)
    def _():
        for r in range(2):
            shift_on(prior, r).start()
        each(1, NQ, lambda d: f1_copy(d).start())
        prior_load.wait()
        fstrip[...] = pb[NQ - 1]

    column = lax.broadcasted_iota(jnp.int32, (8, COLS), 1)
    first_column, last_column = column == 0, column == COLS - 1

    def inside_four(window):
        center = window[8:16]
        return (
            window[7:15],
            window[9:17],
            jnp.where(first_column, 0.0, pltpu.roll(center, 1, 1)),
            jnp.where(last_column, 0.0, pltpu.roll(center, COLS - 1, 1)),
        )

    def fluxes(first_strip, r):
        def one(k, carry):
            rows = pl.ds(pl.multiple_of(k * STRIP + r * GROUP, 8), 24)
            state, coeff = wp[rows], qp[rows]
            here, coeff_here = state[8:16], coeff[8:16]
            total = -here
            for near, near_coeff in zip(inside_four(state), inside_four(coeff)):
                total = total + (0.5 * TAU) * (coeff_here + near_coeff) * (near - here)
            flux[k, group_rows(r)] = total
            return carry

        lax.fori_loop(first_strip, first_strip + 8, one, 0, unroll=2)

    fluxes(8, 0)
    shift_back(0).start()
    for item in edges_out:
        item.wait_recv()
    beside = pl.multiple_of((1 - core) * (PAD + ROWS), 8)
    wp[pl.ds(beside, 8)] = edge[0]
    qp[pl.ds(beside, 8)] = conductance(edge[1], edge[0])
    fluxes(8, 1)
    shift_back(1).start()

    fluxes(0, 0)
    fluxes(0, 1)

    @pl.when(z == NZ - 1)
    def _():
        @pl.when(q != NQ - 1)
        def _():
            f1_copy(1).wait_recv()

        each(1, NZ, lambda d: f2_copy(d).start())

    def p2_copy(r, d):
        target = (q + d) % NQ
        return copy(
            res.at[target, group_rows(r)], a1.at[q, group_rows(r)],
            p2_send.at[r, d], p2_recv.at[r, d], target * NZ + z, core,
        )

    damping, damping_next = scalar(T_IN), scalar(T_NEXT)

    def residuals(r):
        rows = group_rows(r)

        def on(k, carry):
            res[k, rows] = (prev[k, rows] + flux[k, rows]) * damping
            return carry

        def back(k, carry):
            own = wp[pl.ds(pl.multiple_of(PAD + k * STRIP + r * GROUP, 8), GROUP)]
            res[k, rows] = (own + prev[k, rows]) * damping_next
            return carry

        def back_first(k, carry):
            res[k, rows] = (pb[k, rows] + prev[k, rows]) * damping_next
            return carry

        shift_back(r).wait_recv()

        @pl.when(jnp.logical_not(owner))
        def _():
            lax.fori_loop(8, 16, back, 0, unroll=4)

        @pl.when(owner)
        def _():
            lax.fori_loop(8, 16, back_first, 0, unroll=4)

        shift_on(w_strips, r).wait_recv()
        lax.fori_loop(0, 8, on, 0, unroll=4)
        each(1, NQ, lambda d: p2_copy(r, d).start())
        a1[q, rows] = res[q, rows]

    residuals(0)
    residuals(1)

    def tiles(body):
        def one(u, carry):
            body(u, pl.ds(pl.multiple_of(u * 128, 128), 128))
            return carry

        lax.fori_loop(0, 4, one, 0, unroll=2)

    def plane_forward(r):
        rows = group_rows(r)

        def body(u, columns):
            result = real_forward([a1[k, rows, columns] for k in range(NQ)])
            yb[0, 0, rows, columns] = result[0][0]
            yb[0, 1, rows, columns] = result[8][0]
            for k in range(1, 8):
                yb[k, 0, rows, columns] = result[k][0]
                yb[k, 1, rows, columns] = result[k][1]

        tiles(body)

    def p3_copy(r, d):
        rows = group_rows(r)
        return copy(
            yb.at[(z + d) % NZ, :, rows], a2.at[z, :, rows],
            p3_send.at[r, d], p3_recv.at[r, d], ring(d), core,
        )


    lane = lax.broadcasted_iota(jnp.int32, (8, 128), 1)
    sublane = lax.broadcasted_iota(jnp.int32, (8, 128), 0)

    def one_of(parts, choice):
        low = jnp.where(choice == 0, parts[0], parts[1])
        return jnp.where(choice < 2, low, jnp.where(choice == 2, parts[2], parts[3]))

    def moved(part, index):
        return jnp.take_along_axis(part, index, axis=1)

    within, block = lane % 4, lane // 32

    def columns_spread(parts):
        mixed = [one_of(parts, (within + s) % 4) for s in range(4)]
        mixed = [moved(mixed[s], 4 * (lane % 32) + (block - s) % 4) for s in range(4)]
        return [one_of(mixed, (block - u) % 4) for u in range(4)]

    def columns_joined(parts):
        mixed = [one_of(parts, (block - s) % 4) for s in range(4)]
        mixed = [moved(mixed[s], 32 * ((within + s) % 4) + lane // 4) for s in range(4)]
        return [one_of(mixed, (u - within) % 4) for u in range(4)]

    def quarters(value):
        return [value[:, u * 128 : (u + 1) * 128] for u in range(4)]

    def rearranged(ref, r, change):
        rows = group_rows(r)

        def one(t, carry):
            for field in range(2):
                parts = change([ref[t, field, u, rows] for u in range(4)])
                for u, part in enumerate(parts):
                    ref[t, field, u, rows] = part
            return carry

        lax.fori_loop(0, 8, one, 0, unroll=4)

    def partners(act):
        each(1, 8, lambda d: act((slot + d) % 8))

        @pl.when(apart)
        def _():
            act(slot)

    def main_copy(r, src, dst, send, recv, k):
        rows = pl.ds(pl.multiple_of(HALO + slot * STRIP + r * GROUP, 8), GROUP)
        return copy(
            src(k).at[:, :, group_rows(r)], dst.at[:, :, rows],
            send.at[r, k], recv.at[r, slot], partner(k), half,
        )

    def main_arriving(r, src, dst, send, recv, k):
        rows = pl.ds(pl.multiple_of(HALO + slot * STRIP + r * GROUP, 8), GROUP)
        return copy(
            src(k).at[:, :, group_rows(r)], dst.at[:, :, rows],
            send.at[r, k], recv.at[r, k], partner(k), half,
        )

    def spread_start(r, src, dst, send, recv):
        partners(lambda k: main_copy(r, src, dst, send, recv, k).start())

        @pl.when(jnp.logical_not(apart))
        def _():
            own = pl.ds(pl.multiple_of(HALO + slot * STRIP + r * GROUP, 8), GROUP)
            dst[:, :, own] = src(slot)[:, :, group_rows(r)]

    def spread_arrived(r, src, dst, send, recv):
        partners(lambda k: main_arriving(r, src, dst, send, recv, k).wait_recv())

    def spread_sent(r, src, dst, send, recv):
        partners(lambda k: main_copy(r, src, dst, send, recv, k).wait_send())

    facing = (8 * (1 - half) + slot) * NZ + z
    down = HALO + BLOCK - HALO

    def halo_copy(field, send, recv, far):
        goes_down = (core == 1) if far else (core == 0)
        first = pl.multiple_of(jnp.where(goes_down, down, HALO), 8)
        into = pl.multiple_of(jnp.where(goes_down, 0, HALO + BLOCK), 8)
        index = 1 if far else 0
        return copy(
            field.at[:, :, pl.ds(first, HALO)], field.at[:, :, pl.ds(into, HALO)],
            send.at[index], recv.at[index], facing if far else n, other,
        )

    def halo(field, send, recv, act):
        act(halo_copy(field, send, recv, False))

        @pl.when(apart)
        def _():
            act(halo_copy(field, send, recv, True))

    @pl.when(jnp.logical_not(apart))
    def _():
        outer = pl.ds(pl.multiple_of(core * (HALO + BLOCK), 8), HALO)
        fq[:, :, outer] = jnp.zeros((1, 4, HALO, 128), jnp.float32)
        ta[:, :, outer] = jnp.zeros((2, 4, HALO, 128), jnp.float32)

    def plane_to_ring(r):
        each(1, NQ, lambda d: p2_copy(r, d).wait_recv())
        plane_forward(r)
        each(1, NZ, lambda d: p3_copy(r, d).start())
        a2[z, :, group_rows(r)] = yb[z, :, group_rows(r)]

    plane_to_ring(0)

    @pl.when(z != NZ - 1)
    def _():
        f2_copy(1).wait_recv()

    for row in (0, 8):
        own = cond[pl.ds(pl.multiple_of(q * STRIP + row, 8), 8)]
        frozen = conductance(own, fstrip[row : row + 8])
        for u, part in enumerate(columns_spread(quarters(frozen))):
            fmix[0, u, row : row + 8] = part

    f3 = (lambda k: fmix, fq, f3_send, f3_recv)
    for r in range(2):
        spread_start(r, *f3)

    plane_to_ring(1)
    for r in range(2):
        spread_arrived(r, *f3)
    halo(fq, fh_send, fh_recv, lambda item: item.start())

    twiddle = [(scalar(T_TWIDDLE + 2 * k), scalar(T_TWIDDLE + 2 * k + 1)) for k in range(NZ)]
    start = 2 * NZ * half
    twiddle_first = (scalar(T_TWIDDLE + start), scalar(T_TWIDDLE + start + 1))
    sign = jnp.where(half == 1, -1.0, 1.0)

    def source(k):
        return (k + NZ - half) % NZ

    def ring_forward(r):
        rows = group_rows(r)

        @pl.when(z != 0)
        def _():
            def body(u, columns):
                values = []
                for k in range(NZ):
                    real, imag = a2[source(k), 0, rows, columns], a2[source(k), 1, rows, columns]
                    cosine, sine = twiddle[k] if k else twiddle_first
                    values.append((cosine * real + sine * imag, cosine * imag - sine * real))
                for k, value in enumerate(complex_transform(values, -1.0)):
                    sb[k, 0, u, rows] = value[0]
                    sb[k, 1, u, rows] = value[1]

            tiles(body)

        @pl.when(z == 0)
        def _():
            def body(u, columns):
                even = real_forward([a2[source(k), 0, rows, columns] for k in range(NZ)])
                sb[0, 0, u, rows] = even[0][0]
                sb[0, 1, u, rows] = even[4][0]
                values = [a2[source(k), 1, rows, columns] for k in range(NZ)]
                values[0] = sign * values[0]
                odd = [turned((values[k], -values[k + 4]), -k / 16) for k in range(4)]
                odd = complex_transform(odd, -1.0)
                for k, value in list(zip((1, 2, 3), even[1:4])) + list(zip((4, 5, 6, 7), odd)):
                    sb[k, 0, u, rows] = value[0]
                    sb[k, 1, u, rows] = value[1]

            tiles(body)

    p4 = (lambda k: sb.at[k], ta, p4_send, p4_recv)
    for r in range(2):
        each(1, NZ, lambda d: p3_copy(r, d).wait_recv())
        ring_forward(r)
        rearranged(sb, r, columns_spread)
        spread_start(r, *p4)
    halo(fq, fh_send, fh_recv, lambda item: item.wait_recv())
    top = half * ROWS + core * BLOCK - HALO
    scale = TAU / HALF

    def spaced(ref, field, t):
        rows = pl.ds(t, 8, stride=GROUPS)
        return [ref[field, u, rows] for u in range(4)]

    def weights(t, here, below):
        row = GROUPS * sublane + t
        closed = (row == SPAN - 1) | (row + top == 2 * ROWS - 1) | (row + top == -1)
        rim = (row + top == 0) | (row + top == 2 * ROWS - 1)
        before = pltpu.roll(here[3], 1, 1)
        beyond = [here[1], here[2], here[3], pltpu.roll(here[0], 127, 1)]
        west[t] = jnp.where(lane == 0, 0.0, scale * (here[0] + before))
        for u in range(4):
            columns = slice(u * 128, (u + 1) * 128)
            wts[0, t, :, columns] = jnp.where(closed, 0.0, scale * (here[u] + below[u]))
            east = scale * (here[u] + beyond[u])
            center = jnp.where(rim, scale * here[u], 0.0) - 2.0
            if u == 0:
                center = center + jnp.where(lane == 0, scale * here[u], 0.0)
            if u == 3:
                center = center + jnp.where(lane == 127, scale * here[u], 0.0)
                east = jnp.where(lane == 127, 0.0, east)
            wts[1, t, :, columns] = east
            wts[2, t, :, columns] = center

    def weight_rows(t, carry):
        weights(t, spaced(fq, 0, t), spaced(fq, 0, t + 1))
        return carry

    lax.fori_loop(0, GROUPS - 1, weight_rows, 0, unroll=3)
    weights(
        GROUPS - 1,
        spaced(fq, 0, GROUPS - 1),
        [pltpu.roll(part, 7, 0) for part in spaced(fq, 0, 0)],
    )
    tj[...] = jnp.zeros(tj.shape, jnp.float32)
    for r in range(2):
        spread_arrived(r, *p4)
    halo(ta, p4h_send, p4h_recv, lambda item: item.start())
    halo(ta, p4h_send, p4h_recv, lambda item: item.wait_recv())


    first = [scalar(T_DELTA + k) for k in range(3)]

    def begin(t, carry):
        real, imag = spaced(ta, 0, t), spaced(ta, 1, t)
        for u in range(4):
            columns = slice(u * 128, (u + 1) * 128)
            ti[0, t, :, columns] = real[u]
            ti[1, t, :, columns] = imag[u]
            xi[0, t, :, columns] = first[0] * real[u] - first[1] * imag[u]
            xi[1, t, :, columns] = first[1] * real[u] + first[2] * imag[u]
        return carry

    lax.fori_loop(0, GROUPS, begin, 0, unroll=2)

    def swept_row(now, old, t, here, below, flux_above, factors):
        south, east, center = (quarters(wts[k, t]) for k in range(3))
        west_weight = west[t]
        fresh, flux_below = [], []
        for field in range(2):
            v = here[field]
            before, beyond = pltpu.roll(v[3], 1, 1), pltpu.roll(v[0], 127, 1)
            eastward = [east[u] * ((v[u + 1] if u < 3 else beyond) - v[u]) for u in range(4)]
            westward = [west_weight * (v[0] - before)] + eastward[:3]
            downward = [south[u] * (below[field][u] - v[u]) for u in range(4)]
            result = []
            for u in range(4):
                columns = slice(u * 128, (u + 1) * 128)
                value = (center[u] * v[u] - old[field, t, :, columns]) + (
                    (flux_above[field][u] - downward[u]) + (westward[u] - eastward[u])
                )
                old[field, t, :, columns] = value
                result.append(value)
            fresh.append(result)
            flux_below.append(downward)
        if factors is not None:
            for u in range(4):
                columns = slice(u * 128, (u + 1) * 128)
                real, imag = here[0][u], here[1][u]
                xi[0, t, :, columns] = xi[0, t, :, columns] + (
                    (factors[0] * real - factors[1] * imag)
                    + (factors[3] * fresh[0][u] - factors[4] * fresh[1][u])
                )
                xi[1, t, :, columns] = xi[1, t, :, columns] + (
                    (factors[1] * real + factors[2] * imag)
                    + (factors[4] * fresh[0][u] + factors[5] * fresh[1][u])
                )
        return flux_below

    def sweep(now, old, factors):
        begin_rows = [quarters(now[field, 0]) for field in range(2)]
        wrapped = [[pltpu.roll(part, 7, 0) for part in begin_rows[field]] for field in range(2)]
        end_rows = [quarters(now[field, GROUPS - 1]) for field in range(2)]
        end_south = quarters(wts[0, GROUPS - 1])
        flux_above = [
            [
                pltpu.roll(end_south[u] * (wrapped[field][u] - end_rows[field][u]), 1, 0)
                for u in range(4)
            ]
            for field in range(2)
        ]

        def one(t, carried):
            here, above = carried
            below = [quarters(now[field, t + 1]) for field in range(2)]
            return below, swept_row(now, old, t, here, below, above, factors)

        here, above = lax.fori_loop(
            0, GROUPS - 1, one, (begin_rows, flux_above), unroll=GROUPS - 1
        )
        swept_row(now, old, GROUPS - 1, here, wrapped, above, factors)

    def two_sweeps(m, carry):
        k = 2 * m + 1
        factors = [scalar(T_DELTA + 3 * k + each) for each in range(6)]
        sweep(ti, tj, None)
        sweep(tj, ti, factors)
        return carry

    lax.fori_loop(0, SWEEPS // 2, two_sweeps, 0)

    def finish(t, carry):
        for field in range(2):
            for u in range(4):
                columns = slice(u * 128, (u + 1) * 128)
                xb[field, u, pl.ds(t, 8, stride=GROUPS)] = xi[field, t, :, columns]
        return carry

    lax.fori_loop(0, GROUPS, finish, 0, unroll=2)

    def p6_copy(r, k, index):
        rows = pl.ds(pl.multiple_of(HALO + k * STRIP + r * GROUP, 8), GROUP)
        return copy(
            xb.at[:, :, rows], a3.at[slot, :, :, group_rows(r)],
            p6_send.at[r, k], p6_recv.at[r, index], partner(k), half,
        )

    for r in range(2):
        partners(lambda k: p6_copy(r, k, slot).start())

        @pl.when(jnp.logical_not(apart))
        def _():
            own = pl.ds(pl.multiple_of(HALO + slot * STRIP + r * GROUP, 8), GROUP)
            a3[slot, :, :, group_rows(r)] = xb[:, :, own]

    def ring_backward(r):
        rows = group_rows(r)

        @pl.when(z != 0)
        def _():
            def body(u, columns):
                values = [(a3[k, 0, u, rows], a3[k, 1, u, rows]) for k in range(8)]
                for k, (real, imag) in enumerate(complex_transform(values, 1.0)):
                    cosine, sine = twiddle[k]
                    if k:
                        real, imag = cosine * real - sine * imag, cosine * imag + sine * real
                    ub[k, 0, u, rows] = real
                    ub[k, 1, u, rows] = imag

            tiles(body)

        @pl.when(z == 0)
        def _():
            def body(u, columns):
                values = [(a3[k, 0, u, rows], a3[k, 1, u, rows]) for k in range(8)]
                even = [(values[0][0], None)] + values[1:4] + [(values[0][1], None)]
                for k, value in enumerate(real_backward(even)):
                    ub[k, 0, u, rows] = value
                for k, value in enumerate(complex_transform(values[4:8], 1.0)):
                    real, imag = turned(value, k / 16)
                    ub[k, 1, u, rows] = 2.0 * real
                    ub[k + 4, 1, u, rows] = -2.0 * imag

            tiles(body)

    def p7_copy(r, d):
        rows = group_rows(r)
        return copy(
            ub.at[(z + d) % NZ, :, :, rows], a4.at[z, :, :, rows],
            p7_send.at[r, d], p7_recv.at[r, d], ring(d), core,
        )

    for r in range(2):
        partners(lambda k: p6_copy(r, k, k).wait_recv())
        ring_backward(r)
        rearranged(ub, r, columns_joined)
        each(1, NZ, lambda d: p7_copy(r, d).start())
        a4[z, :, :, group_rows(r)] = ub[z, :, :, group_rows(r)]

    scale_out = [scalar(T_OUT + k) for k in range(NQ)]

    def plane_backward(r):
        rows = group_rows(r)

        def body(u, columns):
            values = [(a4[k, 0, u, rows], a4[k, 1, u, rows]) for k in range(8)]
            values = [(values[0][0], None)] + values[1:] + [(values[0][1], None)]
            for k, value in enumerate(real_backward(values)):
                cb[k, rows, columns] = scale_out[k] * value

        tiles(body)

    def p8_copy(r, d):
        rows = group_rows(r)
        return copy(
            cb.at[(q + d) % NQ, rows], out.at[q, rows],
            p8_send.at[r, d], p8_recv.at[r, d], plane(d), core,
        )

    own_strips = [
        pltpu.make_async_copy(
            cb.at[q, group_rows(r)], out.at[q, group_rows(r)], load_sem.at[4 + r]
        )
        for r in range(2)
    ]
    for r in range(2):
        each(1, NZ, lambda d: p7_copy(r, d).wait_recv())
        plane_backward(r)
        each(1, NQ, lambda d: p8_copy(r, d).start())
        own_strips[r].start()

    for item in edges_out:
        item.wait_send()
    for r in range(2):
        shift_on(w_strips, r).wait_send()
        shift_back(r).wait_send()

    @pl.when(owner)
    def _():
        each(1, NQ, lambda d: f1_copy(d).wait_send())

    @pl.when(z == NZ - 1)
    def _():
        each(1, NZ, lambda d: f2_copy(d).wait_send())

    for r in range(2):
        each(1, NQ, lambda d: p2_copy(r, d).wait_send())
        for sent in (p3_copy, p7_copy):
            each(1, NZ, lambda d: sent(r, d).wait_send())
        partners(lambda k: p6_copy(r, k, slot).wait_send())
        spread_sent(r, *f3)
        spread_sent(r, *p4)
    halo(fq, fh_send, fh_recv, lambda item: item.wait_send())
    halo(ta, p4h_send, p4h_recv, lambda item: item.wait_send())

    for r in range(2):
        each(1, NQ, lambda d: p8_copy(r, d).wait_recv())
        own_strips[r].wait()
        each(1, NQ, lambda d: p8_copy(r, d).wait_send())


def body(window_state, prior_window, conductivity):
    f32 = jnp.float32
    dma = pltpu.SemaphoreType.DMA
    padded_rows = ROWS + 2 * PAD
    strips = (NQ, STRIP, COLS)
    pairs = (8, 2, STRIP, COLS)
    pairs_apart = (8, 2, 4, STRIP, 128)
    shapes = [
        (ROWS, COLS),
        (padded_rows, COLS),
        (padded_rows, COLS),
        (2, 8, COLS),
        strips,
        strips,
        strips,
        strips,
        pairs,
        pairs,
        pairs_apart,
        strips,
        (STRIP, COLS),
        (1, 4, STRIP, 128),
        (1, 4, SPAN, 128),
        (2, 4, SPAN, 128),
        (2, GROUPS, 8, COLS),
        (2, GROUPS, 8, COLS),
        (2, GROUPS, 8, COLS),
        (2, 4, SPAN, 128),
        (3, GROUPS, 8, COLS),
        (GROUPS, 8, 128),
        pairs_apart,
        pairs_apart,
        pairs_apart,
        strips,
    ]
    sems = [(6,), (2,), (2,), (2, 2), (2, 2), (16,), (1,), (8,), (1,), (2, 8), (2, 8), (2,), (2,)]
    sems += [(2, 16), (2, 16), (2, 8), (2, 8), (2, 8), (2, 8), (2,), (2,)]
    sems += [(2, 8), (2, 8), (2, 8), (2, 8), (2, 16), (2, 16)]
    correction = pl.pallas_call(
        kernel,
        out_shape=jax.ShapeDtypeStruct(strips, f32),
        in_specs=5 * [pl.BlockSpec(memory_space=pl.ANY)],
        out_specs=pl.BlockSpec(memory_space=pl.ANY),
        scratch_shapes=[pltpu.SMEM((1, T_WIDTH), f32)]
        + [pltpu.VMEM(shape, f32) for shape in shapes]
        + [dma(shape) for shape in sems],
        compiler_params=pltpu.CompilerParams(
            collective_id=0, has_side_effects=True, vmem_limit_bytes=60 * 1024 * 1024
        ),
    )(
        jnp.asarray(scalar_table()),
        window_state[0],
        window_state.reshape(strips),
        prior_window.reshape(strips),
        conductivity,
    )
    return window_state + correction.reshape(1, ROWS, COLS)


def solution(mesh):
    in_specs = (P("tm", "space", None), P("tm", "space", None), P("space", None))
    out_specs = P("tm", "space", None)
    return jax.shard_map(body, mesh=mesh, in_specs=in_specs, out_specs=out_specs, check_vma=False)
```

```python
import math

import jax
import jax.numpy as jnp
import numpy as np
from jax import lax
from jax.experimental import pallas as pl
from jax.experimental.pallas import tpu as pltpu
from jax.sharding import PartitionSpec as P

SWEEPS = 24
STEPS = 128
TAU = 2.0
ALPHA = 0.01
HALF = 12.0 * TAU

NQ, NZ = 16, 8
ROWS, COLS = 256, 512
STRIP = 16
BLOCK = 128
HALO = 24
SPAN = BLOCK + 2 * HALO
PAD = 8
GROUP = 8
GROUPS = SPAN // 8
MESH = pl.DeviceIdType.MESH

T_DELTA, T_IN, T_NEXT, T_TWIDDLE, T_OUT, T_WIDTH = 0, 75, 76, 80, 100, 128


def shift_of(frequency):
    beta = math.exp(math.log(ALPHA) / STEPS)
    angle = 2.0 * math.pi * frequency / STEPS
    return 1.0 - beta * math.cos(angle) + 1j * beta * math.sin(angle)


def polynomial_of(frequency):
    points = 64
    theta = (np.arange(points) + 0.5) * np.pi / points
    image_factor = shift_of(frequency) + HALF * (np.cos(theta) + 1.0)
    center = shift_of(frequency) + HALF
    relative = center / HALF
    solution = np.zeros(points, complex)
    remain = np.ones(points, complex)
    search = remain / center
    factor = 1.0 / relative
    for _ in range(SWEEPS):
        solution = solution + search
        remain = remain - image_factor * search
        renewed = 1.0 / (2.0 * relative - factor)
        search = renewed * factor * search + (2.0 * renewed / HALF) * remain
        factor = renewed
    values = solution + search
    first = [2.0 / points * np.sum(values * np.cos(k * theta)) for k in range(SWEEPS + 3)]
    first[0] = first[0] / 2
    second = [(first[k] - first[k + 2]) / 2 for k in range(SWEEPS + 1)]
    second[0] = first[0] - first[2] / 2
    return np.array(second)


def frequency_of(pair, slot):
    if pair:
        return pair + 16 * slot
    return 16 * slot if slot < 4 else 8 + 32 * (slot - 4)


def scalar_table():
    table = np.zeros((STEPS, T_WIDTH))
    for step in range(STEPS):
        plane, ring = step // NZ, step % NZ
        slot = plane % 8
        delta = polynomial_of(frequency_of(ring, slot))
        real, imag, last = delta.real, delta.imag, delta.real
        if ring == 0 and slot == 0:
            imag, last = 0.0 * imag, polynomial_of(64).real
        table[step, 0:75:3], table[step, 1:75:3], table[step, 2:75:3] = real, imag, last
        table[step, T_IN] = math.exp(math.log(ALPHA) * step / STEPS)
        following = (step + 1) % STEPS
        table[step, T_NEXT] = math.exp(math.log(ALPHA) * following / STEPS)
        for k in range(NQ):
            arrival = NZ * k + ring
            table[step, T_OUT + k] = math.exp(-math.log(ALPHA) * arrival / STEPS) / STEPS
        for k in range(NZ + 1):
            angle = 2.0 * math.pi * ring * k / STEPS
            table[step, T_TWIDDLE + 2 * k] = math.cos(angle)
            table[step, T_TWIDDLE + 2 * k + 1] = math.sin(angle)
    return table.astype(np.float32).reshape(STEPS, 1, T_WIDTH)


def turned(value, turn):
    real, imag = value
    turn = turn % 1.0
    if turn == 0.0:
        return value
    if turn == 0.25:
        return ((-imag if imag is not None else None), real)
    if turn == 0.5:
        return (-real, -imag if imag is not None else None)
    if turn == 0.75:
        return (imag, -real)
    cosine, sine = math.cos(2 * math.pi * turn), math.sin(2 * math.pi * turn)
    if imag is None:
        return (cosine * real, sine * real)
    if turn % 0.25 == 0.125:
        scale = math.sqrt(0.5)
        if turn == 0.125:
            return (scale * (real - imag), scale * (real + imag))
        if turn == 0.375:
            return (-scale * (real + imag), scale * (real - imag))
        if turn == 0.625:
            return (scale * (imag - real), -scale * (real + imag))
        return (scale * (real + imag), scale * (imag - real))
    return (cosine * real - sine * imag, sine * real + cosine * imag)


def part_sum(left, right):
    if left is None:
        return right
    return left if right is None else left + right


def part_difference(left, right):
    if right is None:
        return left
    return -right if left is None else left - right


def plus(left, right):
    return (part_sum(left[0], right[0]), part_sum(left[1], right[1]))


def minus(left, right):
    return (part_difference(left[0], right[0]), part_difference(left[1], right[1]))


def conjugate(value):
    return (value[0], None if value[1] is None else -value[1])


def real_forward(values):
    count = len(values)
    if count == 2:
        return [(values[0] + values[1], None), (values[0] - values[1], None)]
    even, odd = real_forward(values[0::2]), real_forward(values[1::2])
    result = [None] * (count // 2 + 1)
    for k in range(count // 4 + 1):
        term = turned(odd[k], -k / count)
        result[k] = plus(even[k], term)
        if k < count // 4:
            result[count // 2 - k] = conjugate(minus(even[k], term))
    return result


def real_backward(values):
    count = 2 * (len(values) - 1)
    if count == 2:
        return [values[0][0] + values[1][0], values[0][0] - values[1][0]]
    even, odd = [], []
    for k in range(count // 4):
        mirror = conjugate(values[count // 2 - k])
        even.append(plus(values[k], mirror))
        odd.append(turned(minus(values[k], mirror), k / count))
    middle = values[count // 4]
    even.append((2.0 * middle[0], None))
    odd.append((-2.0 * middle[1], None))
    result = [None] * count
    result[0::2], result[1::2] = real_backward(even), real_backward(odd)
    return result


def complex_transform(values, sign):
    count = len(values)
    if count == 1:
        return values
    even = complex_transform(values[0::2], sign)
    odd = complex_transform(values[1::2], sign)
    odd = [turned(odd[k], sign * k / count) for k in range(count // 2)]
    return [plus(a, b) for a, b in zip(even, odd)] + [minus(a, b) for a, b in zip(even, odd)]


def conductance(conductivity, values):
    return conductivity * (1.0 + 0.5 * jnp.tanh(values))


def kernel(
    table_in, w, w_strips, prior, cond_in, out,
    table, cond, wp, qp, edge, flux, prev, res, a1, yb, a2, sb, pb, fstrip, fmix, fq,
    ta, ti, tj, xi, xb, wts, west, a3, ub, a4, cb, load_sem,
    edge_send, edge_recv, shift_send, shift_recv,
    f1_send, f1_recv, f2_send, f2_recv, f3_send, f3_recv, fh_send, fh_recv,
    p2_send, p2_recv, p3_send, p3_recv, p4_send, p4_recv, p4h_send, p4h_recv,
    p6_send, p6_recv, p7_send, p7_recv, p8_send, p8_recv,
):
    n = lax.axis_index("tm")
    core = lax.axis_index("space")
    q, z = n // NZ, n % NZ
    half, slot = q // 8, q % 8
    other = 1 - core
    apart = half != core
    owner = n == STEPS - 1

    def scalar(index):
        return table[0, index]

    def plane(distance):
        return ((q + distance) % NQ) * NZ + z

    def ring(distance):
        return q * NZ + (z + distance) % NZ

    def partner(k):
        return (8 * core + k) * NZ + z

    def copy(src, dst, send, recv, step, space):
        return pltpu.make_async_remote_copy(
            src_ref=src, dst_ref=dst, send_sem=send, recv_sem=recv,
            device_id=(step, space), device_id_type=MESH,
        )

    def each(low, high, act):
        def one(d, carry):
            act(d)
            return carry

        lax.fori_loop(low, high, one, 0)

    def ring_order(act):
        def one(i, carry):
            step = (i + 1) // 2
            far = NZ // 2 + jnp.where(i % 2 == 1, -step, step)
            act(far)
            return carry

        lax.fori_loop(0, NZ - 1, one, 0)

    loads = [
        pltpu.make_async_copy(w, wp.at[pl.ds(PAD, ROWS)], load_sem.at[0]),
        pltpu.make_async_copy(cond_in, cond, load_sem.at[1]),
        pltpu.make_async_copy(table_in.at[n], table, load_sem.at[2]),
    ]
    for load in loads:
        load.start()
    prior_load = pltpu.make_async_copy(prior, pb, load_sem.at[3])

    @pl.when(owner)
    def _():
        prior_load.start()

    barrier = pltpu.get_barrier_semaphore()

    def greet(step, space):
        pl.semaphore_signal(barrier, inc=1, device_id=(step, space), device_id_type=MESH)

    greet(n, other)
    before, after = (n + STEPS - 1) % STEPS, (n + 1) % STEPS
    greet(before, core)
    greet(after, core)
    each(1, NQ, lambda d: greet(plane(d), core))
    each(1, NZ, lambda d: greet(ring(d), core))

    @pl.when(apart)
    def _():
        each(0, 8, lambda k: greet(partner(k), half))

    zero_rows = jnp.zeros((8, COLS), jnp.float32)
    for load in loads:
        load.wait()
    qp[PAD : PAD + ROWS] = conductance(cond[...], wp[PAD : PAD + ROWS])
    for ref in (wp, qp):
        ref[0:PAD] = zero_rows
        ref[PAD + ROWS : PAD + ROWS + 8] = zero_rows

    pl.semaphore_wait(barrier, NQ - 1 + NZ - 1 + 3 + jnp.where(apart, 8, 0))

    edge_row = pl.multiple_of((1 - core) * (ROWS - 8), 8)
    edges_out = [
        copy(src.at[pl.ds(edge_row, 8)], edge.at[k], edge_send.at[k], edge_recv.at[k], n, other)
        for k, src in enumerate((w, cond_in))
    ]
    for item in edges_out:
        item.start()

    def group_rows(r):
        return pl.ds(r * GROUP, GROUP)

    def shift_on(src, r):
        return copy(
            src.at[pl.ds(0, 8), group_rows(r)], prev.at[pl.ds(0, 8), group_rows(r)],
            shift_send.at[0, r], shift_recv.at[0, r], after, core,
        )

    def shift_back(r):
        return copy(
            flux.at[pl.ds(8, 8), group_rows(r)], prev.at[pl.ds(8, 8), group_rows(r)],
            shift_send.at[1, r], shift_recv.at[1, r], before, core,
        )

    def shift_on_start(r):
        @pl.when(jnp.logical_not(owner))
        def _():
            shift_on(w_strips, r).start()

        @pl.when(owner)
        def _():
            shift_on(prior, r).start()

    shift_on_start(0)

    def f1_copy(d):
        target = (q + d) % NQ
        return copy(
            prior.at[target], fstrip, f1_send.at[d], f1_recv.at[0], target * NZ + z, core
        )

    def f2_copy(d):
        return copy(fstrip, fstrip, f2_send.at[d], f2_recv.at[0], ring(d), core)

    @pl.when(owner)
    def _():
        each(1, NQ, lambda d: f1_copy(d).start())
        prior_load.wait()
        fstrip[...] = pb[NQ - 1]

    column = lax.broadcasted_iota(jnp.int32, (8, COLS), 1)
    first_column, last_column = column == 0, column == COLS - 1

    def inside_four(window):
        center = window[8:16]
        return (
            window[7:15],
            window[9:17],
            jnp.where(first_column, 0.0, pltpu.roll(center, 1, 1)),
            jnp.where(last_column, 0.0, pltpu.roll(center, COLS - 1, 1)),
        )

    def fluxes(first_strip, r):
        def one(k, carry):
            rows = pl.ds(pl.multiple_of(k * STRIP + r * GROUP, 8), 24)
            state, coeff = wp[rows], qp[rows]
            here, coeff_here = state[8:16], coeff[8:16]
            total = -here
            for near, near_coeff in zip(inside_four(state), inside_four(coeff)):
                total = total + (0.5 * TAU) * (coeff_here + near_coeff) * (near - here)
            flux[k, group_rows(r)] = total
            return carry

        lax.fori_loop(first_strip, first_strip + 8, one, 0, unroll=2)

    fluxes(8, 0)
    shift_back(0).start()
    for item in edges_out:
        item.wait_recv()
    beside = pl.multiple_of((1 - core) * (PAD + ROWS), 8)
    wp[pl.ds(beside, 8)] = edge[0]
    qp[pl.ds(beside, 8)] = conductance(edge[1], edge[0])
    fluxes(8, 1)
    shift_on(w_strips, 0).wait_send()
    shift_on_start(1)
    shift_back(0).wait_send()
    shift_back(1).start()

    fluxes(0, 0)
    fluxes(0, 1)

    @pl.when(z == NZ - 1)
    def _():
        @pl.when(q != NQ - 1)
        def _():
            f1_copy(1).wait_recv()

        each(1, NZ, lambda d: f2_copy(d).start())

    def p2_copy(r, d):
        target = (q + d) % NQ
        return copy(
            res.at[target, group_rows(r)], a1.at[q, group_rows(r)],
            p2_send.at[r, d], p2_recv.at[r, d], target * NZ + z, core,
        )

    damping, damping_next = scalar(T_IN), scalar(T_NEXT)

    def residuals(r):
        rows = group_rows(r)

        def on(k, carry):
            res[k, rows] = (prev[k, rows] + flux[k, rows]) * damping
            return carry

        def back(k, carry):
            own = wp[pl.ds(pl.multiple_of(PAD + k * STRIP + r * GROUP, 8), GROUP)]
            res[k, rows] = (own + prev[k, rows]) * damping_next
            return carry

        def back_first(k, carry):
            res[k, rows] = (pb[k, rows] + prev[k, rows]) * damping_next
            return carry

        shift_back(r).wait_recv()

        @pl.when(jnp.logical_not(owner))
        def _():
            lax.fori_loop(8, 16, back, 0, unroll=4)

        @pl.when(owner)
        def _():
            lax.fori_loop(8, 16, back_first, 0, unroll=4)

        shift_on(w_strips, r).wait_recv()
        lax.fori_loop(0, 8, on, 0, unroll=4)
        each(1, NQ, lambda d: p2_copy(r, d).start())
        a1[q, rows] = res[q, rows]

    residuals(0)
    residuals(1)

    def tiles(body):
        def one(u, carry):
            body(u, pl.ds(pl.multiple_of(u * 128, 128), 128))
            return carry

        lax.fori_loop(0, 4, one, 0, unroll=2)

    def plane_forward(r):
        rows = group_rows(r)

        def body(u, columns):
            result = real_forward([a1[k, rows, columns] for k in range(NQ)])
            yb[0, 0, rows, columns] = result[0][0]
            yb[0, 1, rows, columns] = result[8][0]
            for k in range(1, 8):
                yb[k, 0, rows, columns] = result[k][0]
                yb[k, 1, rows, columns] = result[k][1]

        tiles(body)

    def p3_copy(r, d):
        rows = group_rows(r)
        return copy(
            yb.at[(z + d) % NZ, :, rows], a2.at[z, :, rows],
            p3_send.at[r, d], p3_recv.at[r, d], ring(d), core,
        )


    lane = lax.broadcasted_iota(jnp.int32, (8, 128), 1)
    sublane = lax.broadcasted_iota(jnp.int32, (8, 128), 0)

    def one_of(parts, choice):
        low = jnp.where(choice == 0, parts[0], parts[1])
        return jnp.where(choice < 2, low, jnp.where(choice == 2, parts[2], parts[3]))

    def moved(part, index):
        return jnp.take_along_axis(part, index, axis=1)

    within, block = lane % 4, lane // 32

    def columns_spread(parts):
        mixed = [one_of(parts, (within + s) % 4) for s in range(4)]
        mixed = [moved(mixed[s], 4 * (lane % 32) + (block - s) % 4) for s in range(4)]
        return [one_of(mixed, (block - u) % 4) for u in range(4)]

    def columns_joined(parts):
        mixed = [one_of(parts, (block - s) % 4) for s in range(4)]
        mixed = [moved(mixed[s], 32 * ((within + s) % 4) + lane // 4) for s in range(4)]
        return [one_of(mixed, (u - within) % 4) for u in range(4)]

    def quarters(value):
        return [value[:, u * 128 : (u + 1) * 128] for u in range(4)]

    def rearranged(ref, r, change):
        rows = group_rows(r)

        def one(t, carry):
            for field in range(2):
                parts = change([ref[t, field, u, rows] for u in range(4)])
                for u, part in enumerate(parts):
                    ref[t, field, u, rows] = part
            return carry

        lax.fori_loop(0, 8, one, 0, unroll=4)

    def partners(act):
        each(1, 8, lambda d: act((slot + d) % 8))

        @pl.when(apart)
        def _():
            act(slot)

    def main_copy(r, src, dst, send, recv, k):
        rows = pl.ds(pl.multiple_of(HALO + slot * STRIP + r * GROUP, 8), GROUP)
        return copy(
            src(k).at[:, :, group_rows(r)], dst.at[:, :, rows],
            send.at[r, k], recv.at[r, slot], partner(k), half,
        )

    def main_arriving(r, src, dst, send, recv, k):
        rows = pl.ds(pl.multiple_of(HALO + slot * STRIP + r * GROUP, 8), GROUP)
        return copy(
            src(k).at[:, :, group_rows(r)], dst.at[:, :, rows],
            send.at[r, k], recv.at[r, k], partner(k), half,
        )

    def spread_start(r, src, dst, send, recv):
        partners(lambda k: main_copy(r, src, dst, send, recv, k).start())

        @pl.when(jnp.logical_not(apart))
        def _():
            own = pl.ds(pl.multiple_of(HALO + slot * STRIP + r * GROUP, 8), GROUP)
            dst[:, :, own] = src(slot)[:, :, group_rows(r)]

    def spread_arrived(r, src, dst, send, recv):
        partners(lambda k: main_arriving(r, src, dst, send, recv, k).wait_recv())

    def spread_sent(r, src, dst, send, recv):
        partners(lambda k: main_copy(r, src, dst, send, recv, k).wait_send())

    facing = (8 * (1 - half) + slot) * NZ + z
    down = HALO + BLOCK - HALO

    def halo_copy(field, send, recv, far):
        goes_down = (core == 1) if far else (core == 0)
        first = pl.multiple_of(jnp.where(goes_down, down, HALO), 8)
        into = pl.multiple_of(jnp.where(goes_down, 0, HALO + BLOCK), 8)
        index = 1 if far else 0
        return copy(
            field.at[:, :, pl.ds(first, HALO)], field.at[:, :, pl.ds(into, HALO)],
            send.at[index], recv.at[index], facing if far else n, other,
        )

    def halo(field, send, recv, act):
        act(halo_copy(field, send, recv, False))

        @pl.when(apart)
        def _():
            act(halo_copy(field, send, recv, True))

    @pl.when(jnp.logical_not(apart))
    def _():
        outer = pl.ds(pl.multiple_of(core * (HALO + BLOCK), 8), HALO)
        fq[:, :, outer] = jnp.zeros((1, 4, HALO, 128), jnp.float32)
        ta[:, :, outer] = jnp.zeros((2, 4, HALO, 128), jnp.float32)

    def plane_to_ring(r):
        each(1, NQ, lambda d: p2_copy(r, d).wait_recv())
        plane_forward(r)
        if r:
            each(1, NZ, lambda d: p3_copy(0, d).wait_send())
        ring_order(lambda d: p3_copy(r, d).start())
        a2[z, :, group_rows(r)] = yb[z, :, group_rows(r)]

    plane_to_ring(0)

    @pl.when(z != NZ - 1)
    def _():
        f2_copy(1).wait_recv()

    for row in (0, 8):
        own = cond[pl.ds(pl.multiple_of(q * STRIP + row, 8), 8)]
        frozen = conductance(own, fstrip[row : row + 8])
        for u, part in enumerate(columns_spread(quarters(frozen))):
            fmix[0, u, row : row + 8] = part

    f3 = (lambda k: fmix, fq, f3_send, f3_recv)
    for r in range(2):
        spread_start(r, *f3)

    plane_to_ring(1)
    for r in range(2):
        spread_arrived(r, *f3)
    halo(fq, fh_send, fh_recv, lambda item: item.start())

    twiddle = [(scalar(T_TWIDDLE + 2 * k), scalar(T_TWIDDLE + 2 * k + 1)) for k in range(NZ)]
    start = 2 * NZ * half
    twiddle_first = (scalar(T_TWIDDLE + start), scalar(T_TWIDDLE + start + 1))
    sign = jnp.where(half == 1, -1.0, 1.0)

    def source(k):
        return (k + NZ - half) % NZ

    def ring_forward(r):
        rows = group_rows(r)

        @pl.when(z != 0)
        def _():
            def body(u, columns):
                values = []
                for k in range(NZ):
                    real, imag = a2[source(k), 0, rows, columns], a2[source(k), 1, rows, columns]
                    cosine, sine = twiddle[k] if k else twiddle_first
                    values.append((cosine * real + sine * imag, cosine * imag - sine * real))
                for k, value in enumerate(complex_transform(values, -1.0)):
                    sb[k, 0, u, rows] = value[0]
                    sb[k, 1, u, rows] = value[1]

            tiles(body)

        @pl.when(z == 0)
        def _():
            def body(u, columns):
                even = real_forward([a2[source(k), 0, rows, columns] for k in range(NZ)])
                sb[0, 0, u, rows] = even[0][0]
                sb[0, 1, u, rows] = even[4][0]
                values = [a2[source(k), 1, rows, columns] for k in range(NZ)]
                values[0] = sign * values[0]
                odd = [turned((values[k], -values[k + 4]), -k / 16) for k in range(4)]
                odd = complex_transform(odd, -1.0)
                for k, value in list(zip((1, 2, 3), even[1:4])) + list(zip((4, 5, 6, 7), odd)):
                    sb[k, 0, u, rows] = value[0]
                    sb[k, 1, u, rows] = value[1]

            tiles(body)

    p4 = (lambda k: sb.at[k], ta, p4_send, p4_recv)
    for r in range(2):
        each(1, NZ, lambda d: p3_copy(r, d).wait_recv())
        ring_forward(r)
        rearranged(sb, r, columns_spread)
        spread_start(r, *p4)
    halo(fq, fh_send, fh_recv, lambda item: item.wait_recv())
    top = half * ROWS + core * BLOCK - HALO
    scale = TAU / HALF

    def spaced(ref, field, t):
        rows = pl.ds(t, 8, stride=GROUPS)
        return [ref[field, u, rows] for u in range(4)]

    def weights(t, here, below):
        row = GROUPS * sublane + t
        closed = (row == SPAN - 1) | (row + top == 2 * ROWS - 1) | (row + top == -1)
        rim = (row + top == 0) | (row + top == 2 * ROWS - 1)
        before = pltpu.roll(here[3], 1, 1)
        beyond = [here[1], here[2], here[3], pltpu.roll(here[0], 127, 1)]
        west[t] = jnp.where(lane == 0, 0.0, scale * (here[0] + before))
        for u in range(4):
            columns = slice(u * 128, (u + 1) * 128)
            wts[0, t, :, columns] = jnp.where(closed, 0.0, scale * (here[u] + below[u]))
            east = scale * (here[u] + beyond[u])
            center = jnp.where(rim, scale * here[u], 0.0) - 2.0
            if u == 0:
                center = center + jnp.where(lane == 0, scale * here[u], 0.0)
            if u == 3:
                center = center + jnp.where(lane == 127, scale * here[u], 0.0)
                east = jnp.where(lane == 127, 0.0, east)
            wts[1, t, :, columns] = east
            wts[2, t, :, columns] = center

    def weight_rows(t, carry):
        weights(t, spaced(fq, 0, t), spaced(fq, 0, t + 1))
        return carry

    lax.fori_loop(0, GROUPS - 1, weight_rows, 0, unroll=3)
    weights(
        GROUPS - 1,
        spaced(fq, 0, GROUPS - 1),
        [pltpu.roll(part, 7, 0) for part in spaced(fq, 0, 0)],
    )
    tj[...] = jnp.zeros(tj.shape, jnp.float32)
    for r in range(2):
        spread_arrived(r, *p4)
    halo(ta, p4h_send, p4h_recv, lambda item: item.start())
    halo(ta, p4h_send, p4h_recv, lambda item: item.wait_recv())


    first = [scalar(T_DELTA + k) for k in range(3)]

    def begin(t, carry):
        real, imag = spaced(ta, 0, t), spaced(ta, 1, t)
        for u in range(4):
            columns = slice(u * 128, (u + 1) * 128)
            ti[0, t, :, columns] = real[u]
            ti[1, t, :, columns] = imag[u]
            xi[0, t, :, columns] = first[0] * real[u] - first[1] * imag[u]
            xi[1, t, :, columns] = first[1] * real[u] + first[2] * imag[u]
        return carry

    lax.fori_loop(0, GROUPS, begin, 0, unroll=2)

    def swept_row(now, old, t, here, below, flux_above, factors):
        south, east, center = (quarters(wts[k, t]) for k in range(3))
        west_weight = west[t]
        fresh, flux_below = [], []
        for field in range(2):
            v = here[field]
            before, beyond = pltpu.roll(v[3], 1, 1), pltpu.roll(v[0], 127, 1)
            eastward = [east[u] * ((v[u + 1] if u < 3 else beyond) - v[u]) for u in range(4)]
            westward = [west_weight * (v[0] - before)] + eastward[:3]
            downward = [south[u] * (below[field][u] - v[u]) for u in range(4)]
            result = []
            for u in range(4):
                columns = slice(u * 128, (u + 1) * 128)
                value = (center[u] * v[u] - old[field, t, :, columns]) + (
                    (flux_above[field][u] - downward[u]) + (westward[u] - eastward[u])
                )
                old[field, t, :, columns] = value
                result.append(value)
            fresh.append(result)
            flux_below.append(downward)
        if factors is not None:
            for u in range(4):
                columns = slice(u * 128, (u + 1) * 128)
                real, imag = here[0][u], here[1][u]
                xi[0, t, :, columns] = xi[0, t, :, columns] + (
                    (factors[0] * real - factors[1] * imag)
                    + (factors[3] * fresh[0][u] - factors[4] * fresh[1][u])
                )
                xi[1, t, :, columns] = xi[1, t, :, columns] + (
                    (factors[1] * real + factors[2] * imag)
                    + (factors[4] * fresh[0][u] + factors[5] * fresh[1][u])
                )
        return flux_below

    def sweep(now, old, factors):
        begin_rows = [quarters(now[field, 0]) for field in range(2)]
        wrapped = [[pltpu.roll(part, 7, 0) for part in begin_rows[field]] for field in range(2)]
        end_rows = [quarters(now[field, GROUPS - 1]) for field in range(2)]
        end_south = quarters(wts[0, GROUPS - 1])
        flux_above = [
            [
                pltpu.roll(end_south[u] * (wrapped[field][u] - end_rows[field][u]), 1, 0)
                for u in range(4)
            ]
            for field in range(2)
        ]

        def one(t, carried):
            here, above = carried
            below = [quarters(now[field, t + 1]) for field in range(2)]
            return below, swept_row(now, old, t, here, below, above, factors)

        here, above = lax.fori_loop(
            0, GROUPS - 1, one, (begin_rows, flux_above), unroll=GROUPS - 1
        )
        swept_row(now, old, GROUPS - 1, here, wrapped, above, factors)

    def two_sweeps(m, carry):
        k = 2 * m + 1
        factors = [scalar(T_DELTA + 3 * k + each) for each in range(6)]
        sweep(ti, tj, None)
        sweep(tj, ti, factors)
        return carry

    lax.fori_loop(0, SWEEPS // 2, two_sweeps, 0)

    def finish(t, carry):
        for field in range(2):
            for u in range(4):
                columns = slice(u * 128, (u + 1) * 128)
                xb[field, u, pl.ds(t, 8, stride=GROUPS)] = xi[field, t, :, columns]
        return carry

    lax.fori_loop(0, GROUPS, finish, 0, unroll=2)

    def p6_copy(r, k, index):
        rows = pl.ds(pl.multiple_of(HALO + k * STRIP + r * GROUP, 8), GROUP)
        return copy(
            xb.at[:, :, rows], a3.at[slot, :, :, group_rows(r)],
            p6_send.at[r, k], p6_recv.at[r, index], partner(k), half,
        )

    for r in range(2):
        if r:
            partners(lambda k: p6_copy(0, k, slot).wait_send())
        partners(lambda k: p6_copy(r, k, slot).start())

        @pl.when(jnp.logical_not(apart))
        def _():
            own = pl.ds(pl.multiple_of(HALO + slot * STRIP + r * GROUP, 8), GROUP)
            a3[slot, :, :, group_rows(r)] = xb[:, :, own]

    def ring_backward(r):
        rows = group_rows(r)

        @pl.when(z != 0)
        def _():
            def body(u, columns):
                values = [(a3[k, 0, u, rows], a3[k, 1, u, rows]) for k in range(8)]
                for k, (real, imag) in enumerate(complex_transform(values, 1.0)):
                    cosine, sine = twiddle[k]
                    if k:
                        real, imag = cosine * real - sine * imag, cosine * imag + sine * real
                    ub[k, 0, u, rows] = real
                    ub[k, 1, u, rows] = imag

            tiles(body)

        @pl.when(z == 0)
        def _():
            def body(u, columns):
                values = [(a3[k, 0, u, rows], a3[k, 1, u, rows]) for k in range(8)]
                even = [(values[0][0], None)] + values[1:4] + [(values[0][1], None)]
                for k, value in enumerate(real_backward(even)):
                    ub[k, 0, u, rows] = value
                for k, value in enumerate(complex_transform(values[4:8], 1.0)):
                    real, imag = turned(value, k / 16)
                    ub[k, 1, u, rows] = 2.0 * real
                    ub[k + 4, 1, u, rows] = -2.0 * imag

            tiles(body)

    def p7_copy(r, d):
        rows = group_rows(r)
        return copy(
            ub.at[(z + d) % NZ, :, :, rows], a4.at[z, :, :, rows],
            p7_send.at[r, d], p7_recv.at[r, d], ring(d), core,
        )

    for r in range(2):
        partners(lambda k: p6_copy(r, k, k).wait_recv())
        ring_backward(r)
        rearranged(ub, r, columns_joined)
        if r:
            each(1, NZ, lambda d: p7_copy(0, d).wait_send())
        ring_order(lambda d: p7_copy(r, d).start())
        a4[z, :, :, group_rows(r)] = ub[z, :, :, group_rows(r)]

    scale_out = [scalar(T_OUT + k) for k in range(NQ)]

    def plane_backward(r):
        rows = group_rows(r)

        def body(u, columns):
            values = [(a4[k, 0, u, rows], a4[k, 1, u, rows]) for k in range(8)]
            values = [(values[0][0], None)] + values[1:] + [(values[0][1], None)]
            for k, value in enumerate(real_backward(values)):
                cb[k, rows, columns] = scale_out[k] * value

        tiles(body)

    def p8_copy(r, d):
        rows = group_rows(r)
        return copy(
            cb.at[(q + d) % NQ, rows], out.at[q, rows],
            p8_send.at[r, d], p8_recv.at[r, d], plane(d), core,
        )

    own_strips = [
        pltpu.make_async_copy(
            cb.at[q, group_rows(r)], out.at[q, group_rows(r)], load_sem.at[4 + r]
        )
        for r in range(2)
    ]
    for r in range(2):
        each(1, NZ, lambda d: p7_copy(r, d).wait_recv())
        plane_backward(r)
        each(1, NQ, lambda d: p8_copy(r, d).start())
        own_strips[r].start()

    for item in edges_out:
        item.wait_send()
    shift_on(w_strips, 1).wait_send()
    shift_back(1).wait_send()

    @pl.when(owner)
    def _():
        each(1, NQ, lambda d: f1_copy(d).wait_send())

    @pl.when(z == NZ - 1)
    def _():
        each(1, NZ, lambda d: f2_copy(d).wait_send())

    for r in range(2):
        each(1, NQ, lambda d: p2_copy(r, d).wait_send())
        spread_sent(r, *f3)
        spread_sent(r, *p4)
    for sent in (p3_copy, p7_copy):
        each(1, NZ, lambda d: sent(1, d).wait_send())
    partners(lambda k: p6_copy(1, k, slot).wait_send())
    halo(fq, fh_send, fh_recv, lambda item: item.wait_send())
    halo(ta, p4h_send, p4h_recv, lambda item: item.wait_send())

    for r in range(2):
        each(1, NQ, lambda d: p8_copy(r, d).wait_recv())
        own_strips[r].wait()
        each(1, NQ, lambda d: p8_copy(r, d).wait_send())


def body(window_state, prior_window, conductivity):
    f32 = jnp.float32
    dma = pltpu.SemaphoreType.DMA
    padded_rows = ROWS + 2 * PAD
    strips = (NQ, STRIP, COLS)
    pairs = (8, 2, STRIP, COLS)
    pairs_apart = (8, 2, 4, STRIP, 128)
    shapes = [
        (ROWS, COLS),
        (padded_rows, COLS),
        (padded_rows, COLS),
        (2, 8, COLS),
        strips,
        strips,
        strips,
        strips,
        pairs,
        pairs,
        pairs_apart,
        strips,
        (STRIP, COLS),
        (1, 4, STRIP, 128),
        (1, 4, SPAN, 128),
        (2, 4, SPAN, 128),
        (2, GROUPS, 8, COLS),
        (2, GROUPS, 8, COLS),
        (2, GROUPS, 8, COLS),
        (2, 4, SPAN, 128),
        (3, GROUPS, 8, COLS),
        (GROUPS, 8, 128),
        pairs_apart,
        pairs_apart,
        pairs_apart,
        strips,
    ]
    sems = [(6,), (2,), (2,), (2, 2), (2, 2), (16,), (1,), (8,), (1,), (2, 8), (2, 8), (2,), (2,)]
    sems += [(2, 16), (2, 16), (2, 8), (2, 8), (2, 8), (2, 8), (2,), (2,)]
    sems += [(2, 8), (2, 8), (2, 8), (2, 8), (2, 16), (2, 16)]
    correction = pl.pallas_call(
        kernel,
        out_shape=jax.ShapeDtypeStruct(strips, f32),
        in_specs=5 * [pl.BlockSpec(memory_space=pl.ANY)],
        out_specs=pl.BlockSpec(memory_space=pl.ANY),
        scratch_shapes=[pltpu.SMEM((1, T_WIDTH), f32)]
        + [pltpu.VMEM(shape, f32) for shape in shapes]
        + [dma(shape) for shape in sems],
        compiler_params=pltpu.CompilerParams(
            collective_id=0, has_side_effects=True, vmem_limit_bytes=60 * 1024 * 1024
        ),
    )(
        jnp.asarray(scalar_table()),
        window_state[0],
        window_state.reshape(strips),
        prior_window.reshape(strips),
        conductivity,
    )
    return window_state + correction.reshape(1, ROWS, COLS)


def solution(mesh):
    in_specs = (P("tm", "space", None), P("tm", "space", None), P("space", None))
    out_specs = P("tm", "space", None)
    return jax.shard_map(body, mesh=mesh, in_specs=in_specs, out_specs=out_specs, check_vma=False)
```

```python
import math

import jax
import jax.numpy as jnp
import numpy as np
from jax import lax
from jax.experimental import pallas as pl
from jax.experimental.pallas import tpu as pltpu
from jax.sharding import PartitionSpec as P

SWEEPS = 24
STEPS = 128
TAU = 2.0
ALPHA = 0.01
HALF = 12.0 * TAU

NQ, NZ = 16, 8
ROWS, COLS = 256, 512
STRIP = 16
BLOCK = 128
HALO = 24
SPAN = BLOCK + 2 * HALO
PAD = 8
GROUP = 8
GROUPS = SPAN // 8
MESH = pl.DeviceIdType.MESH

T_DELTA, T_IN, T_NEXT, T_TWIDDLE, T_OUT, T_WIDTH = 0, 75, 76, 80, 100, 128


def shift_of(frequency):
    beta = math.exp(math.log(ALPHA) / STEPS)
    angle = 2.0 * math.pi * frequency / STEPS
    return 1.0 - beta * math.cos(angle) + 1j * beta * math.sin(angle)


def polynomial_of(frequency):
    points = 64
    theta = (np.arange(points) + 0.5) * np.pi / points
    image_factor = shift_of(frequency) + HALF * (np.cos(theta) + 1.0)
    center = shift_of(frequency) + HALF
    relative = center / HALF
    solution = np.zeros(points, complex)
    remain = np.ones(points, complex)
    search = remain / center
    factor = 1.0 / relative
    for _ in range(SWEEPS):
        solution = solution + search
        remain = remain - image_factor * search
        renewed = 1.0 / (2.0 * relative - factor)
        search = renewed * factor * search + (2.0 * renewed / HALF) * remain
        factor = renewed
    values = solution + search
    first = [2.0 / points * np.sum(values * np.cos(k * theta)) for k in range(SWEEPS + 3)]
    first[0] = first[0] / 2
    second = [(first[k] - first[k + 2]) / 2 for k in range(SWEEPS + 1)]
    second[0] = first[0] - first[2] / 2
    return np.array(second)


def frequency_of(pair, slot):
    if pair:
        return pair + 16 * slot
    return 16 * slot if slot < 4 else 8 + 32 * (slot - 4)


def scalar_table():
    table = np.zeros((STEPS, T_WIDTH))
    for step in range(STEPS):
        plane, ring = step // NZ, step % NZ
        slot = plane % 8
        delta = polynomial_of(frequency_of(ring, slot))
        real, imag, last = delta.real, delta.imag, delta.real
        if ring == 0 and slot == 0:
            imag, last = 0.0 * imag, polynomial_of(64).real
        table[step, 0:75:3], table[step, 1:75:3], table[step, 2:75:3] = real, imag, last
        table[step, T_IN] = math.exp(math.log(ALPHA) * step / STEPS)
        following = (step + 1) % STEPS
        table[step, T_NEXT] = math.exp(math.log(ALPHA) * following / STEPS)
        for k in range(NQ):
            arrival = NZ * k + ring
            table[step, T_OUT + k] = math.exp(-math.log(ALPHA) * arrival / STEPS) / STEPS
        for k in range(NZ + 1):
            angle = 2.0 * math.pi * ring * k / STEPS
            table[step, T_TWIDDLE + 2 * k] = math.cos(angle)
            table[step, T_TWIDDLE + 2 * k + 1] = math.sin(angle)
    return table.astype(np.float32).reshape(STEPS, 1, T_WIDTH)


def turned(value, turn):
    real, imag = value
    turn = turn % 1.0
    if turn == 0.0:
        return value
    if turn == 0.25:
        return ((-imag if imag is not None else None), real)
    if turn == 0.5:
        return (-real, -imag if imag is not None else None)
    if turn == 0.75:
        return (imag, -real)
    cosine, sine = math.cos(2 * math.pi * turn), math.sin(2 * math.pi * turn)
    if imag is None:
        return (cosine * real, sine * real)
    if turn % 0.25 == 0.125:
        scale = math.sqrt(0.5)
        if turn == 0.125:
            return (scale * (real - imag), scale * (real + imag))
        if turn == 0.375:
            return (-scale * (real + imag), scale * (real - imag))
        if turn == 0.625:
            return (scale * (imag - real), -scale * (real + imag))
        return (scale * (real + imag), scale * (imag - real))
    return (cosine * real - sine * imag, sine * real + cosine * imag)


def part_sum(left, right):
    if left is None:
        return right
    return left if right is None else left + right


def part_difference(left, right):
    if right is None:
        return left
    return -right if left is None else left - right


def plus(left, right):
    return (part_sum(left[0], right[0]), part_sum(left[1], right[1]))


def minus(left, right):
    return (part_difference(left[0], right[0]), part_difference(left[1], right[1]))


def conjugate(value):
    return (value[0], None if value[1] is None else -value[1])


def real_forward(values):
    count = len(values)
    if count == 2:
        return [(values[0] + values[1], None), (values[0] - values[1], None)]
    even, odd = real_forward(values[0::2]), real_forward(values[1::2])
    result = [None] * (count // 2 + 1)
    for k in range(count // 4 + 1):
        term = turned(odd[k], -k / count)
        result[k] = plus(even[k], term)
        if k < count // 4:
            result[count // 2 - k] = conjugate(minus(even[k], term))
    return result


def real_backward(values):
    count = 2 * (len(values) - 1)
    if count == 2:
        return [values[0][0] + values[1][0], values[0][0] - values[1][0]]
    even, odd = [], []
    for k in range(count // 4):
        mirror = conjugate(values[count // 2 - k])
        even.append(plus(values[k], mirror))
        odd.append(turned(minus(values[k], mirror), k / count))
    middle = values[count // 4]
    even.append((2.0 * middle[0], None))
    odd.append((-2.0 * middle[1], None))
    result = [None] * count
    result[0::2], result[1::2] = real_backward(even), real_backward(odd)
    return result


def complex_transform(values, sign):
    count = len(values)
    if count == 1:
        return values
    even = complex_transform(values[0::2], sign)
    odd = complex_transform(values[1::2], sign)
    odd = [turned(odd[k], sign * k / count) for k in range(count // 2)]
    return [plus(a, b) for a, b in zip(even, odd)] + [minus(a, b) for a, b in zip(even, odd)]


def conductance(conductivity, values):
    return conductivity * (1.0 + 0.5 * jnp.tanh(values))


def kernel(
    table_in, w, w_strips, prior, cond_in, out,
    table, cond, wp, qp, edge, flux, prev, res, a1, yb, a2, sb, pb, fstrip, fmix, fq,
    ta, ti, tj, xi, xb, wts, west, a3, ub, a4, cb, load_sem,
    edge_send, edge_recv, shift_send, shift_recv,
    f1_send, f1_recv, f2_send, f2_recv, f3_send, f3_recv, fh_send, fh_recv,
    p2_send, p2_recv, p3_send, p3_recv, p4_send, p4_recv, p4h_send, p4h_recv,
    p6_send, p6_recv, p7_send, p7_recv, p8_send, p8_recv,
):
    n = lax.axis_index("tm")
    core = lax.axis_index("space")
    q, z = n // NZ, n % NZ
    half, slot = q // 8, q % 8
    other = 1 - core
    apart = half != core
    owner = n == STEPS - 1

    def scalar(index):
        return table[0, index]

    def plane(distance):
        return ((q + distance) % NQ) * NZ + z

    def ring(distance):
        return q * NZ + (z + distance) % NZ

    def partner(k):
        return (8 * core + k) * NZ + z

    def copy(src, dst, send, recv, step, space):
        return pltpu.make_async_remote_copy(
            src_ref=src, dst_ref=dst, send_sem=send, recv_sem=recv,
            device_id=(step, space), device_id_type=MESH,
        )

    def each(low, high, act):
        def one(d, carry):
            act(d)
            return carry

        lax.fori_loop(low, high, one, 0)

    def ring_order(act):
        def one(i, carry):
            step = (i + 1) // 2
            far = NZ // 2 + jnp.where(i % 2 == 1, -step, step)
            act(far)
            return carry

        lax.fori_loop(0, NZ - 1, one, 0)

    loads = [
        pltpu.make_async_copy(w, wp.at[pl.ds(PAD, ROWS)], load_sem.at[0]),
        pltpu.make_async_copy(cond_in, cond, load_sem.at[1]),
        pltpu.make_async_copy(table_in.at[n], table, load_sem.at[2]),
    ]
    for load in loads:
        load.start()
    prior_load = pltpu.make_async_copy(prior, pb, load_sem.at[3])

    @pl.when(owner)
    def _():
        prior_load.start()

    barrier = pltpu.get_barrier_semaphore()

    def greet(step, space):
        pl.semaphore_signal(barrier, inc=1, device_id=(step, space), device_id_type=MESH)

    greet(n, other)
    before, after = (n + STEPS - 1) % STEPS, (n + 1) % STEPS
    greet(before, core)
    greet(after, core)
    each(1, NQ, lambda d: greet(plane(d), core))
    each(1, NZ, lambda d: greet(ring(d), core))

    @pl.when(apart)
    def _():
        each(0, 8, lambda k: greet(partner(k), half))

    zero_rows = jnp.zeros((8, COLS), jnp.float32)
    for load in loads:
        load.wait()
    qp[PAD : PAD + ROWS] = conductance(cond[...], wp[PAD : PAD + ROWS])
    for ref in (wp, qp):
        ref[0:PAD] = zero_rows
        ref[PAD + ROWS : PAD + ROWS + 8] = zero_rows

    pl.semaphore_wait(barrier, NQ - 1 + NZ - 1 + 3 + jnp.where(apart, 8, 0))

    edge_row = pl.multiple_of((1 - core) * (ROWS - 8), 8)
    edges_out = [
        copy(src.at[pl.ds(edge_row, 8)], edge.at[k], edge_send.at[k], edge_recv.at[k], n, other)
        for k, src in enumerate((w, cond_in))
    ]
    for item in edges_out:
        item.start()

    def group_rows(r):
        return pl.ds(r * GROUP, GROUP)

    def shift_on(src, r):
        return copy(
            src.at[pl.ds(0, 8), group_rows(r)], prev.at[pl.ds(0, 8), group_rows(r)],
            shift_send.at[0, r], shift_recv.at[0, r], after, core,
        )

    def shift_back(r):
        return copy(
            flux.at[pl.ds(8, 8), group_rows(r)], prev.at[pl.ds(8, 8), group_rows(r)],
            shift_send.at[1, r], shift_recv.at[1, r], before, core,
        )

    def shift_on_start(r):
        @pl.when(jnp.logical_not(owner))
        def _():
            shift_on(w_strips, r).start()

        @pl.when(owner)
        def _():
            shift_on(prior, r).start()

    shift_on_start(0)

    def f1_copy(d):
        target = (q + d) % NQ
        return copy(
            prior.at[target], fstrip, f1_send.at[d], f1_recv.at[0], target * NZ + z, core
        )

    def f2_copy(d):
        return copy(fstrip, fstrip, f2_send.at[d], f2_recv.at[0], ring(d), core)

    @pl.when(owner)
    def _():
        each(1, NQ, lambda d: f1_copy(d).start())
        prior_load.wait()
        fstrip[...] = pb[NQ - 1]

    column = lax.broadcasted_iota(jnp.int32, (8, COLS), 1)
    first_column, last_column = column == 0, column == COLS - 1

    def inside_four(window):
        center = window[8:16]
        return (
            window[7:15],
            window[9:17],
            jnp.where(first_column, 0.0, pltpu.roll(center, 1, 1)),
            jnp.where(last_column, 0.0, pltpu.roll(center, COLS - 1, 1)),
        )

    def fluxes(first_strip, r):
        def one(k, carry):
            rows = pl.ds(pl.multiple_of(k * STRIP + r * GROUP, 8), 24)
            state, coeff = wp[rows], qp[rows]
            here, coeff_here = state[8:16], coeff[8:16]
            total = -here
            for near, near_coeff in zip(inside_four(state), inside_four(coeff)):
                total = total + (0.5 * TAU) * (coeff_here + near_coeff) * (near - here)
            flux[k, group_rows(r)] = total
            return carry

        lax.fori_loop(first_strip, first_strip + 8, one, 0, unroll=4)

    fluxes(8, 0)
    shift_back(0).start()
    for item in edges_out:
        item.wait_recv()
    beside = pl.multiple_of((1 - core) * (PAD + ROWS), 8)
    wp[pl.ds(beside, 8)] = edge[0]
    qp[pl.ds(beside, 8)] = conductance(edge[1], edge[0])
    fluxes(8, 1)
    shift_on(w_strips, 0).wait_send()
    shift_on_start(1)
    shift_back(0).wait_send()
    shift_back(1).start()

    fluxes(0, 0)
    fluxes(0, 1)

    @pl.when(z == NZ - 1)
    def _():
        @pl.when(q != NQ - 1)
        def _():
            f1_copy(1).wait_recv()

        each(1, NZ, lambda d: f2_copy(d).start())

    def p2_copy(r, d):
        target = (q + d) % NQ
        return copy(
            res.at[target, group_rows(r)], a1.at[q, group_rows(r)],
            p2_send.at[r, d], p2_recv.at[r, d], target * NZ + z, core,
        )

    damping, damping_next = scalar(T_IN), scalar(T_NEXT)

    def residuals(r):
        rows = group_rows(r)

        def on(k, carry):
            res[k, rows] = (prev[k, rows] + flux[k, rows]) * damping
            return carry

        def back(k, carry):
            own = wp[pl.ds(pl.multiple_of(PAD + k * STRIP + r * GROUP, 8), GROUP)]
            res[k, rows] = (own + prev[k, rows]) * damping_next
            return carry

        def back_first(k, carry):
            res[k, rows] = (pb[k, rows] + prev[k, rows]) * damping_next
            return carry

        shift_back(r).wait_recv()

        @pl.when(jnp.logical_not(owner))
        def _():
            lax.fori_loop(8, 16, back, 0, unroll=4)

        @pl.when(owner)
        def _():
            lax.fori_loop(8, 16, back_first, 0, unroll=4)

        shift_on(w_strips, r).wait_recv()
        lax.fori_loop(0, 8, on, 0, unroll=4)
        each(1, NQ, lambda d: p2_copy(r, d).start())
        a1[q, rows] = res[q, rows]

    residuals(0)
    residuals(1)

    def tiles(body):
        def one(u, carry):
            body(u, pl.ds(pl.multiple_of(u * 128, 128), 128))
            return carry

        lax.fori_loop(0, 4, one, 0, unroll=2)

    def plane_forward(r):
        rows = group_rows(r)

        def body(u, columns):
            result = real_forward([a1[k, rows, columns] for k in range(NQ)])
            yb[0, 0, rows, columns] = result[0][0]
            yb[0, 1, rows, columns] = result[8][0]
            for k in range(1, 8):
                yb[k, 0, rows, columns] = result[k][0]
                yb[k, 1, rows, columns] = result[k][1]

        tiles(body)

    def p3_copy(r, d):
        rows = group_rows(r)
        return copy(
            yb.at[(z + d) % NZ, :, rows], a2.at[z, :, rows],
            p3_send.at[r, d], p3_recv.at[r, d], ring(d), core,
        )


    lane = lax.broadcasted_iota(jnp.int32, (8, 128), 1)
    sublane = lax.broadcasted_iota(jnp.int32, (8, 128), 0)

    def one_of(parts, choice):
        low = jnp.where(choice == 0, parts[0], parts[1])
        return jnp.where(choice < 2, low, jnp.where(choice == 2, parts[2], parts[3]))

    def moved(part, index):
        return jnp.take_along_axis(part, index, axis=1)

    within, block = lane % 4, lane // 32

    def columns_spread(parts):
        mixed = [one_of(parts, (within + s) % 4) for s in range(4)]
        mixed = [moved(mixed[s], 4 * (lane % 32) + (block - s) % 4) for s in range(4)]
        return [one_of(mixed, (block - u) % 4) for u in range(4)]

    def columns_joined(parts):
        mixed = [one_of(parts, (block - s) % 4) for s in range(4)]
        mixed = [moved(mixed[s], 32 * ((within + s) % 4) + lane // 4) for s in range(4)]
        return [one_of(mixed, (u - within) % 4) for u in range(4)]

    def quarters(value):
        return [value[:, u * 128 : (u + 1) * 128] for u in range(4)]

    def rearranged(ref, r, change):
        rows = group_rows(r)

        def one(t, carry):
            for field in range(2):
                parts = change([ref[t, field, u, rows] for u in range(4)])
                for u, part in enumerate(parts):
                    ref[t, field, u, rows] = part
            return carry

        lax.fori_loop(0, 8, one, 0, unroll=4)

    def partners(act):
        each(1, 8, lambda d: act((slot + d) % 8))

        @pl.when(apart)
        def _():
            act(slot)

    def main_copy(r, src, dst, send, recv, k):
        rows = pl.ds(pl.multiple_of(HALO + slot * STRIP + r * GROUP, 8), GROUP)
        return copy(
            src(k).at[:, :, group_rows(r)], dst.at[:, :, rows],
            send.at[r, k], recv.at[r, slot], partner(k), half,
        )

    def main_arriving(r, src, dst, send, recv, k):
        rows = pl.ds(pl.multiple_of(HALO + slot * STRIP + r * GROUP, 8), GROUP)
        return copy(
            src(k).at[:, :, group_rows(r)], dst.at[:, :, rows],
            send.at[r, k], recv.at[r, k], partner(k), half,
        )

    def spread_start(r, src, dst, send, recv):
        partners(lambda k: main_copy(r, src, dst, send, recv, k).start())

        @pl.when(jnp.logical_not(apart))
        def _():
            own = pl.ds(pl.multiple_of(HALO + slot * STRIP + r * GROUP, 8), GROUP)
            dst[:, :, own] = src(slot)[:, :, group_rows(r)]

    def spread_arrived(r, src, dst, send, recv):
        partners(lambda k: main_arriving(r, src, dst, send, recv, k).wait_recv())

    def spread_sent(r, src, dst, send, recv):
        partners(lambda k: main_copy(r, src, dst, send, recv, k).wait_send())

    facing = (8 * (1 - half) + slot) * NZ + z
    down = HALO + BLOCK - HALO

    def halo_copy(field, send, recv, far):
        goes_down = (core == 1) if far else (core == 0)
        first = pl.multiple_of(jnp.where(goes_down, down, HALO), 8)
        into = pl.multiple_of(jnp.where(goes_down, 0, HALO + BLOCK), 8)
        index = 1 if far else 0
        return copy(
            field.at[:, :, pl.ds(first, HALO)], field.at[:, :, pl.ds(into, HALO)],
            send.at[index], recv.at[index], facing if far else n, other,
        )

    def halo(field, send, recv, act):
        act(halo_copy(field, send, recv, False))

        @pl.when(apart)
        def _():
            act(halo_copy(field, send, recv, True))

    @pl.when(jnp.logical_not(apart))
    def _():
        outer = pl.ds(pl.multiple_of(core * (HALO + BLOCK), 8), HALO)
        fq[:, :, outer] = jnp.zeros((1, 4, HALO, 128), jnp.float32)
        ta[:, :, outer] = jnp.zeros((2, 4, HALO, 128), jnp.float32)

    def plane_to_ring(r):
        each(1, NQ, lambda d: p2_copy(r, d).wait_recv())
        plane_forward(r)
        if r:
            each(1, NZ, lambda d: p3_copy(0, d).wait_send())
        ring_order(lambda d: p3_copy(r, d).start())
        a2[z, :, group_rows(r)] = yb[z, :, group_rows(r)]

    plane_to_ring(0)

    @pl.when(z != NZ - 1)
    def _():
        f2_copy(1).wait_recv()

    for row in (0, 8):
        own = cond[pl.ds(pl.multiple_of(q * STRIP + row, 8), 8)]
        frozen = conductance(own, fstrip[row : row + 8])
        for u, part in enumerate(columns_spread(quarters(frozen))):
            fmix[0, u, row : row + 8] = part

    f3 = (lambda k: fmix, fq, f3_send, f3_recv)
    for r in range(2):
        spread_start(r, *f3)

    plane_to_ring(1)
    for r in range(2):
        spread_arrived(r, *f3)
    halo(fq, fh_send, fh_recv, lambda item: item.start())

    twiddle = [(scalar(T_TWIDDLE + 2 * k), scalar(T_TWIDDLE + 2 * k + 1)) for k in range(NZ)]
    start = 2 * NZ * half
    twiddle_first = (scalar(T_TWIDDLE + start), scalar(T_TWIDDLE + start + 1))
    sign = jnp.where(half == 1, -1.0, 1.0)

    def source(k):
        return (k + NZ - half) % NZ

    def ring_forward(r):
        rows = group_rows(r)

        @pl.when(z != 0)
        def _():
            def body(u, columns):
                values = []
                for k in range(NZ):
                    real, imag = a2[source(k), 0, rows, columns], a2[source(k), 1, rows, columns]
                    cosine, sine = twiddle[k] if k else twiddle_first
                    values.append((cosine * real + sine * imag, cosine * imag - sine * real))
                for k, value in enumerate(complex_transform(values, -1.0)):
                    sb[k, 0, u, rows] = value[0]
                    sb[k, 1, u, rows] = value[1]

            tiles(body)

        @pl.when(z == 0)
        def _():
            def body(u, columns):
                even = real_forward([a2[source(k), 0, rows, columns] for k in range(NZ)])
                sb[0, 0, u, rows] = even[0][0]
                sb[0, 1, u, rows] = even[4][0]
                values = [a2[source(k), 1, rows, columns] for k in range(NZ)]
                values[0] = sign * values[0]
                odd = [turned((values[k], -values[k + 4]), -k / 16) for k in range(4)]
                odd = complex_transform(odd, -1.0)
                for k, value in list(zip((1, 2, 3), even[1:4])) + list(zip((4, 5, 6, 7), odd)):
                    sb[k, 0, u, rows] = value[0]
                    sb[k, 1, u, rows] = value[1]

            tiles(body)

    p4 = (lambda k: sb.at[k], ta, p4_send, p4_recv)
    for r in range(2):
        each(1, NZ, lambda d: p3_copy(r, d).wait_recv())
        ring_forward(r)
        rearranged(sb, r, columns_spread)
        spread_start(r, *p4)
    halo(fq, fh_send, fh_recv, lambda item: item.wait_recv())
    top = half * ROWS + core * BLOCK - HALO
    scale = TAU / HALF

    def spaced(ref, field, t):
        rows = pl.ds(t, 8, stride=GROUPS)
        return [ref[field, u, rows] for u in range(4)]

    def weights(t, here, below):
        row = GROUPS * sublane + t
        closed = (row == SPAN - 1) | (row + top == 2 * ROWS - 1) | (row + top == -1)
        rim = (row + top == 0) | (row + top == 2 * ROWS - 1)
        before = pltpu.roll(here[3], 1, 1)
        beyond = [here[1], here[2], here[3], pltpu.roll(here[0], 127, 1)]
        west[t] = jnp.where(lane == 0, 0.0, scale * (here[0] + before))
        for u in range(4):
            columns = slice(u * 128, (u + 1) * 128)
            wts[0, t, :, columns] = jnp.where(closed, 0.0, scale * (here[u] + below[u]))
            east = scale * (here[u] + beyond[u])
            center = jnp.where(rim, scale * here[u], 0.0) - 2.0
            if u == 0:
                center = center + jnp.where(lane == 0, scale * here[u], 0.0)
            if u == 3:
                center = center + jnp.where(lane == 127, scale * here[u], 0.0)
                east = jnp.where(lane == 127, 0.0, east)
            wts[1, t, :, columns] = east
            wts[2, t, :, columns] = center

    def weight_rows(t, carry):
        weights(t, spaced(fq, 0, t), spaced(fq, 0, t + 1))
        return carry

    lax.fori_loop(0, GROUPS - 1, weight_rows, 0, unroll=3)
    weights(
        GROUPS - 1,
        spaced(fq, 0, GROUPS - 1),
        [pltpu.roll(part, 7, 0) for part in spaced(fq, 0, 0)],
    )
    tj[...] = jnp.zeros(tj.shape, jnp.float32)
    for r in range(2):
        spread_arrived(r, *p4)
    halo(ta, p4h_send, p4h_recv, lambda item: item.start())
    halo(ta, p4h_send, p4h_recv, lambda item: item.wait_recv())


    first = [scalar(T_DELTA + k) for k in range(3)]

    def begin(t, carry):
        real, imag = spaced(ta, 0, t), spaced(ta, 1, t)
        for u in range(4):
            columns = slice(u * 128, (u + 1) * 128)
            ti[0, t, :, columns] = real[u]
            ti[1, t, :, columns] = imag[u]
            xi[0, t, :, columns] = first[0] * real[u] - first[1] * imag[u]
            xi[1, t, :, columns] = first[1] * real[u] + first[2] * imag[u]
        return carry

    lax.fori_loop(0, GROUPS, begin, 0, unroll=11)

    def swept_row(now, old, t, here, below, flux_above, factors):
        south, east, center = (quarters(wts[k, t]) for k in range(3))
        west_weight = west[t]
        fresh, flux_below = [], []
        for field in range(2):
            v = here[field]
            before, beyond = pltpu.roll(v[3], 1, 1), pltpu.roll(v[0], 127, 1)
            eastward = [east[u] * ((v[u + 1] if u < 3 else beyond) - v[u]) for u in range(4)]
            westward = [west_weight * (v[0] - before)] + eastward[:3]
            downward = [south[u] * (below[field][u] - v[u]) for u in range(4)]
            result = []
            for u in range(4):
                columns = slice(u * 128, (u + 1) * 128)
                value = (center[u] * v[u] - old[field, t, :, columns]) + (
                    (flux_above[field][u] - downward[u]) + (westward[u] - eastward[u])
                )
                old[field, t, :, columns] = value
                result.append(value)
            fresh.append(result)
            flux_below.append(downward)
        if factors is not None:
            for u in range(4):
                columns = slice(u * 128, (u + 1) * 128)
                real, imag = here[0][u], here[1][u]
                xi[0, t, :, columns] = xi[0, t, :, columns] + (
                    (factors[0] * real - factors[1] * imag)
                    + (factors[3] * fresh[0][u] - factors[4] * fresh[1][u])
                )
                xi[1, t, :, columns] = xi[1, t, :, columns] + (
                    (factors[1] * real + factors[2] * imag)
                    + (factors[4] * fresh[0][u] + factors[5] * fresh[1][u])
                )
        return flux_below

    def sweep(now, old, factors):
        begin_rows = [quarters(now[field, 0]) for field in range(2)]
        wrapped = [[pltpu.roll(part, 7, 0) for part in begin_rows[field]] for field in range(2)]
        end_rows = [quarters(now[field, GROUPS - 1]) for field in range(2)]
        end_south = quarters(wts[0, GROUPS - 1])
        flux_above = [
            [
                pltpu.roll(end_south[u] * (wrapped[field][u] - end_rows[field][u]), 1, 0)
                for u in range(4)
            ]
            for field in range(2)
        ]

        def one(t, carried):
            here, above = carried
            below = [quarters(now[field, t + 1]) for field in range(2)]
            return below, swept_row(now, old, t, here, below, above, factors)

        here, above = lax.fori_loop(
            0, GROUPS - 1, one, (begin_rows, flux_above), unroll=GROUPS - 1
        )
        swept_row(now, old, GROUPS - 1, here, wrapped, above, factors)

    def two_sweeps(m, carry):
        k = 2 * m + 1
        factors = [scalar(T_DELTA + 3 * k + each) for each in range(6)]
        sweep(ti, tj, None)
        sweep(tj, ti, factors)
        return carry

    lax.fori_loop(0, SWEEPS // 2, two_sweeps, 0)

    def finish(t, carry):
        for field in range(2):
            for u in range(4):
                columns = slice(u * 128, (u + 1) * 128)
                xb[field, u, pl.ds(t, 8, stride=GROUPS)] = xi[field, t, :, columns]
        return carry

    lax.fori_loop(0, GROUPS, finish, 0, unroll=11)

    def p6_copy(r, k, index):
        rows = pl.ds(pl.multiple_of(HALO + k * STRIP + r * GROUP, 8), GROUP)
        return copy(
            xb.at[:, :, rows], a3.at[slot, :, :, group_rows(r)],
            p6_send.at[r, k], p6_recv.at[r, index], partner(k), half,
        )

    for r in range(2):
        if r:
            partners(lambda k: p6_copy(0, k, slot).wait_send())
        partners(lambda k: p6_copy(r, k, slot).start())

        @pl.when(jnp.logical_not(apart))
        def _():
            own = pl.ds(pl.multiple_of(HALO + slot * STRIP + r * GROUP, 8), GROUP)
            a3[slot, :, :, group_rows(r)] = xb[:, :, own]

    def ring_backward(r):
        rows = group_rows(r)

        @pl.when(z != 0)
        def _():
            def body(u, columns):
                values = [(a3[k, 0, u, rows], a3[k, 1, u, rows]) for k in range(8)]
                for k, (real, imag) in enumerate(complex_transform(values, 1.0)):
                    cosine, sine = twiddle[k]
                    if k:
                        real, imag = cosine * real - sine * imag, cosine * imag + sine * real
                    ub[k, 0, u, rows] = real
                    ub[k, 1, u, rows] = imag

            tiles(body)

        @pl.when(z == 0)
        def _():
            def body(u, columns):
                values = [(a3[k, 0, u, rows], a3[k, 1, u, rows]) for k in range(8)]
                even = [(values[0][0], None)] + values[1:4] + [(values[0][1], None)]
                for k, value in enumerate(real_backward(even)):
                    ub[k, 0, u, rows] = value
                for k, value in enumerate(complex_transform(values[4:8], 1.0)):
                    real, imag = turned(value, k / 16)
                    ub[k, 1, u, rows] = 2.0 * real
                    ub[k + 4, 1, u, rows] = -2.0 * imag

            tiles(body)

    def p7_copy(r, d):
        rows = group_rows(r)
        return copy(
            ub.at[(z + d) % NZ, :, :, rows], a4.at[z, :, :, rows],
            p7_send.at[r, d], p7_recv.at[r, d], ring(d), core,
        )

    for r in range(2):
        partners(lambda k: p6_copy(r, k, k).wait_recv())
        ring_backward(r)
        rearranged(ub, r, columns_joined)
        if r:
            each(1, NZ, lambda d: p7_copy(0, d).wait_send())
        ring_order(lambda d: p7_copy(r, d).start())
        a4[z, :, :, group_rows(r)] = ub[z, :, :, group_rows(r)]

    scale_out = [scalar(T_OUT + k) for k in range(NQ)]

    def plane_backward(r):
        rows = group_rows(r)

        def body(u, columns):
            values = [(a4[k, 0, u, rows], a4[k, 1, u, rows]) for k in range(8)]
            values = [(values[0][0], None)] + values[1:] + [(values[0][1], None)]
            for k, value in enumerate(real_backward(values)):
                cb[k, rows, columns] = scale_out[k] * value

        tiles(body)

    def p8_copy(r, d):
        rows = group_rows(r)
        return copy(
            cb.at[(q + d) % NQ, rows], out.at[q, rows],
            p8_send.at[r, d], p8_recv.at[r, d], plane(d), core,
        )

    own_strips = [
        pltpu.make_async_copy(
            cb.at[q, group_rows(r)], out.at[q, group_rows(r)], load_sem.at[4 + r]
        )
        for r in range(2)
    ]
    for r in range(2):
        each(1, NZ, lambda d: p7_copy(r, d).wait_recv())
        plane_backward(r)
        each(1, NQ, lambda d: p8_copy(r, d).start())
        own_strips[r].start()

    for item in edges_out:
        item.wait_send()
    shift_on(w_strips, 1).wait_send()
    shift_back(1).wait_send()

    @pl.when(owner)
    def _():
        each(1, NQ, lambda d: f1_copy(d).wait_send())

    @pl.when(z == NZ - 1)
    def _():
        each(1, NZ, lambda d: f2_copy(d).wait_send())

    for r in range(2):
        each(1, NQ, lambda d: p2_copy(r, d).wait_send())
        spread_sent(r, *f3)
        spread_sent(r, *p4)
    for sent in (p3_copy, p7_copy):
        each(1, NZ, lambda d: sent(1, d).wait_send())
    partners(lambda k: p6_copy(1, k, slot).wait_send())
    halo(fq, fh_send, fh_recv, lambda item: item.wait_send())
    halo(ta, p4h_send, p4h_recv, lambda item: item.wait_send())

    for r in range(2):
        each(1, NQ, lambda d: p8_copy(r, d).wait_recv())
        own_strips[r].wait()
        each(1, NQ, lambda d: p8_copy(r, d).wait_send())


def body(window_state, prior_window, conductivity):
    f32 = jnp.float32
    dma = pltpu.SemaphoreType.DMA
    padded_rows = ROWS + 2 * PAD
    strips = (NQ, STRIP, COLS)
    pairs = (8, 2, STRIP, COLS)
    pairs_apart = (8, 2, 4, STRIP, 128)
    shapes = [
        (ROWS, COLS),
        (padded_rows, COLS),
        (padded_rows, COLS),
        (2, 8, COLS),
        strips,
        strips,
        strips,
        strips,
        pairs,
        pairs,
        pairs_apart,
        strips,
        (STRIP, COLS),
        (1, 4, STRIP, 128),
        (1, 4, SPAN, 128),
        (2, 4, SPAN, 128),
        (2, GROUPS, 8, COLS),
        (2, GROUPS, 8, COLS),
        (2, GROUPS, 8, COLS),
        (2, 4, SPAN, 128),
        (3, GROUPS, 8, COLS),
        (GROUPS, 8, 128),
        pairs_apart,
        pairs_apart,
        pairs_apart,
        strips,
    ]
    sems = [(6,), (2,), (2,), (2, 2), (2, 2), (16,), (1,), (8,), (1,), (2, 8), (2, 8), (2,), (2,)]
    sems += [(2, 16), (2, 16), (2, 8), (2, 8), (2, 8), (2, 8), (2,), (2,)]
    sems += [(2, 8), (2, 8), (2, 8), (2, 8), (2, 16), (2, 16)]
    correction = pl.pallas_call(
        kernel,
        out_shape=jax.ShapeDtypeStruct(strips, f32),
        in_specs=5 * [pl.BlockSpec(memory_space=pl.ANY)],
        out_specs=pl.BlockSpec(memory_space=pl.ANY),
        scratch_shapes=[pltpu.SMEM((1, T_WIDTH), f32)]
        + [pltpu.VMEM(shape, f32) for shape in shapes]
        + [dma(shape) for shape in sems],
        compiler_params=pltpu.CompilerParams(
            collective_id=0, has_side_effects=True, vmem_limit_bytes=60 * 1024 * 1024
        ),
    )(
        jnp.asarray(scalar_table()),
        window_state[0],
        window_state.reshape(strips),
        prior_window.reshape(strips),
        conductivity,
    )
    return window_state + correction.reshape(1, ROWS, COLS)


def solution(mesh):
    in_specs = (P("tm", "space", None), P("tm", "space", None), P("space", None))
    out_specs = P("tm", "space", None)
    return jax.shard_map(body, mesh=mesh, in_specs=in_specs, out_specs=out_specs, check_vma=False)
```

```python
import math

import jax
import jax.numpy as jnp
import numpy as np
from jax import lax
from jax.experimental import pallas as pl
from jax.experimental.pallas import tpu as pltpu
from jax.sharding import PartitionSpec as P

SWEEPS = 24
STEPS = 128
TAU = 2.0
ALPHA = 0.01
HALF = 12.0 * TAU

NQ, NZ = 16, 8
ROWS, COLS = 256, 512
STRIP = 16
BLOCK = 128
HALO = 24
SPAN = BLOCK + 2 * HALO
PAD = 8
GROUP = 8
GROUPS = SPAN // 8
MESH = pl.DeviceIdType.MESH

T_DELTA, T_IN, T_NEXT, T_TWIDDLE, T_OUT, T_WIDTH = 0, 75, 76, 80, 100, 128


def shift_of(frequency):
    beta = math.exp(math.log(ALPHA) / STEPS)
    angle = 2.0 * math.pi * frequency / STEPS
    return 1.0 - beta * math.cos(angle) + 1j * beta * math.sin(angle)


def polynomial_of(frequency):
    points = 64
    theta = (np.arange(points) + 0.5) * np.pi / points
    image_factor = shift_of(frequency) + HALF * (np.cos(theta) + 1.0)
    center = shift_of(frequency) + HALF
    relative = center / HALF
    solution = np.zeros(points, complex)
    remain = np.ones(points, complex)
    search = remain / center
    factor = 1.0 / relative
    for _ in range(SWEEPS):
        solution = solution + search
        remain = remain - image_factor * search
        renewed = 1.0 / (2.0 * relative - factor)
        search = renewed * factor * search + (2.0 * renewed / HALF) * remain
        factor = renewed
    values = solution + search
    first = [2.0 / points * np.sum(values * np.cos(k * theta)) for k in range(SWEEPS + 3)]
    first[0] = first[0] / 2
    second = [(first[k] - first[k + 2]) / 2 for k in range(SWEEPS + 1)]
    second[0] = first[0] - first[2] / 2
    return np.array(second)


def frequency_of(pair, slot):
    if pair:
        return pair + 16 * slot
    return 16 * slot if slot < 4 else 8 + 32 * (slot - 4)


def scalar_table():
    table = np.zeros((STEPS, T_WIDTH))
    for step in range(STEPS):
        plane, ring = step // NZ, step % NZ
        slot = plane % 8
        delta = polynomial_of(frequency_of(ring, slot))
        real, imag, last = delta.real, delta.imag, delta.real
        if ring == 0 and slot == 0:
            imag, last = 0.0 * imag, polynomial_of(64).real
        table[step, 0:75:3], table[step, 1:75:3], table[step, 2:75:3] = real, imag, last
        table[step, T_IN] = math.exp(math.log(ALPHA) * step / STEPS)
        following = (step + 1) % STEPS
        table[step, T_NEXT] = math.exp(math.log(ALPHA) * following / STEPS)
        for k in range(NQ):
            arrival = NZ * k + ring
            table[step, T_OUT + k] = math.exp(-math.log(ALPHA) * arrival / STEPS) / STEPS
        for k in range(NZ + 1):
            angle = 2.0 * math.pi * ring * k / STEPS
            table[step, T_TWIDDLE + 2 * k] = math.cos(angle)
            table[step, T_TWIDDLE + 2 * k + 1] = math.sin(angle)
    return table.astype(np.float32).reshape(STEPS, 1, T_WIDTH)


def turned(value, turn):
    real, imag = value
    turn = turn % 1.0
    if turn == 0.0:
        return value
    if turn == 0.25:
        return ((-imag if imag is not None else None), real)
    if turn == 0.5:
        return (-real, -imag if imag is not None else None)
    if turn == 0.75:
        return (imag, -real)
    cosine, sine = math.cos(2 * math.pi * turn), math.sin(2 * math.pi * turn)
    if imag is None:
        return (cosine * real, sine * real)
    if turn % 0.25 == 0.125:
        scale = math.sqrt(0.5)
        if turn == 0.125:
            return (scale * (real - imag), scale * (real + imag))
        if turn == 0.375:
            return (-scale * (real + imag), scale * (real - imag))
        if turn == 0.625:
            return (scale * (imag - real), -scale * (real + imag))
        return (scale * (real + imag), scale * (imag - real))
    return (cosine * real - sine * imag, sine * real + cosine * imag)


def part_sum(left, right):
    if left is None:
        return right
    return left if right is None else left + right


def part_difference(left, right):
    if right is None:
        return left
    return -right if left is None else left - right


def plus(left, right):
    return (part_sum(left[0], right[0]), part_sum(left[1], right[1]))


def minus(left, right):
    return (part_difference(left[0], right[0]), part_difference(left[1], right[1]))


def conjugate(value):
    return (value[0], None if value[1] is None else -value[1])


def real_forward(values):
    count = len(values)
    if count == 2:
        return [(values[0] + values[1], None), (values[0] - values[1], None)]
    even, odd = real_forward(values[0::2]), real_forward(values[1::2])
    result = [None] * (count // 2 + 1)
    for k in range(count // 4 + 1):
        term = turned(odd[k], -k / count)
        result[k] = plus(even[k], term)
        if k < count // 4:
            result[count // 2 - k] = conjugate(minus(even[k], term))
    return result


def real_backward(values):
    count = 2 * (len(values) - 1)
    if count == 2:
        return [values[0][0] + values[1][0], values[0][0] - values[1][0]]
    even, odd = [], []
    for k in range(count // 4):
        mirror = conjugate(values[count // 2 - k])
        even.append(plus(values[k], mirror))
        odd.append(turned(minus(values[k], mirror), k / count))
    middle = values[count // 4]
    even.append((2.0 * middle[0], None))
    odd.append((-2.0 * middle[1], None))
    result = [None] * count
    result[0::2], result[1::2] = real_backward(even), real_backward(odd)
    return result


def complex_transform(values, sign):
    count = len(values)
    if count == 1:
        return values
    even = complex_transform(values[0::2], sign)
    odd = complex_transform(values[1::2], sign)
    odd = [turned(odd[k], sign * k / count) for k in range(count // 2)]
    return [plus(a, b) for a, b in zip(even, odd)] + [minus(a, b) for a, b in zip(even, odd)]


def conductance(conductivity, values):
    return conductivity * (1.0 + 0.5 * jnp.tanh(values))


def kernel(
    table_in, w, w_strips, prior, cond_in, out,
    table, cond, wp, qp, edge, flux, prev, res, a1, yb, a2, sb, pb, fstrip, fmix, fq,
    ta, ti, tj, xi, xb, wts, west, a3, ub, a4, cb, load_sem,
    edge_send, edge_recv, shift_send, shift_recv,
    f1_send, f1_recv, f2_send, f2_recv, f3_send, f3_recv, fh_send, fh_recv,
    p2_send, p2_recv, p3_send, p3_recv, p4_send, p4_recv, p4h_send, p4h_recv,
    p6_send, p6_recv, p7_send, p7_recv, p8_send, p8_recv,
):
    n = lax.axis_index("tm")
    core = lax.axis_index("space")
    q, z = n // NZ, n % NZ
    half, slot = q // 8, q % 8
    other = 1 - core
    apart = half != core
    owner = n == STEPS - 1

    def scalar(index):
        return table[0, index]

    def plane_of(d):
        return ((q // 4 + d // 4) % 4) * 4 + (q + d) % 4

    def plane(d):
        return plane_of(d) * NZ + z

    def ring(distance):
        return q * NZ + (z + distance) % NZ

    def partner(k):
        return (8 * core + k) * NZ + z

    def copy(src, dst, send, recv, step, space):
        return pltpu.make_async_remote_copy(
            src_ref=src, dst_ref=dst, send_sem=send, recv_sem=recv,
            device_id=(step, space), device_id_type=MESH,
        )

    def each(low, high, act):
        def one(d, carry):
            act(d)
            return carry

        lax.fori_loop(low, high, one, 0)

    def ring_order(act):
        def one(i, carry):
            step = (i + 1) // 2
            far = NZ // 2 + jnp.where(i % 2 == 1, -step, step)
            act(far)
            return carry

        lax.fori_loop(0, NZ - 1, one, 0)

    def plane_order(act):
        for d in (10, 9, 11, 6, 14, 2, 8, 5, 15, 7, 13, 1, 3, 4, 12):
            act(d)

    loads = [
        pltpu.make_async_copy(w, wp.at[pl.ds(PAD, ROWS)], load_sem.at[0]),
        pltpu.make_async_copy(cond_in, cond, load_sem.at[1]),
        pltpu.make_async_copy(table_in.at[n], table, load_sem.at[2]),
    ]
    for load in loads:
        load.start()
    prior_load = pltpu.make_async_copy(prior, pb, load_sem.at[3])

    @pl.when(owner)
    def _():
        prior_load.start()

    barrier = pltpu.get_barrier_semaphore()

    def greet(step, space):
        pl.semaphore_signal(barrier, inc=1, device_id=(step, space), device_id_type=MESH)

    greet(n, other)
    before, after = (n + STEPS - 1) % STEPS, (n + 1) % STEPS
    greet(before, core)
    greet(after, core)
    each(1, NQ, lambda d: greet(plane(d), core))
    each(1, NZ, lambda d: greet(ring(d), core))

    @pl.when(apart)
    def _():
        each(0, 8, lambda k: greet(partner(k), half))

    zero_rows = jnp.zeros((8, COLS), jnp.float32)
    for load in loads:
        load.wait()
    qp[PAD : PAD + ROWS] = conductance(cond[...], wp[PAD : PAD + ROWS])
    for ref in (wp, qp):
        ref[0:PAD] = zero_rows
        ref[PAD + ROWS : PAD + ROWS + 8] = zero_rows

    pl.semaphore_wait(barrier, NQ - 1 + NZ - 1 + 3 + jnp.where(apart, 8, 0))

    edge_row = pl.multiple_of((1 - core) * (ROWS - 8), 8)
    edges_out = [
        copy(src.at[pl.ds(edge_row, 8)], edge.at[k], edge_send.at[k], edge_recv.at[k], n, other)
        for k, src in enumerate((w, cond_in))
    ]
    for item in edges_out:
        item.start()

    def group_rows(r):
        return pl.ds(r * GROUP, GROUP)

    def shift_on(src, r):
        return copy(
            src.at[pl.ds(0, 8), group_rows(r)], prev.at[pl.ds(0, 8), group_rows(r)],
            shift_send.at[0, r], shift_recv.at[0, r], after, core,
        )

    def shift_back(r):
        return copy(
            flux.at[pl.ds(8, 8), group_rows(r)], prev.at[pl.ds(8, 8), group_rows(r)],
            shift_send.at[1, r], shift_recv.at[1, r], before, core,
        )

    def shift_on_start(r):
        @pl.when(jnp.logical_not(owner))
        def _():
            shift_on(w_strips, r).start()

        @pl.when(owner)
        def _():
            shift_on(prior, r).start()

    shift_on_start(0)

    def f1_copy(d):
        target = plane_of(d)
        return copy(
            prior.at[target], fstrip, f1_send.at[d], f1_recv.at[0], target * NZ + z, core
        )

    def f2_copy(d):
        return copy(fstrip, fstrip, f2_send.at[d], f2_recv.at[0], ring(d), core)

    @pl.when(owner)
    def _():
        each(1, NQ, lambda d: f1_copy(d).start())
        prior_load.wait()
        fstrip[...] = pb[NQ - 1]

    column = lax.broadcasted_iota(jnp.int32, (8, COLS), 1)
    first_column, last_column = column == 0, column == COLS - 1

    def inside_four(window):
        center = window[8:16]
        return (
            window[7:15],
            window[9:17],
            jnp.where(first_column, 0.0, pltpu.roll(center, 1, 1)),
            jnp.where(last_column, 0.0, pltpu.roll(center, COLS - 1, 1)),
        )

    def fluxes(first_strip, r):
        def one(k, carry):
            rows = pl.ds(pl.multiple_of(k * STRIP + r * GROUP, 8), 24)
            state, coeff = wp[rows], qp[rows]
            here, coeff_here = state[8:16], coeff[8:16]
            total = -here
            for near, near_coeff in zip(inside_four(state), inside_four(coeff)):
                total = total + (0.5 * TAU) * (coeff_here + near_coeff) * (near - here)
            flux[k, group_rows(r)] = total
            return carry

        lax.fori_loop(first_strip, first_strip + 8, one, 0, unroll=4)

    fluxes(8, 0)
    shift_back(0).start()
    for item in edges_out:
        item.wait_recv()
    beside = pl.multiple_of((1 - core) * (PAD + ROWS), 8)
    wp[pl.ds(beside, 8)] = edge[0]
    qp[pl.ds(beside, 8)] = conductance(edge[1], edge[0])
    fluxes(8, 1)
    shift_on(w_strips, 0).wait_send()
    shift_on_start(1)
    shift_back(0).wait_send()
    shift_back(1).start()

    fluxes(0, 0)
    fluxes(0, 1)

    @pl.when(z == NZ - 1)
    def _():
        @pl.when(q != NQ - 1)
        def _():
            f1_copy(1).wait_recv()

        each(1, NZ, lambda d: f2_copy(d).start())

    def p2_copy(r, d):
        target = plane_of(d)
        return copy(
            res.at[target, group_rows(r)], a1.at[q, group_rows(r)],
            p2_send.at[r, d], p2_recv.at[r, d], target * NZ + z, core,
        )

    damping, damping_next = scalar(T_IN), scalar(T_NEXT)

    def residuals(r):
        rows = group_rows(r)

        def on(k, carry):
            res[k, rows] = (prev[k, rows] + flux[k, rows]) * damping
            return carry

        def back(k, carry):
            own = wp[pl.ds(pl.multiple_of(PAD + k * STRIP + r * GROUP, 8), GROUP)]
            res[k, rows] = (own + prev[k, rows]) * damping_next
            return carry

        def back_first(k, carry):
            res[k, rows] = (pb[k, rows] + prev[k, rows]) * damping_next
            return carry

        shift_back(r).wait_recv()

        @pl.when(jnp.logical_not(owner))
        def _():
            lax.fori_loop(8, 16, back, 0, unroll=4)

        @pl.when(owner)
        def _():
            lax.fori_loop(8, 16, back_first, 0, unroll=4)

        shift_on(w_strips, r).wait_recv()
        lax.fori_loop(0, 8, on, 0, unroll=4)
        plane_order(lambda d: p2_copy(r, d).start())
        a1[q, rows] = res[q, rows]

    residuals(0)
    residuals(1)

    def tiles(body):
        def one(u, carry):
            body(u, pl.ds(pl.multiple_of(u * 128, 128), 128))
            return carry

        lax.fori_loop(0, 4, one, 0, unroll=2)

    def plane_forward(r):
        rows = group_rows(r)

        def body(u, columns):
            result = real_forward([a1[k, rows, columns] for k in range(NQ)])
            yb[0, 0, rows, columns] = result[0][0]
            yb[0, 1, rows, columns] = result[8][0]
            for k in range(1, 8):
                yb[k, 0, rows, columns] = result[k][0]
                yb[k, 1, rows, columns] = result[k][1]

        tiles(body)

    def p3_copy(r, d):
        rows = group_rows(r)
        return copy(
            yb.at[(z + d) % NZ, :, rows], a2.at[z, :, rows],
            p3_send.at[r, d], p3_recv.at[r, d], ring(d), core,
        )


    lane = lax.broadcasted_iota(jnp.int32, (8, 128), 1)
    sublane = lax.broadcasted_iota(jnp.int32, (8, 128), 0)

    def one_of(parts, choice):
        low = jnp.where(choice == 0, parts[0], parts[1])
        return jnp.where(choice < 2, low, jnp.where(choice == 2, parts[2], parts[3]))

    def moved(part, index):
        return jnp.take_along_axis(part, index, axis=1)

    within, block = lane % 4, lane // 32

    def columns_spread(parts):
        mixed = [one_of(parts, (within + s) % 4) for s in range(4)]
        mixed = [moved(mixed[s], 4 * (lane % 32) + (block - s) % 4) for s in range(4)]
        return [one_of(mixed, (block - u) % 4) for u in range(4)]

    def columns_joined(parts):
        mixed = [one_of(parts, (block - s) % 4) for s in range(4)]
        mixed = [moved(mixed[s], 32 * ((within + s) % 4) + lane // 4) for s in range(4)]
        return [one_of(mixed, (u - within) % 4) for u in range(4)]

    def quarters(value):
        return [value[:, u * 128 : (u + 1) * 128] for u in range(4)]

    def rearranged(ref, r, change):
        rows = group_rows(r)

        def one(t, carry):
            for field in range(2):
                parts = change([ref[t, field, u, rows] for u in range(4)])
                for u, part in enumerate(parts):
                    ref[t, field, u, rows] = part
            return carry

        lax.fori_loop(0, 8, one, 0, unroll=4)

    def partners(act):
        each(1, 8, lambda d: act((slot + d) % 8))

        @pl.when(apart)
        def _():
            act(slot)

    def main_copy(r, src, dst, send, recv, k):
        rows = pl.ds(pl.multiple_of(HALO + slot * STRIP + r * GROUP, 8), GROUP)
        return copy(
            src(k).at[:, :, group_rows(r)], dst.at[:, :, rows],
            send.at[r, k], recv.at[r, slot], partner(k), half,
        )

    def main_arriving(r, src, dst, send, recv, k):
        rows = pl.ds(pl.multiple_of(HALO + slot * STRIP + r * GROUP, 8), GROUP)
        return copy(
            src(k).at[:, :, group_rows(r)], dst.at[:, :, rows],
            send.at[r, k], recv.at[r, k], partner(k), half,
        )

    def spread_start(r, src, dst, send, recv):
        partners(lambda k: main_copy(r, src, dst, send, recv, k).start())

        @pl.when(jnp.logical_not(apart))
        def _():
            own = pl.ds(pl.multiple_of(HALO + slot * STRIP + r * GROUP, 8), GROUP)
            dst[:, :, own] = src(slot)[:, :, group_rows(r)]

    def spread_arrived(r, src, dst, send, recv):
        partners(lambda k: main_arriving(r, src, dst, send, recv, k).wait_recv())

    def spread_sent(r, src, dst, send, recv):
        partners(lambda k: main_copy(r, src, dst, send, recv, k).wait_send())

    facing = (8 * (1 - half) + slot) * NZ + z
    down = HALO + BLOCK - HALO

    def halo_copy(field, send, recv, far):
        goes_down = (core == 1) if far else (core == 0)
        first = pl.multiple_of(jnp.where(goes_down, down, HALO), 8)
        into = pl.multiple_of(jnp.where(goes_down, 0, HALO + BLOCK), 8)
        index = 1 if far else 0
        return copy(
            field.at[:, :, pl.ds(first, HALO)], field.at[:, :, pl.ds(into, HALO)],
            send.at[index], recv.at[index], facing if far else n, other,
        )

    def halo(field, send, recv, act):
        act(halo_copy(field, send, recv, False))

        @pl.when(apart)
        def _():
            act(halo_copy(field, send, recv, True))

    @pl.when(jnp.logical_not(apart))
    def _():
        outer = pl.ds(pl.multiple_of(core * (HALO + BLOCK), 8), HALO)
        fq[:, :, outer] = jnp.zeros((1, 4, HALO, 128), jnp.float32)
        ta[:, :, outer] = jnp.zeros((2, 4, HALO, 128), jnp.float32)

    def plane_to_ring(r):
        each(1, NQ, lambda d: p2_copy(r, d).wait_recv())
        plane_forward(r)
        if r:
            each(1, NZ, lambda d: p3_copy(0, d).wait_send())
        ring_order(lambda d: p3_copy(r, d).start())
        a2[z, :, group_rows(r)] = yb[z, :, group_rows(r)]

    plane_to_ring(0)

    @pl.when(z != NZ - 1)
    def _():
        f2_copy(1).wait_recv()

    for row in (0, 8):
        own = cond[pl.ds(pl.multiple_of(q * STRIP + row, 8), 8)]
        frozen = conductance(own, fstrip[row : row + 8])
        for u, part in enumerate(columns_spread(quarters(frozen))):
            fmix[0, u, row : row + 8] = part

    f3 = (lambda k: fmix, fq, f3_send, f3_recv)
    for r in range(2):
        spread_start(r, *f3)

    plane_to_ring(1)
    for r in range(2):
        spread_arrived(r, *f3)
    halo(fq, fh_send, fh_recv, lambda item: item.start())

    twiddle = [(scalar(T_TWIDDLE + 2 * k), scalar(T_TWIDDLE + 2 * k + 1)) for k in range(NZ)]
    start = 2 * NZ * half
    twiddle_first = (scalar(T_TWIDDLE + start), scalar(T_TWIDDLE + start + 1))
    sign = jnp.where(half == 1, -1.0, 1.0)

    def source(k):
        return (k + NZ - half) % NZ

    def ring_forward(r):
        rows = group_rows(r)

        @pl.when(z != 0)
        def _():
            def body(u, columns):
                values = []
                for k in range(NZ):
                    real, imag = a2[source(k), 0, rows, columns], a2[source(k), 1, rows, columns]
                    cosine, sine = twiddle[k] if k else twiddle_first
                    values.append((cosine * real + sine * imag, cosine * imag - sine * real))
                for k, value in enumerate(complex_transform(values, -1.0)):
                    sb[k, 0, u, rows] = value[0]
                    sb[k, 1, u, rows] = value[1]

            tiles(body)

        @pl.when(z == 0)
        def _():
            def body(u, columns):
                even = real_forward([a2[source(k), 0, rows, columns] for k in range(NZ)])
                sb[0, 0, u, rows] = even[0][0]
                sb[0, 1, u, rows] = even[4][0]
                values = [a2[source(k), 1, rows, columns] for k in range(NZ)]
                values[0] = sign * values[0]
                odd = [turned((values[k], -values[k + 4]), -k / 16) for k in range(4)]
                odd = complex_transform(odd, -1.0)
                for k, value in list(zip((1, 2, 3), even[1:4])) + list(zip((4, 5, 6, 7), odd)):
                    sb[k, 0, u, rows] = value[0]
                    sb[k, 1, u, rows] = value[1]

            tiles(body)

    p4 = (lambda k: sb.at[k], ta, p4_send, p4_recv)
    for r in range(2):
        each(1, NZ, lambda d: p3_copy(r, d).wait_recv())
        ring_forward(r)
        rearranged(sb, r, columns_spread)
        spread_start(r, *p4)
    halo(fq, fh_send, fh_recv, lambda item: item.wait_recv())
    top = half * ROWS + core * BLOCK - HALO
    scale = TAU / HALF

    def spaced(ref, field, t):
        rows = pl.ds(t, 8, stride=GROUPS)
        return [ref[field, u, rows] for u in range(4)]

    def weights(t, here, below):
        row = GROUPS * sublane + t
        closed = (row == SPAN - 1) | (row + top == 2 * ROWS - 1) | (row + top == -1)
        rim = (row + top == 0) | (row + top == 2 * ROWS - 1)
        before = pltpu.roll(here[3], 1, 1)
        beyond = [here[1], here[2], here[3], pltpu.roll(here[0], 127, 1)]
        west[t] = jnp.where(lane == 0, 0.0, scale * (here[0] + before))
        for u in range(4):
            columns = slice(u * 128, (u + 1) * 128)
            wts[0, t, :, columns] = jnp.where(closed, 0.0, scale * (here[u] + below[u]))
            east = scale * (here[u] + beyond[u])
            center = jnp.where(rim, scale * here[u], 0.0) - 2.0
            if u == 0:
                center = center + jnp.where(lane == 0, scale * here[u], 0.0)
            if u == 3:
                center = center + jnp.where(lane == 127, scale * here[u], 0.0)
                east = jnp.where(lane == 127, 0.0, east)
            wts[1, t, :, columns] = east
            wts[2, t, :, columns] = center

    def weight_rows(t, carry):
        weights(t, spaced(fq, 0, t), spaced(fq, 0, t + 1))
        return carry

    lax.fori_loop(0, GROUPS - 1, weight_rows, 0, unroll=3)
    weights(
        GROUPS - 1,
        spaced(fq, 0, GROUPS - 1),
        [pltpu.roll(part, 7, 0) for part in spaced(fq, 0, 0)],
    )
    tj[...] = jnp.zeros(tj.shape, jnp.float32)
    for r in range(2):
        spread_arrived(r, *p4)
    halo(ta, p4h_send, p4h_recv, lambda item: item.start())
    halo(ta, p4h_send, p4h_recv, lambda item: item.wait_recv())


    first = [scalar(T_DELTA + k) for k in range(3)]

    def begin(t, carry):
        real, imag = spaced(ta, 0, t), spaced(ta, 1, t)
        for u in range(4):
            columns = slice(u * 128, (u + 1) * 128)
            ti[0, t, :, columns] = real[u]
            ti[1, t, :, columns] = imag[u]
            xi[0, t, :, columns] = first[0] * real[u] - first[1] * imag[u]
            xi[1, t, :, columns] = first[1] * real[u] + first[2] * imag[u]
        return carry

    lax.fori_loop(0, GROUPS, begin, 0, unroll=11)

    def swept_row(now, old, t, here, below, flux_above, factors):
        south, east, center = (quarters(wts[k, t]) for k in range(3))
        west_weight = west[t]
        fresh, flux_below = [], []
        for field in range(2):
            v = here[field]
            before, beyond = pltpu.roll(v[3], 1, 1), pltpu.roll(v[0], 127, 1)
            eastward = [east[u] * ((v[u + 1] if u < 3 else beyond) - v[u]) for u in range(4)]
            westward = [west_weight * (v[0] - before)] + eastward[:3]
            downward = [south[u] * (below[field][u] - v[u]) for u in range(4)]
            result = []
            for u in range(4):
                columns = slice(u * 128, (u + 1) * 128)
                value = (center[u] * v[u] - old[field, t, :, columns]) + (
                    (flux_above[field][u] - downward[u]) + (westward[u] - eastward[u])
                )
                old[field, t, :, columns] = value
                result.append(value)
            fresh.append(result)
            flux_below.append(downward)
        if factors is not None:
            for u in range(4):
                columns = slice(u * 128, (u + 1) * 128)
                real, imag = here[0][u], here[1][u]
                xi[0, t, :, columns] = xi[0, t, :, columns] + (
                    (factors[0] * real - factors[1] * imag)
                    + (factors[3] * fresh[0][u] - factors[4] * fresh[1][u])
                )
                xi[1, t, :, columns] = xi[1, t, :, columns] + (
                    (factors[1] * real + factors[2] * imag)
                    + (factors[4] * fresh[0][u] + factors[5] * fresh[1][u])
                )
        return flux_below

    def sweep(now, old, factors):
        begin_rows = [quarters(now[field, 0]) for field in range(2)]
        wrapped = [[pltpu.roll(part, 7, 0) for part in begin_rows[field]] for field in range(2)]
        end_rows = [quarters(now[field, GROUPS - 1]) for field in range(2)]
        end_south = quarters(wts[0, GROUPS - 1])
        flux_above = [
            [
                pltpu.roll(end_south[u] * (wrapped[field][u] - end_rows[field][u]), 1, 0)
                for u in range(4)
            ]
            for field in range(2)
        ]

        def one(t, carried):
            here, above = carried
            below = [quarters(now[field, t + 1]) for field in range(2)]
            return below, swept_row(now, old, t, here, below, above, factors)

        here, above = lax.fori_loop(
            0, GROUPS - 1, one, (begin_rows, flux_above), unroll=GROUPS - 1
        )
        swept_row(now, old, GROUPS - 1, here, wrapped, above, factors)

    def two_sweeps(m, carry):
        k = 2 * m + 1
        factors = [scalar(T_DELTA + 3 * k + each) for each in range(6)]
        sweep(ti, tj, None)
        sweep(tj, ti, factors)
        return carry

    lax.fori_loop(0, SWEEPS // 2, two_sweeps, 0)

    def finish(t, carry):
        for field in range(2):
            for u in range(4):
                columns = slice(u * 128, (u + 1) * 128)
                xb[field, u, pl.ds(t, 8, stride=GROUPS)] = xi[field, t, :, columns]
        return carry

    lax.fori_loop(0, GROUPS, finish, 0, unroll=11)

    def p6_copy(r, k, index):
        rows = pl.ds(pl.multiple_of(HALO + k * STRIP + r * GROUP, 8), GROUP)
        return copy(
            xb.at[:, :, rows], a3.at[slot, :, :, group_rows(r)],
            p6_send.at[r, k], p6_recv.at[r, index], partner(k), half,
        )

    for r in range(2):
        if r:
            partners(lambda k: p6_copy(0, k, slot).wait_send())
        partners(lambda k: p6_copy(r, k, slot).start())

        @pl.when(jnp.logical_not(apart))
        def _():
            own = pl.ds(pl.multiple_of(HALO + slot * STRIP + r * GROUP, 8), GROUP)
            a3[slot, :, :, group_rows(r)] = xb[:, :, own]

    def ring_backward(r):
        rows = group_rows(r)

        @pl.when(z != 0)
        def _():
            def body(u, columns):
                values = [(a3[k, 0, u, rows], a3[k, 1, u, rows]) for k in range(8)]
                for k, (real, imag) in enumerate(complex_transform(values, 1.0)):
                    cosine, sine = twiddle[k]
                    if k:
                        real, imag = cosine * real - sine * imag, cosine * imag + sine * real
                    ub[k, 0, u, rows] = real
                    ub[k, 1, u, rows] = imag

            tiles(body)

        @pl.when(z == 0)
        def _():
            def body(u, columns):
                values = [(a3[k, 0, u, rows], a3[k, 1, u, rows]) for k in range(8)]
                even = [(values[0][0], None)] + values[1:4] + [(values[0][1], None)]
                for k, value in enumerate(real_backward(even)):
                    ub[k, 0, u, rows] = value
                for k, value in enumerate(complex_transform(values[4:8], 1.0)):
                    real, imag = turned(value, k / 16)
                    ub[k, 1, u, rows] = 2.0 * real
                    ub[k + 4, 1, u, rows] = -2.0 * imag

            tiles(body)

    def p7_copy(r, d):
        rows = group_rows(r)
        return copy(
            ub.at[(z + d) % NZ, :, :, rows], a4.at[z, :, :, rows],
            p7_send.at[r, d], p7_recv.at[r, d], ring(d), core,
        )

    for r in range(2):
        partners(lambda k: p6_copy(r, k, k).wait_recv())
        ring_backward(r)
        rearranged(ub, r, columns_joined)
        if r:
            each(1, NZ, lambda d: p7_copy(0, d).wait_send())
        ring_order(lambda d: p7_copy(r, d).start())
        a4[z, :, :, group_rows(r)] = ub[z, :, :, group_rows(r)]

    scale_out = [scalar(T_OUT + k) for k in range(NQ)]

    def plane_backward(r):
        rows = group_rows(r)

        def body(u, columns):
            values = [(a4[k, 0, u, rows], a4[k, 1, u, rows]) for k in range(8)]
            values = [(values[0][0], None)] + values[1:] + [(values[0][1], None)]
            for k, value in enumerate(real_backward(values)):
                cb[k, rows, columns] = scale_out[k] * value

        tiles(body)

    def p8_copy(r, d):
        rows = group_rows(r)
        return copy(
            cb.at[plane_of(d), rows], out.at[q, rows],
            p8_send.at[r, d], p8_recv.at[r, d], plane(d), core,
        )

    own_strips = [
        pltpu.make_async_copy(
            cb.at[q, group_rows(r)], out.at[q, group_rows(r)], load_sem.at[4 + r]
        )
        for r in range(2)
    ]
    for r in range(2):
        each(1, NZ, lambda d: p7_copy(r, d).wait_recv())
        plane_backward(r)
        plane_order(lambda d: p8_copy(r, d).start())
        own_strips[r].start()

    for item in edges_out:
        item.wait_send()
    shift_on(w_strips, 1).wait_send()
    shift_back(1).wait_send()

    @pl.when(owner)
    def _():
        each(1, NQ, lambda d: f1_copy(d).wait_send())

    @pl.when(z == NZ - 1)
    def _():
        each(1, NZ, lambda d: f2_copy(d).wait_send())

    for r in range(2):
        each(1, NQ, lambda d: p2_copy(r, d).wait_send())
        spread_sent(r, *f3)
        spread_sent(r, *p4)
    for sent in (p3_copy, p7_copy):
        each(1, NZ, lambda d: sent(1, d).wait_send())
    partners(lambda k: p6_copy(1, k, slot).wait_send())
    halo(fq, fh_send, fh_recv, lambda item: item.wait_send())
    halo(ta, p4h_send, p4h_recv, lambda item: item.wait_send())

    for r in range(2):
        each(1, NQ, lambda d: p8_copy(r, d).wait_recv())
        own_strips[r].wait()
        each(1, NQ, lambda d: p8_copy(r, d).wait_send())


def body(window_state, prior_window, conductivity):
    f32 = jnp.float32
    dma = pltpu.SemaphoreType.DMA
    padded_rows = ROWS + 2 * PAD
    strips = (NQ, STRIP, COLS)
    pairs = (8, 2, STRIP, COLS)
    pairs_apart = (8, 2, 4, STRIP, 128)
    shapes = [
        (ROWS, COLS),
        (padded_rows, COLS),
        (padded_rows, COLS),
        (2, 8, COLS),
        strips,
        strips,
        strips,
        strips,
        pairs,
        pairs,
        pairs_apart,
        strips,
        (STRIP, COLS),
        (1, 4, STRIP, 128),
        (1, 4, SPAN, 128),
        (2, 4, SPAN, 128),
        (2, GROUPS, 8, COLS),
        (2, GROUPS, 8, COLS),
        (2, GROUPS, 8, COLS),
        (2, 4, SPAN, 128),
        (3, GROUPS, 8, COLS),
        (GROUPS, 8, 128),
        pairs_apart,
        pairs_apart,
        pairs_apart,
        strips,
    ]
    sems = [(6,), (2,), (2,), (2, 2), (2, 2), (16,), (1,), (8,), (1,), (2, 8), (2, 8), (2,), (2,)]
    sems += [(2, 16), (2, 16), (2, 8), (2, 8), (2, 8), (2, 8), (2,), (2,)]
    sems += [(2, 8), (2, 8), (2, 8), (2, 8), (2, 16), (2, 16)]
    correction = pl.pallas_call(
        kernel,
        out_shape=jax.ShapeDtypeStruct(strips, f32),
        in_specs=5 * [pl.BlockSpec(memory_space=pl.ANY)],
        out_specs=pl.BlockSpec(memory_space=pl.ANY),
        scratch_shapes=[pltpu.SMEM((1, T_WIDTH), f32)]
        + [pltpu.VMEM(shape, f32) for shape in shapes]
        + [dma(shape) for shape in sems],
        compiler_params=pltpu.CompilerParams(
            collective_id=0, has_side_effects=True, vmem_limit_bytes=60 * 1024 * 1024
        ),
    )(
        jnp.asarray(scalar_table()),
        window_state[0],
        window_state.reshape(strips),
        prior_window.reshape(strips),
        conductivity,
    )
    return window_state + correction.reshape(1, ROWS, COLS)


def solution(mesh):
    in_specs = (P("tm", "space", None), P("tm", "space", None), P("space", None))
    out_specs = P("tm", "space", None)
    return jax.shard_map(body, mesh=mesh, in_specs=in_specs, out_specs=out_specs, check_vma=False)
```
